128 devices in a mesh: section: 2 (over core), seq: 8 (over x, z_hi), wshard: 8 (over y, z_lo).
Axes of the slice: x: 4, y: 4, z: 4 (z_hi: 2, z_lo: 2; z = z_hi * 2 + z_lo), core: 2. Of those that a mesh axis runs over, the one named last changes fastest.
Arguments:
- tokens: bfloat16 [16, 1024, 1024], P('wshard', 'seq'), may hold values from -6 to 6
- positions: int32 [16, 1024], P('wshard'), may hold values from 0 to 1021, as said below
- w_qkv: bfloat16 [2, 1024, 3072], P('section', 'wshard'), may hold values from -0.1875 to 0.1875
- b_qkv: bfloat16 [2, 3072], P('section', 'wshard'), may hold values from -1.1953125 to 1.1953125
- w_dense: bfloat16 [2, 1024, 1024], P('section', 'wshard'), may hold values from -3 to 3
- b_dense: bfloat16 [2, 1024], P('section', 'wshard'), may hold values from -1.1953125 to 1.1953125
- w_up: bfloat16 [2, 1024, 4096], P('section', 'wshard'), may hold values from -0.1875 to 0.1875
- b_up: bfloat16 [2, 4096], P('section', 'wshard'), may hold values from -1.1953125 to 1.1953125
- w_down: bfloat16 [2, 4096, 1024], P('section', 'wshard'), may hold values from -0.09375 to 0.09375
- b_down: bfloat16 [2, 1024], P('section', 'wshard'), may hold values from -1.1953125 to 1.1953125
- norm1_gain: bfloat16 [2, 1024], P('section', 'wshard'), may hold values from 0.5 to 1.5
- norm1_shift: bfloat16 [2, 1024], P('section', 'wshard'), may hold values from -1.1953125 to 1.1953125
- norm2_gain: bfloat16 [2, 1024], P('section', 'wshard'), may hold values from 0.5 to 1.5
- norm2_shift: bfloat16 [2, 1024], P('section', 'wshard'), may hold values from -1.1953125 to 1.1953125
- cotangent: bfloat16 [16, 1024, 1024], P('wshard', 'seq'), may hold values from -6 to 6
Outputs:
- hidden: bfloat16 [2, 16, 1024, 1024], P('section', 'wshard', 'seq')
- in_grads: float32 [2, 16, 1024, 1024], P('section', 'wshard', 'seq')
- grad_w_qkv: float32 [2, 1024, 3072], P('section', 'wshard')
- grad_b_qkv: float32 [2, 2048], P('section', 'wshard')
- grad_b_values: float32 [2, 1024], P('section', 'wshard')
- grad_w_dense: float32 [2, 1024, 1024], P('section', 'wshard')
- grad_b_dense: float32 [2, 1024], P('section', 'wshard')
- grad_w_up: float32 [2, 1024, 4096], P('section', 'wshard')
- grad_b_up: float32 [2, 4096], P('section', 'wshard')
- grad_w_down: float32 [2, 4096, 1024], P('section', 'wshard')
- grad_b_down: float32 [2, 1024], P('section', 'wshard')
- grad_norm1_gain: float32 [2, 1024], P('section', 'wshard')
- grad_norm1_shift: float32 [2, 1024], P('section', 'wshard')
- grad_norm2_gain: float32 [2, 1024], P('section', 'wshard')
- grad_norm2_shift: float32 [2, 1024], P('section', 'wshard')
The draws below stay inside these ranges and needn't reach their ends.
Inputs may be any that keep to these rules, and one draw needn't show every extreme that they name: Each sequence packs three documents; positions count from 0 at each document's first token and rise by one; the middle document begins within the first 128 tokens (the first 4 where 128 is smaller) and ends within the last 128 tokens (the last 4 where 128 is smaller).
All inputs are finite; a program needn't handle non-finite values.
Results may differ from the reference program's by a relative error of at most 0.018.
Values may be sent and summed in bfloat16 or wider, within the bound.
No kernel may reach another device: no remote copies, remote signals or barrier semaphores. Data moves between devices by JAX's collectives and lax.ppermute only.
A program may use at most 256 MiB of HBM per device.

```python
import math
import jax
import jax.numpy as jnp
from jax import lax

D = 1024
HEADS = 16
HEAD = 64
ROT = 16
FF = 4096
LAYERS = 2
SEQ_LEN = 1024
SHARD = 128
SEQS = 16


def draw_positions(key, part):
    key = jax.random.fold_in(key, 7)
    first_key, second_key, third_key = jax.random.split(key, 3)
    reach = max(SHARD, 4)
    opening = jax.random.randint(first_key, (SEQS, 1), 1, reach)
    closing = jax.random.randint(second_key, (SEQS, 1), SEQ_LEN - reach + 1, SEQ_LEN)
    spanning = jax.random.randint(third_key, (), 0, SEQS)
    whole_row = jnp.arange(SEQS, dtype=jnp.int32)[:, None] == spanning
    opening = jnp.where(whole_row, 1, opening).astype(jnp.int32)
    closing = jnp.where(whole_row, SEQ_LEN - 1, closing).astype(jnp.int32)
    places = jnp.arange(SEQ_LEN, dtype=jnp.int32)[None, :]
    begins = jnp.where(places < opening, 0, jnp.where(places < closing, opening, closing))
    return (places - begins).astype(jnp.int32)


def levels(own_key, extent, cuts, smallest, top_value):
    loudness = 1.0
    for position, blocks in cuts:
        steps = jax.random.uniform(jax.random.fold_in(jax.random.fold_in(own_key, 6), position), (blocks,), jnp.float32, smallest / len(cuts), top_value / len(cuts))
        loudness = loudness * jnp.repeat(jnp.exp(steps), extent[position] // blocks).reshape((-1,) + (1,) * (len(extent) - 1 - position))
    return loudness


def noise(stream_key, extent, deviation, limit, cuts=(), kind=jnp.bfloat16):
    array = deviation * jax.random.normal(stream_key, extent, jnp.float32)
    if cuts:
        array = array * levels(stream_key, extent, cuts, -0.22, 0.18)
    return jnp.clip(array, -limit, limit).astype(kind)


def setup_inputs(seed: int = 0) -> dict:
    key_of = jax.random.split(jax.random.key(seed), 16)
    tokens = noise(key_of[0], (SEQS, SEQ_LEN, D), 1.0, 6.0, ((0, 8), (1, 8)))
    positions = draw_positions(jax.random.fold_in(key_of[15], 71), 0)
    w_qkv = noise(key_of[2], (LAYERS, D, 3 * D), D ** -0.5, 0.1875, ((0, 2), (1, 8)))
    b_qkv = noise(key_of[3], (LAYERS, 3 * D), 0.2, 1.1953125, ((0, 2), (1, 8)))
    w_dense = noise(key_of[4], (LAYERS, D, D), (max(D // 256, 1)) ** -0.5, 3.0, ((0, 2), (1, 8)))
    b_dense = noise(key_of[5], (LAYERS, D), 0.2, 1.1953125, ((0, 2), (1, 8)))
    w_up = noise(key_of[6], (LAYERS, D, FF), D ** -0.5, 0.1875, ((0, 2), (1, 8)))
    b_up = noise(key_of[7], (LAYERS, FF), 0.2, 1.1953125, ((0, 2), (1, 8)))
    w_down = noise(key_of[8], (LAYERS, FF, D), FF ** -0.5, 0.09375, ((0, 2), (1, 8)))
    b_down = noise(key_of[9], (LAYERS, D), 0.2, 1.1953125, ((0, 2), (1, 8)))
    norm1_gain = jnp.clip(1.0 + 0.1 * jax.random.normal(key_of[10], (LAYERS, D), jnp.float32), 0.5, 1.5).astype(jnp.bfloat16)
    norm1_shift = noise(key_of[11], (LAYERS, D), 0.2, 1.1953125, ((0, 2), (1, 8)))
    norm2_gain = jnp.clip(1.0 + 0.1 * jax.random.normal(key_of[12], (LAYERS, D), jnp.float32), 0.5, 1.5).astype(jnp.bfloat16)
    norm2_shift = noise(key_of[13], (LAYERS, D), 0.2, 1.1953125, ((0, 2), (1, 8)))
    cotangent = noise(key_of[14], (SEQS, SEQ_LEN, D), 1.0, 6.0, ((0, 8), (1, 8)))
    return dict(tokens=tokens, positions=positions, w_qkv=w_qkv, b_qkv=b_qkv, w_dense=w_dense, b_dense=b_dense, w_up=w_up, b_up=b_up, w_down=w_down, b_down=b_down, norm1_gain=norm1_gain, norm1_shift=norm1_shift, norm2_gain=norm2_gain, norm2_shift=norm2_shift, cotangent=cotangent)


NORM_EPS = 1e-05

@jax.custom_vjp
def low(v):
    return lax.optimization_barrier(v.astype(jnp.bfloat16)).astype(jnp.float32)

@jax.custom_vjp
def low_back(v):
    return v

def low_keep(v):
    return (low(v), None)

def low_pass(kept, grad):
    return (grad,)

def back_keep(v):
    return (v, None)

def back_low(kept, grad):
    return (low(grad),)
low.defvjp(low_keep, low_pass)
low_back.defvjp(back_keep, back_low)

def matmul(left, right):
    return jnp.dot(left, right, precision=lax.Precision.HIGHEST, preferred_element_type=jnp.float32)

def norm_rows(values, gain, shift):
    centre = lax.optimization_barrier(jnp.mean(values, axis=-1, keepdims=True))
    centred = values - centre
    spread = lax.optimization_barrier(jnp.mean(centred * centred, axis=-1, keepdims=True))
    return centred * lax.rsqrt(spread + NORM_EPS) * gain + shift

def rotate(values, places):
    half_width = ROT // 2
    frequency = 1.0 / 10000.0 ** (jnp.arange(half_width).astype(jnp.float32) * 2.0 / ROT)
    angles = places.astype(jnp.float32)[:, None] * frequency[None, :]
    cosine = jnp.concatenate([jnp.cos(angles), jnp.cos(angles)], axis=-1)[:, None, :]
    sine_part = jnp.concatenate([jnp.sin(angles), jnp.sin(angles)], axis=-1)[:, None, :]
    leading = values[..., :ROT]
    turned = jnp.concatenate([-leading[..., half_width:], leading[..., :half_width]], axis=-1)
    return jnp.concatenate([leading * cosine + turned * sine_part, values[..., ROT:]], axis=-1)

def visible(offset, block_rows, length, place_block):
    query_rows = offset + jnp.arange(block_rows, dtype=jnp.int32)
    key_rows = jnp.arange(length, dtype=jnp.int32)
    behind = key_rows[None, :] <= query_rows[:, None]
    inside = query_rows[:, None] - key_rows[None, :] <= place_block[:, None]
    return behind & inside

def attend(queries, keys_rot, values, places):
    length = queries.shape[0]
    block_rows = min(512, length)
    scaling = 1.0 / math.sqrt(HEAD)

    def one_block(offset):
        query_block = lax.dynamic_slice_in_dim(queries, offset, block_rows, 0)
        place_block = lax.dynamic_slice_in_dim(places, offset, block_rows, 0)
        scores = jnp.einsum('qhd,khd->hqk', query_block, keys_rot, precision=lax.Precision.HIGHEST) * scaling
        scores = jnp.where(visible(offset, block_rows, length, place_block)[None], scores, -1e+30)
        scores = low_back(scores)
        attn_probs = low(jax.nn.softmax(scores, axis=-1))
        return jnp.einsum('hqk,khd->qhd', attn_probs, values, precision=lax.Precision.HIGHEST)
    offsets = (jnp.arange(length // block_rows) * block_rows).astype(jnp.int32)
    mixed = lax.map(jax.checkpoint(one_block), offsets)
    return mixed.reshape(queries.shape)

def layer(inputs, places, weights):
    w_qkv, b_qkv, w_dense, b_dense, w_up, b_up, w_down, b_down, gain_one, shift_one, gain_two, shift_two = weights
    length = inputs.shape[0]
    normed_one = low(norm_rows(inputs, gain_one, shift_one))
    projected = low(low_back(matmul(normed_one, w_qkv) + b_qkv)).reshape(length, 3, HEADS, HEAD)
    queries = low(rotate(projected[:, 0], places))
    keys_rot = low(rotate(projected[:, 1], places))
    mixed = attend(queries, keys_rot, projected[:, 2], places)
    mixed = low(low_back(mixed.reshape(length, D)))
    normed_two = low(norm_rows(inputs, gain_two, shift_two))
    middle = low_back(matmul(normed_two, w_up) + b_up)
    activated = low(jax.nn.gelu(middle, approximate=False))
    return inputs + matmul(mixed, w_dense) + b_dense + matmul(activated, w_down) + b_down

def forward(inputs, places, bridge, first_layer, second_layer):
    between = low(low_back(layer(inputs, places, first_layer))) + bridge
    return (layer(between, places, second_layer), between)

def reference(tokens, positions, w_qkv, b_qkv, w_dense, b_dense, w_up, b_up, w_down, b_down, norm1_gain, norm1_shift, norm2_gain, norm2_shift, cotangent):
    weights = tuple((member.astype(jnp.float32) for member in (w_qkv, b_qkv, w_dense, b_dense, w_up, b_up, w_down, b_down, norm1_gain, norm1_shift, norm2_gain, norm2_shift)))
    first_layer = tuple((member[0] for member in weights))
    second_layer = tuple((member[1] for member in weights))

    def one_sequence(totals, element):
        inputs, places, upstream = element
        inputs = inputs.astype(jnp.float32)
        upstream = upstream.astype(jnp.float32)
        bridge = jnp.zeros_like(inputs)

        def run_forward(inputs_now, bridge_now, layer_first, layer_second):
            return forward(inputs_now, places, bridge_now, layer_first, layer_second)
        result, pull, between = jax.vjp(run_forward, inputs, bridge, first_layer, second_layer, has_aux=True)
        d_inputs, d_between, grad_first, grad_second = pull(upstream)
        totals = tuple((running + jnp.stack([part_first, part_second]) for running, part_first, part_second in zip(totals, grad_first, grad_second)))
        outputs = jnp.stack([between, result]).astype(jnp.bfloat16)
        gradients = jnp.stack([d_inputs, low(d_between)])
        return (totals, (outputs, gradients))
    zeros = tuple((jnp.zeros_like(member) for member in weights))
    totals, (hidden, in_grads) = lax.scan(one_sequence, zeros, (tokens, positions, cotangent))
    hidden = jnp.swapaxes(hidden, 0, 1)
    in_grads = jnp.swapaxes(in_grads, 0, 1)
    return (hidden, in_grads, totals[0], totals[1][:, :2 * D], totals[1][:, 2 * D:], totals[2], totals[3], totals[4], totals[5], totals[6], totals[7], totals[8], totals[9], totals[10], totals[11])
```

```python
import math

import jax
import jax.numpy as jnp
from jax import lax
from jax.experimental import pallas as pl
from jax.experimental.pallas import tpu as pltpu
from jax.sharding import PartitionSpec as P

HEAD = 64
ROT = 16
NORM_EPS = 1e-05
BF = jnp.bfloat16
F32 = jnp.float32
AXES = ("section", "seq", "wshard")
LENGTH = 1024
WIDTH = 1024
QROWS = 256
UNIT = 64


def place_of(index):
    core, seq, shard = index // 64, (index // 8) % 8, index % 8
    return core, seq // 2, seq % 2, shard // 2, shard % 2


def index_of(core, x, zh, y, zl):
    return core * 64 + (2 * x + zh) * 8 + 2 * y + zl


def route(block, target):
    pairs = [(i, index_of(*target(*place_of(i)))) for i in range(128)]
    return lax.ppermute(block, AXES, pairs)


def along_x(block, step):
    return route(block, lambda c, x, zh, y, zl: (c, (x + step) % 4, zh, y, zl))


def along_y(block, step):
    return route(block, lambda c, x, zh, y, zl: (c, x, zh, (y + step) % 4, zl))


def across_cores(block):
    return route(block, lambda c, x, zh, y, zl: (1 - c, x, zh, y, zl))


def across_high(block):
    return route(block, lambda c, x, zh, y, zl: (c, x, 1 - zh, y, zl))


def across_low(block):
    return route(block, lambda c, x, zh, y, zl: (c, x, zh, y, 1 - zl))


def transposed(block):
    return route(block, lambda c, x, zh, y, zl: (zl, y, zh, x, c))


def pick(array, index, axis=0):
    return lax.dynamic_index_in_dim(array, index, axis, keepdims=False)


def dot(left, right):
    return jnp.dot(left, right, preferred_element_type=F32)


def dot_left(left, right):
    return lax.dot_general(left, right, (((0,), (0,)), ((), ())), preferred_element_type=F32)


def dot_right(left, right):
    return lax.dot_general(left, right, (((1,), (1,)), ((), ())), preferred_element_type=F32)


def head_lanes(rows, head):
    lanes = lax.broadcasted_iota(jnp.int32, (rows, 2 * HEAD), 1)
    return (lanes >= head * HEAD) & (lanes < (head + 1) * HEAD)


def turned(values, cosine, sine_low, sine_high):
    return (
        values * cosine
        + pltpu.roll(values, ROT // 2, 1) * sine_low
        + pltpu.roll(values, 2 * HEAD - ROT // 2, 1) * sine_high
    )


def masked_scores(query, keys, begin, block, reach):
    scores = dot_right(query, keys)
    rows = block * QROWS + lax.broadcasted_iota(jnp.int32, (QROWS, reach), 0)
    columns = lax.broadcasted_iota(jnp.int32, (QROWS, reach), 1)
    seen = (columns <= rows) & (columns >= begin)
    return jnp.where(seen, scores, -1e30)


def attend_kernel(
    where_ref, proj_ref, cos_ref, low_ref, high_ref, begin_ref, mixed_ref, q_ref, k_ref, v_ref, o_ref, lse_ref
):
    for m in range(LENGTH // UNIT):
        here = pl.ds(m * UNIT, UNIT)
        there = pl.ds(pl.multiple_of(where_ref[m] * UNIT, UNIT), UNIT)
        proj = proj_ref[there, :]
        cosine, low, high = cos_ref[here, :], low_ref[here, :], high_ref[here, :]
        query = turned(proj[:, :128].astype(F32), cosine, low, high)
        q_ref[here, :] = (query.astype(BF).astype(F32) * (1.0 / math.sqrt(HEAD))).astype(BF)
        k_ref[here, :] = turned(proj[:, 128:256].astype(F32), cosine, low, high).astype(BF)
        v_ref[here, :] = proj[:, 256:]
    for block in range(LENGTH // QROWS):
        rows = pl.ds(block * QROWS, QROWS)
        reach = (block + 1) * QROWS
        keys, values = k_ref[:reach, :], v_ref[:reach, :]
        query = q_ref[rows, :]
        begin = begin_ref[rows, :1]
        outs, logs = [], []
        for head in range(2):
            own = head_lanes(QROWS, head)
            scores = masked_scores(jnp.where(own, query, jnp.zeros_like(query)), keys, begin, block, reach)
            highest = jnp.max(scores, axis=-1, keepdims=True)
            exponent = jnp.exp(scores - highest)
            total = jnp.sum(exponent, axis=-1, keepdims=True)
            probs = (exponent * (1.0 / total)).astype(BF)
            outs.append(dot(probs, values))
            logs.append(highest + jnp.log(total))
        first = head_lanes(QROWS, 0)
        o_ref[rows, :] = jnp.where(first, outs[0], outs[1]).astype(BF)
        lse_ref[rows, :] = jnp.where(first, logs[0], logs[1])
    for m in range(LENGTH // UNIT):
        there = pl.ds(pl.multiple_of(where_ref[m] * UNIT, UNIT), UNIT)
        mixed_ref[there, :] = o_ref[pl.ds(m * UNIT, UNIT), :]


def attend_back_kernel(
    where_ref, grad_ref, cos_ref, low_ref, high_ref, begin_ref, q_ref, k_ref, v_ref, o_ref, lse_ref,
    out_ref, do_ref, dq_ref, dk_ref, dv_ref,
):
    for m in range(LENGTH // UNIT):
        there = pl.ds(pl.multiple_of(where_ref[m] * UNIT, UNIT), UNIT)
        do_ref[pl.ds(m * UNIT, UNIT), :] = grad_ref[there, :]
    for block in reversed(range(LENGTH // QROWS)):
        rows = pl.ds(block * QROWS, QROWS)
        reach = (block + 1) * QROWS
        keys, values = k_ref[:reach, :], v_ref[:reach, :]
        query, upstream, kept = q_ref[rows, :], do_ref[rows, :], o_ref[rows, :].astype(F32)
        begin = begin_ref[rows, :1]
        grads = []
        for head in range(2):
            own = head_lanes(QROWS, head)
            query_own = jnp.where(own, query, jnp.zeros_like(query))
            up_own = jnp.where(own, upstream, jnp.zeros_like(upstream))
            scores = masked_scores(query_own, keys, begin, block, reach)
            probs = jnp.exp(scores - lse_ref[rows, head * HEAD : head * HEAD + 1])
            centre = jnp.sum(up_own.astype(F32) * kept, axis=-1, keepdims=True)
            moved = (probs * (dot_right(up_own, values) - centre)).astype(BF)
            grads.append(dot(moved, keys))
            dk = dot_left(moved, query_own)
            dv = dot_left(probs.astype(BF), up_own)
            if block == LENGTH // QROWS - 1 and head == 0:
                dk_ref[...] = dk
                dv_ref[...] = dv
            else:
                dk_ref[:reach, :] += dk
                dv_ref[:reach, :] += dv
        first = head_lanes(QROWS, 0)
        dq_ref[rows, :] = jnp.where(first, grads[0], grads[1]) * (1.0 / math.sqrt(HEAD))
    for m in range(LENGTH // UNIT):
        here = pl.ds(m * UNIT, UNIT)
        there = pl.ds(pl.multiple_of(where_ref[m] * UNIT, UNIT), UNIT)
        cosine, low, high = cos_ref[here, :], -low_ref[here, :], -high_ref[here, :]
        out_ref[there, :128] = turned(dq_ref[here, :], cosine, low, high).astype(BF)
        out_ref[there, 128:256] = turned(dk_ref[here, :], cosine, low, high).astype(BF)
        out_ref[there, 256:] = dv_ref[here, :].astype(BF)


def vmem():
    return pl.BlockSpec(memory_space=pltpu.VMEM)


def attend(where, proj, tables):
    small = jax.ShapeDtypeStruct((LENGTH, 128), BF)
    return pl.pallas_call(
        attend_kernel,
        out_shape=[small, small, small, small, small, jax.ShapeDtypeStruct((LENGTH, 128), F32)],
        in_specs=[pl.BlockSpec(memory_space=pltpu.SMEM)] + [vmem()] * 5,
        out_specs=[vmem()] * 6,
        compiler_params=pltpu.CompilerParams(vmem_limit_bytes=40 * 1024 * 1024),
        cost_estimate=pl.CostEstimate(flops=2_000_000_000, bytes_accessed=6_000_000, transcendentals=1_500_000),
    )(where, proj, *tables)


def attend_back(where, grad, tables, kept):
    return pl.pallas_call(
        attend_back_kernel,
        out_shape=jax.ShapeDtypeStruct((LENGTH, 384), BF),
        in_specs=[pl.BlockSpec(memory_space=pltpu.SMEM)] + [vmem()] * 10,
        out_specs=vmem(),
        scratch_shapes=[pltpu.VMEM((LENGTH, 128), BF)] + [pltpu.VMEM((LENGTH, 128), F32)] * 3,
        compiler_params=pltpu.CompilerParams(vmem_limit_bytes=40 * 1024 * 1024),
        cost_estimate=pl.CostEstimate(flops=5_000_000_000, bytes_accessed=6_000_000, transcendentals=1_500_000),
    )(where, grad, *tables, *kept)


def rotary_tables(places):
    half = ROT // 2
    frequency = 1.0 / 10000.0 ** (jnp.arange(half).astype(F32) * 2.0 / ROT)
    angles = places.astype(F32)[:, None] * frequency[None, :]
    cosine, sine = jnp.cos(angles), jnp.sin(angles)
    rest = HEAD - ROT
    nought = jnp.zeros((LENGTH, half), F32)
    blank = jnp.zeros((LENGTH, rest), F32)
    cos_head = jnp.concatenate([cosine, cosine, jnp.ones((LENGTH, rest), F32)], axis=1)
    low_head = jnp.concatenate([nought, sine, blank], axis=1)
    high_head = jnp.concatenate([-sine, nought, blank], axis=1)
    begin = jnp.arange(LENGTH, dtype=jnp.int32) - places
    return (
        jnp.concatenate([cos_head, cos_head], axis=1),
        jnp.concatenate([low_head, low_head], axis=1),
        jnp.concatenate([high_head, high_head], axis=1),
        jnp.broadcast_to(begin[:, None], (LENGTH, 128)),
    )


def gather_rows(mine):
    own = [mine] + [along_x(mine, -r) for r in (1, 2, 3)]
    other = [across_cores(block) for block in own]
    return jnp.concatenate([rows for pair in zip(own, other) for rows in pair], axis=0), other[0]


def scatter_sum(partial):
    blocks = partial.reshape(4, 2, LENGTH // 8, WIDTH)
    total = None
    for r in (2, 1, 3, 0):
        joined = blocks[r, 0].astype(F32) + across_cores(blocks[r, 1]).astype(F32)
        if r:
            joined = along_x(joined.astype(BF), r).astype(F32)
        total = joined if total is None else total + joined
    return total


def normalized(rows):
    values = rows.astype(F32)
    centre = jnp.mean(values, axis=-1, keepdims=True)
    centred = values - centre
    spread = jnp.mean(centred * centred, axis=-1, keepdims=True)
    scale = lax.rsqrt(spread + NORM_EPS)
    return centred * scale, scale


def norm_back(grad, rows):
    unit, scale = normalized(rows)
    mean_grad = jnp.mean(grad, axis=-1, keepdims=True)
    mean_both = jnp.mean(grad * unit, axis=-1, keepdims=True)
    return scale * (grad - mean_grad - unit * mean_both)


def gelu(values):
    return 0.5 * values * (1.0 + lax.erf(values * (1.0 / math.sqrt(2.0))))


def gelu_slope(values):
    phi = jnp.exp(-0.5 * values * values) * (1.0 / math.sqrt(2.0 * math.pi))
    return 0.5 * (1.0 + lax.erf(values * (1.0 / math.sqrt(2.0)))) + values * phi


def shards(
    tokens, positions, w_qkv, b_qkv, w_dense, b_dense, w_up, b_up, w_down, b_down,
    norm1_gain, norm1_shift, norm2_gain, norm2_shift, cotangent,
):
    core = lax.axis_index("section")
    seq = lax.axis_index("seq")
    shard = lax.axis_index("wshard")
    x, zh = seq // 2, seq % 2
    y, zl = shard // 2, shard % 2
    part = 2 * x + core

    def own_rows(array):
        own = lax.dynamic_slice_in_dim(pick(array, zh), core * UNIT, UNIT, 0)
        lent = lax.dynamic_slice_in_dim(pick(array, 1 - zh), core * UNIT, UNIT, 0)
        return jnp.concatenate([own, across_high(lent)], axis=0)

    unit_no = jnp.arange(16, dtype=jnp.int32)
    where = (
        ((unit_no // 4 - x) % 4) * 4
        + jnp.bitwise_xor(unit_no % 2, core) * 2
        + jnp.bitwise_xor((unit_no // 2) % 2, zh)
    ).astype(jnp.int32)
    tables = rotary_tables(pick(positions, zh))

    def both_layers(for_self, for_other):
        other = across_cores(for_other)
        return jnp.where(core == 0, for_self, other), jnp.where(core == 0, other, for_self)

    def sliced(which):
        qkv = pick(w_qkv[0].reshape(128, 3, 8, 128), which, 2).reshape(128, 384)
        up = pick(w_up[0].reshape(128, 8, 8, 64), which, 2).reshape(128, 512)
        down = pick(w_down[0].reshape(8, 64, 1024), which, 0)
        return qkv, up, down

    mine, theirs = sliced(part), sliced(2 * x + 1 - core)
    qkv_rows = both_layers(mine[0], theirs[0])
    up_rows = both_layers(mine[1], theirs[1])
    down_rows = both_layers(mine[2], theirs[2])
    dense_rows = both_layers(w_dense[0], w_dense[0])
    vector = jnp.concatenate(
        [b_qkv[0], b_up[0], b_dense[0], b_down[0], norm1_gain[0], norm1_shift[0], norm2_gain[0], norm2_shift[0]]
    )
    vectors = both_layers(vector, vector)

    def gathered(block):
        return lax.all_gather(block, "wshard", axis=0, tiled=True)

    layers = []
    for layer in range(2):
        qkv = gathered(qkv_rows[layer])
        up = gathered(up_rows[layer])
        down = gathered(down_rows[layer])
        dense = transposed(dense_rows[layer])
        small = lax.all_gather(vectors[layer], "wshard", axis=0, tiled=False).astype(F32)
        bias_qkv = pick(small[:, :384].reshape(3, 8, 128), part, 1).reshape(384)
        bias_up = pick(small[:, 384:896].reshape(8, 8, 64), part, 1).reshape(512)
        bias_out = small[:, 896:1024].reshape(-1) + small[:, 1024:1152].reshape(-1)
        gain_one, shift_one, gain_two, shift_two = (
            small[:, 1152 + 128 * i : 1280 + 128 * i].reshape(-1) for i in range(4)
        )
        wide = jnp.concatenate(
            [
                (gain_one[:, None] * qkv.astype(F32)).astype(BF),
                (gain_two[:, None] * up.astype(F32)).astype(BF),
            ],
            axis=1,
        )
        bias = jnp.concatenate(
            [
                bias_qkv + jnp.sum(shift_one[:, None] * qkv.astype(F32), axis=0),
                bias_up + jnp.sum(shift_two[:, None] * up.astype(F32), axis=0),
            ]
        )
        layers.append((wide, bias, jnp.concatenate([down, dense], axis=0), bias_out))

    def forward(own, weights):
        wide, bias, out_weights, bias_out = weights
        rows, beside = gather_rows(own)
        unit = normalized(rows)[0].astype(BF)
        product = dot(unit, wide) + bias[None, :]
        proj, middle = product[:, :384].astype(BF), product[:, 384:]
        active = gelu(middle).astype(BF)
        mixed, *kept = attend(where, proj, tables)
        ahead = jnp.concatenate([active, mixed], axis=1)
        result = own.astype(F32) + scatter_sum(dot(ahead, out_weights).astype(BF)) + bias_out[None, :]
        return result.astype(BF), (unit, middle, ahead, kept, beside)

    def backward(own, own_input, weights, stored):
        wide, bias, out_weights, bias_out = weights
        unit, middle, ahead, kept, _ = stored
        rows, beside = gather_rows(own)
        pulled = dot_right(rows, out_weights)
        grad_middle = (pulled[:, :512] * gelu_slope(middle)).astype(BF)
        grad_proj = attend_back(where, pulled[:, 512:].astype(BF), tables, kept)
        grads = jnp.concatenate([grad_proj, grad_middle], axis=1)
        grad_unit = scatter_sum(dot_right(grads, wide).astype(BF))
        grad_input = own.astype(F32) + norm_back(grad_unit, own_input)
        out_terms = dot_left(ahead, rows).astype(BF)
        wide_terms = dot_left(unit, grads).astype(BF)
        bias_terms = jnp.concatenate(
            [
                jnp.sum(grads.astype(F32), axis=0),
                jnp.sum(lax.dynamic_slice_in_dim(rows, part * 128, 128, 1).astype(F32), axis=0),
            ]
        )
        return grad_input, (wide_terms, out_terms, bias_terms), beside

    def reduced(terms):
        wide_terms, out_terms, bias_terms = terms
        down = out_terms[:512].reshape(4, 2, 64, 1024)
        down = jnp.concatenate([down[..., :512], down[..., 512:]], axis=2)
        dense = out_terms[512:].reshape(128, 4, 2, 128).transpose(1, 2, 0, 3)
        pieces = jnp.concatenate([wide_terms.reshape(4, 2, 128, 896), down, dense], axis=3)
        tail = jnp.pad(bias_terms.astype(BF)[None, :], ((0, 15), (0, 512)))
        pieces = jnp.concatenate([pieces, jnp.broadcast_to(tail, (4, 2) + tail.shape)], axis=2)
        near = pick(pieces, zl, 1).astype(F32) + across_low(pick(pieces, 1 - zl, 1)).astype(F32)
        near = near.astype(BF)
        total = pick(near, y).astype(F32)
        for step in (1, 2, 3):
            total = total + along_y(pick(near, (y + step) % 4), step).astype(F32)
        total = total.astype(BF)
        total = (total.astype(F32) + across_high(total).astype(F32)).astype(BF)
        dense = transposed(total[:128, 1408:])
        return jnp.concatenate([total[:, :1408], jnp.pad(dense, ((0, 16), (0, 0)))], axis=1)

    def collected(first, second):
        rounds = []
        for block in (first, second):
            rounds.append(jnp.stack([block] + [along_x(block, -r) for r in (1, 2, 3)], axis=0))
        kept = jnp.where(core == 0, rounds[0], rounds[1])
        sent = across_cores(jnp.where(core == 0, rounds[1], rounds[0]))
        pair = jnp.stack([jnp.where(core == 0, kept, sent), jnp.where(core == 0, sent, kept)], axis=1)
        return jnp.roll(pair, x, axis=0).reshape(8, 144, 1536).astype(F32)

    def placed(own, beside, keeper):
        low = jnp.where(core == 0, own, beside)
        high = jnp.where(core == 0, beside, own)
        local = jnp.concatenate([low[:UNIT], high[:UNIT]], axis=0)
        lent = across_high(jnp.concatenate([low[UNIT:], high[UNIT:]], axis=0))
        return jnp.stack([jnp.where(zh == 0, local, lent), jnp.where(zh == 0, lent, local)], axis=0)

    own_tokens = own_rows(tokens)
    own_cotangent = own_rows(cotangent)
    hidden_one, stored_one = forward(own_tokens, layers[0])
    hidden_two, stored_two = forward(hidden_one, layers[1])
    grad_two, terms_two, _ = backward(own_cotangent, hidden_one, layers[1], stored_two)
    grad_mid = grad_two.astype(BF)
    grad_one, terms_one, grad_beside = backward(grad_mid, own_tokens, layers[0], stored_one)
    sums_two = reduced(terms_two)
    sums_one = reduced(terms_one)
    sums = collected(sums_one, sums_two)

    hidden = jnp.where(
        core == 0,
        placed(hidden_one, stored_two[4], 0),
        placed(hidden_two, across_cores(hidden_two), 1),
    )
    grad_low = grad_one.astype(BF)
    in_grads = jnp.where(
        core == 0,
        placed(grad_low, across_cores(grad_low), 0),
        placed(grad_mid, grad_beside, 1),
    ).astype(F32)

    gain_one, shift_one = norm1_gain[0].astype(F32), norm1_shift[0].astype(F32)
    gain_two, shift_two = norm2_gain[0].astype(F32), norm2_shift[0].astype(F32)
    raw_qkv = sums[:, :128, :384].reshape(8, 128, 3, 128).transpose(1, 2, 0, 3).reshape(128, 3072)
    raw_up = sums[:, :128, 384:896].reshape(8, 128, 8, 64).transpose(1, 2, 0, 3).reshape(128, 4096)
    down = sums[:, :128, 896:1408].reshape(8, 2, 64, 512).transpose(0, 2, 1, 3).reshape(512, 1024)
    dense = sums[:, :128, 1408:].transpose(1, 0, 2).reshape(128, 1024)
    sum_qkv = sums[:, 128, :384].reshape(8, 3, 128).transpose(1, 0, 2).reshape(3072)
    sum_up = sums[:, 128, 384:896].reshape(8, 8, 64).transpose(1, 0, 2).reshape(4096)
    sum_out = sums[:, 128, 896:1024].reshape(1024)
    grad_w_qkv = gain_one[:, None] * raw_qkv + shift_one[:, None] * sum_qkv[None, :]
    grad_w_up = gain_two[:, None] * raw_up + shift_two[:, None] * sum_up[None, :]
    qkv_wide, up_wide = w_qkv[0].astype(F32), w_up[0].astype(F32)
    grad_b_out = lax.dynamic_slice_in_dim(sum_out, 128 * shard, 128, 0)
    outs = (
        hidden,
        in_grads,
        grad_w_qkv,
        lax.dynamic_slice_in_dim(sum_qkv, 256 * shard, 256, 0),
        lax.dynamic_slice_in_dim(sum_qkv, 2048 + 128 * shard, 128, 0),
        dense,
        grad_b_out,
        grad_w_up,
        lax.dynamic_slice_in_dim(sum_up, 512 * shard, 512, 0),
        down,
        grad_b_out,
        jnp.sum(qkv_wide * raw_qkv, axis=1),
        jnp.sum(qkv_wide * sum_qkv[None, :], axis=1),
        jnp.sum(up_wide * raw_up, axis=1),
        jnp.sum(up_wide * sum_up[None, :], axis=1),
    )
    return tuple(out[None] for out in outs)


def solution(mesh):
    rows = P("section", "wshard", None)
    vector = P("section", "wshard")
    in_specs = (
        P("wshard", "seq", None),
        P("wshard", None),
        rows, vector, rows, vector, rows, vector, rows, vector, vector, vector, vector, vector,
        P("wshard", "seq", None),
    )
    out_specs = (
        P("section", "wshard", "seq", None),
        P("section", "wshard", "seq", None),
        rows, vector, vector, rows, vector, rows, vector, rows, vector, vector, vector, vector, vector,
    )
    return jax.shard_map(shards, mesh=mesh, in_specs=in_specs, out_specs=out_specs, check_vma=False)
```

```python
import math

import jax
import jax.numpy as jnp
from jax import lax
from jax.experimental import pallas as pl
from jax.experimental.pallas import tpu as pltpu
from jax.sharding import Mesh
from jax.sharding import PartitionSpec as P

HEAD = 64
ROT = 16
NORM_EPS = 1e-05
BF = jnp.bfloat16
F32 = jnp.float32
AXES = ("core", "x", "z_hi", "y", "z_lo")
SHARDS = ("y", "z_lo")
LENGTH = 1024
WIDTH = 1024
QROWS = 256
UNIT = 64


def place_of(index):
    return index // 64, (index // 16) % 4, (index // 8) % 2, (index // 2) % 4, index % 2


def index_of(core, x, zh, y, zl):
    return core * 64 + x * 16 + zh * 8 + 2 * y + zl


def route(block, target):
    targets = [target(*place_of(i)) for i in range(128)]
    pairs = [(i, index_of(*place)) for i, place in enumerate(targets) if place is not None]
    return lax.ppermute(block, AXES, pairs)


def from_all(block, axes):
    count = math.prod(lax.axis_size(axis) for axis in axes)
    return swapped(jnp.broadcast_to(block[None], (count, *block.shape)), axes)


def swapped(blocks, axes):
    return lax.all_to_all(blocks, axes, split_axis=0, concat_axis=0, tiled=True)


def along_x(block, step):
    return route(block, lambda c, x, zh, y, zl: (c, (x + step) % 4, zh, y, zl))


def along_y(block, step):
    return route(block, lambda c, x, zh, y, zl: (c, x, zh, (y + step) % 4, zl))


def across_low(block):
    return route(block, lambda c, x, zh, y, zl: (c, x, zh, y, 1 - zl))


def across_cores(block):
    return route(block, lambda c, x, zh, y, zl: (1 - c, x, zh, y, zl))


def across_high(block):
    return route(block, lambda c, x, zh, y, zl: (c, x, 1 - zh, y, zl))


def transposed(block):
    return route(block, lambda c, x, zh, y, zl: (zl, y, zh, x, c))


def pick(array, index, axis=0):
    return lax.dynamic_index_in_dim(array, index, axis, keepdims=False)


def dot(left, right):
    return jnp.dot(left, right, preferred_element_type=F32)


def dot_left(left, right):
    return lax.dot_general(left, right, (((0,), (0,)), ((), ())), preferred_element_type=F32)


def dot_right(left, right):
    return lax.dot_general(left, right, (((1,), (1,)), ((), ())), preferred_element_type=F32)


def head_lanes(rows, head):
    lanes = lax.broadcasted_iota(jnp.int32, (rows, 2 * HEAD), 1)
    return (lanes >= head * HEAD) & (lanes < (head + 1) * HEAD)


def turned(values, cosine, sine_low, sine_high):
    return (
        values * cosine
        + pltpu.roll(values, ROT // 2, 1) * sine_low
        + pltpu.roll(values, 2 * HEAD - ROT // 2, 1) * sine_high
    )


def masked_scores(query, keys, begin, block, reach):
    scores = dot_right(query, keys)
    rows = block * QROWS + lax.broadcasted_iota(jnp.int32, (QROWS, reach), 0)
    columns = lax.broadcasted_iota(jnp.int32, (QROWS, reach), 1)
    seen = (columns <= rows) & (columns >= begin)
    return jnp.where(seen, scores, -1e30)


def unit_rows(where_ref, m):
    return pl.ds(pl.multiple_of(where_ref[m] * UNIT, UNIT), UNIT)


def attend(where_ref, proj_ref, tables, mixed_ref, q_ref, k_ref, v_ref, o_ref, lse_ref):
    cos_ref, low_ref, high_ref, begin_ref = tables
    for m in range(LENGTH // UNIT):
        here = pl.ds(m * UNIT, UNIT)
        proj = proj_ref[unit_rows(where_ref, m), :]
        cosine, low, high = cos_ref[here, :], low_ref[here, :], high_ref[here, :]
        query = turned(proj[:, :128].astype(F32), cosine, low, high)
        q_ref[here, :] = (query.astype(BF).astype(F32) * (1.0 / math.sqrt(HEAD))).astype(BF)
        k_ref[here, :] = turned(proj[:, 128:256].astype(F32), cosine, low, high).astype(BF)
        v_ref[here, :] = proj[:, 256:]
    for block in range(LENGTH // QROWS):
        rows = pl.ds(block * QROWS, QROWS)
        reach = (block + 1) * QROWS
        keys, values = k_ref[:reach, :], v_ref[:reach, :]
        query = q_ref[rows, :]
        begin = begin_ref[rows, :1]
        outs, logs = [], []
        for head in range(2):
            own = head_lanes(QROWS, head)
            scores = masked_scores(jnp.where(own, query, jnp.zeros_like(query)), keys, begin, block, reach)
            highest = jnp.max(scores, axis=-1, keepdims=True)
            exponent = jnp.exp(scores - highest)
            total = jnp.sum(exponent, axis=-1, keepdims=True)
            probs = (exponent * (1.0 / total)).astype(BF)
            outs.append(dot(probs, values))
            logs.append(highest + jnp.log(total))
        first = head_lanes(QROWS, 0)
        o_ref[rows, :] = jnp.where(first, outs[0], outs[1]).astype(BF)
        lse_ref[rows, :] = jnp.where(first, logs[0], logs[1])
    for m in range(LENGTH // UNIT):
        mixed_ref[unit_rows(where_ref, m), :] = o_ref[pl.ds(m * UNIT, UNIT), :]


def attend_back(where_ref, tables, kept, do_ref, out_ref, dq_ref, dk_ref, dv_ref):
    cos_ref, low_ref, high_ref, begin_ref = tables
    q_ref, k_ref, v_ref, o_ref, lse_ref = kept
    for block in reversed(range(LENGTH // QROWS)):
        rows = pl.ds(block * QROWS, QROWS)
        reach = (block + 1) * QROWS
        keys, values = k_ref[:reach, :], v_ref[:reach, :]
        query, upstream, mixed = q_ref[rows, :], do_ref[rows, :], o_ref[rows, :].astype(F32)
        begin = begin_ref[rows, :1]
        grads = []
        for head in range(2):
            own = head_lanes(QROWS, head)
            query_own = jnp.where(own, query, jnp.zeros_like(query))
            up_own = jnp.where(own, upstream, jnp.zeros_like(upstream))
            scores = masked_scores(query_own, keys, begin, block, reach)
            probs = jnp.exp(scores - lse_ref[rows, head * HEAD : head * HEAD + 1])
            centre = jnp.sum(up_own.astype(F32) * mixed, axis=-1, keepdims=True)
            moved = (probs * (dot_right(up_own, values) - centre)).astype(BF)
            grads.append(dot(moved, keys))
            dk = dot_left(moved, query_own)
            dv = dot_left(probs.astype(BF), up_own)
            if block == LENGTH // QROWS - 1 and head == 0:
                dk_ref[...] = dk
                dv_ref[...] = dv
            else:
                dk_ref[:reach, :] += dk
                dv_ref[:reach, :] += dv
        first = head_lanes(QROWS, 0)
        dq_ref[rows, :] = jnp.where(first, grads[0], grads[1]) * (1.0 / math.sqrt(HEAD))
    for m in range(LENGTH // UNIT):
        here = pl.ds(m * UNIT, UNIT)
        there = unit_rows(where_ref, m)
        cosine, low, high = cos_ref[here, :], -low_ref[here, :], -high_ref[here, :]
        out_ref[there, :128] = turned(dq_ref[here, :], cosine, low, high).astype(BF)
        out_ref[there, 128:256] = turned(dk_ref[here, :], cosine, low, high).astype(BF)
        out_ref[there, 256:384] = dv_ref[here, :].astype(BF)


def barrier(*values):
    flat, tree = jax.tree.flatten(values)
    anywhere = pl.BlockSpec(memory_space=pl.ANY)
    flat = pl.pallas_call(
        lambda *refs: None,
        out_shape=[jax.ShapeDtypeStruct(value.shape, value.dtype) for value in flat],
        in_specs=[anywhere] * len(flat),
        out_specs=[anywhere] * len(flat),
        input_output_aliases={k: k for k in range(len(flat))},
    )(*flat)
    return jax.tree.unflatten(tree, flat)


def after(values, *others):
    flat, tree = jax.tree.flatten(values)
    others = jax.tree.leaves(others)
    anywhere = pl.BlockSpec(memory_space=pl.ANY)
    flat = pl.pallas_call(
        lambda *refs: None,
        out_shape=[jax.ShapeDtypeStruct(value.shape, value.dtype) for value in flat],
        in_specs=[anywhere] * (len(flat) + len(others)),
        out_specs=[anywhere] * len(flat),
        input_output_aliases={k: k for k in range(len(flat))},
    )(*flat, *others)
    return jax.tree.unflatten(tree, flat)


def run(body, scalars, arrays, outs, scratch=(), flops=0, bytes_accessed=4_000_000, spaces=None, limit=60):
    vmem = pl.BlockSpec(memory_space=pltpu.VMEM)
    return pl.pallas_call(
        body,
        out_shape=[jax.ShapeDtypeStruct(*out) for out in outs],
        in_specs=[pl.BlockSpec(memory_space=pltpu.SMEM)] + (spaces or [vmem] * len(arrays)),
        out_specs=[vmem] * len(outs),
        scratch_shapes=list(scratch),
        compiler_params=pltpu.CompilerParams(vmem_limit_bytes=limit * 1024 * 1024),
        cost_estimate=pl.CostEstimate(flops=flops, bytes_accessed=bytes_accessed, transcendentals=0),
    )(scalars, *arrays)


X, CORE, ZH, Y, ZL, PART, SHARD, BIAS = 0, 1, 2, 3, 4, 5, 6, 7


def lanes(start, extent=128):
    return pl.ds(pl.multiple_of(start, extent), extent)


def low_half(rows):
    return lax.broadcasted_iota(jnp.int32, (rows, 128), 1) < 64


def half_tiles(first, second):
    low = low_half(first.shape[0])
    return (
        jnp.where(low, first, pltpu.roll(second, 64, 1)),
        jnp.where(low, pltpu.roll(first, 64, 1), second),
    )


def column(row):
    return jnp.transpose(jnp.broadcast_to(row, (128, 128)))


def slice_kernel(
    at, qkv_all, up_all, down_all, dense_all, bias_qkv_all, bias_up_all, bias_dense, bias_down, gain_one, shift_one,
    gain_two, shift_two,
    qkv_self, qkv_other, rest_self, rest_other,
    qkv, up, down, dense, bias_qkv, small, rows, sems,
):
    x, core = at[X], at[CORE]
    copies = [(up_all.at[:, lanes(512 * k + 128 * x)], up.at[k]) for k in range(8)]
    copies += [(qkv_all.at[:, lanes(1024 * k + 256 * x, 256)], qkv.at[k]) for k in range(3)]
    copies.append((down_all.at[pl.ds(pl.multiple_of(128 * x, 128), 128), :], down))
    copies.append((dense_all.at[:, lanes(256 * x, 256)], dense))
    copies.append((bias_qkv_all, bias_qkv))
    copies.append((bias_up_all.at[:, lanes(128 * x)], small.at[0]))
    for k, vector in enumerate((bias_dense, bias_down, gain_one, shift_one, gain_two, shift_two)):
        copies.append((vector, small.at[1 + k]))
    copies = [pltpu.make_async_copy(*pair, sems.at[k]) for k, pair in enumerate(copies)]
    for copy in copies:
        copy.start()
    for copy in copies:
        copy.wait()
    for k in range(4):
        zero, one = half_tiles(up[2 * k].astype(F32), up[2 * k + 1].astype(F32))
        here = slice(128 * k, 128 * k + 128)
        rest_self[:, here] = jnp.where(core == 0, zero, one).astype(BF)
        rest_other[:, here] = jnp.where(core == 0, one, zero).astype(BF)
    for k in range(3):
        first, second = qkv[k, :, :128], qkv[k, :, 128:]
        here = slice(128 * k, 128 * k + 128)
        qkv_self[:128, here] = jnp.where(core == 0, first, second)
        qkv_other[:128, here] = jnp.where(core == 0, second, first)
    for k in range(2):
        first, second = down[:64, 512 * k : 512 * k + 512], down[64:, 512 * k : 512 * k + 512]
        rest_self[64 * k : 64 * k + 64, 512:] = jnp.where(core == 0, first, second)
        rest_other[64 * k : 64 * k + 64, 512:] = jnp.where(core == 0, second, first)
    first, second = dense[:, :128], dense[:, 128:]
    qkv_self[:128, 384:] = jnp.where(core == 0, first, second)
    qkv_other[:128, 384:] = jnp.where(core == 0, second, first)
    rows[...] = jnp.zeros_like(rows)
    for k in range(3):
        rows[k : k + 1, :] = bias_qkv[:, 128 * k : 128 * k + 128].astype(F32)
    for k in range(7):
        rows[3 + k : 4 + k, :] = small[k].astype(F32)
    plain = rows[...]
    number = lax.broadcasted_iota(jnp.int32, (16, 128), 0)
    moved = jnp.where(number == 3, pltpu.roll(plain, 64, 1), plain)
    for out, upper in ((qkv_self, core), (qkv_other, 1 - core)):
        out[128:, :128] = jnp.where(upper == 0, plain, moved).astype(BF)
        out[128:, 128:] = jnp.zeros((16, 384), BF)


def tables_kernel(at, places, frequency, cos_ref, low_ref, high_ref, begin_ref):
    place = jnp.transpose(jnp.broadcast_to(places[...].astype(F32), (128, LENGTH)))
    lane = lax.broadcasted_iota(jnp.int32, (LENGTH, 128), 1) % HEAD
    angles = place * frequency[...]
    sine = jnp.sin(angles)
    cos_ref[...] = jnp.where(lane < ROT, jnp.cos(angles), 1.0)
    low_ref[...] = jnp.where((lane >= ROT // 2) & (lane < ROT), sine, 0.0)
    high_ref[...] = jnp.where(lane < ROT // 2, -sine, 0.0)
    row = lax.broadcasted_iota(jnp.int32, (LENGTH, 128), 0)
    begin_ref[...] = row - place.astype(jnp.int32)


def prepare_qkv(at, blocks, wide, wide_turned, bias, bias_out, rows):
    bias[...] = jnp.zeros_like(bias)
    for shard, message in blocks:
        vectors = message[128:, :128].astype(F32)
        rows[16 * shard : 16 * shard + 16, :] = vectors
        here = slice(128 * shard, 128 * shard + 128)
        scale = column(vectors[6:7, :])
        for k in range(0, 384, 128):
            wide[here, k : k + 128] = (message[:128, k : k + 128].astype(F32) * scale).astype(BF)
        shift = jnp.broadcast_to(vectors[7:8, :], (8, 128)).astype(BF)
        bias[:, :384] += dot(shift, message[:128, :384])
    for k in range(3):
        bias[:, 128 * k : 128 * k + 128] += jnp.broadcast_to(rows[pl.ds(at[BIAS + k], 1), :], (8, 128))
    for shard in range(8):
        total = rows[16 * shard + 4 : 16 * shard + 5, :] + rows[16 * shard + 5 : 16 * shard + 6, :]
        bias_out[:, 128 * shard : 128 * shard + 128] = jnp.broadcast_to(total, (8, 128))
    wide_turned[...] = jnp.transpose(wide[...])


def prepare_up(at, blocks, rows, up, up_turned, bias):
    bias[...] = jnp.zeros_like(bias)
    for shard, message in blocks:
        vectors = rows[16 * shard : 16 * shard + 16, :]
        here = slice(128 * shard, 128 * shard + 128)
        scale = column(vectors[8:9, :])
        for k in range(0, 512, 128):
            up[here, k : k + 128] = (message[:128, k : k + 128].astype(F32) * scale).astype(BF)
        shift = jnp.broadcast_to(vectors[9:10, :], (8, 128)).astype(BF)
        bias[...] += dot(shift, message[:128, :512])
    for k in range(4):
        first = jnp.broadcast_to(rows[32 * k + 3 : 32 * k + 4, :], (8, 128))
        second = jnp.broadcast_to(rows[32 * k + 19 : 32 * k + 20, :], (8, 128))
        bias[:, 128 * k : 128 * k + 128] += half_tiles(first, second)[0]
    up_turned[...] = jnp.transpose(up[...])


def prepare_qkv_kernel(at, messages, *refs):
    prepare_qkv(at, [(k, messages.at[k]) for k in range(8)], *refs)


def prepare_rest_kernel(at, messages, vectors, up, up_turned, bias, down, down_turned):
    prepare_up(at, [(k, messages.at[k]) for k in range(8)], vectors, up, up_turned, bias)
    prepare_down([messages.at[k, :, 512:] for k in range(8)], down, down_turned)


def prepare_wide_kernel(at, messages, *outs):
    prepare_qkv(at, [(k, messages.at[k]) for k in range(8)], *outs[:5])
    prepare_up(at, [(k, messages.at[k, :, 384:]) for k in range(8)], *outs[4:])


def prepare_down(blocks, down, down_turned):
    for k, halves in enumerate(blocks):
        down[64 * k : 64 * k + 64, :512] = halves[:64, :]
        down[64 * k : 64 * k + 64, 512:] = halves[64:128, :]
    down_turned[...] = jnp.transpose(down[...])


def prepare_down_kernel(at, messages, down, down_turned):
    prepare_down([messages.at[k] for k in range(8)], down, down_turned)


QKV = [((1024, 384), BF), ((384, 1024), BF), ((8, 384), F32), ((8, 1024), F32), ((128, 128), F32)]
UP = [((1024, 512), BF), ((512, 1024), BF), ((8, 512), F32)]
DOWN = [((512, 1024), BF), ((1024, 512), BF)]


def norm_kernel(at, *refs):
    blocks, wide, bias, unit, proj = refs[:8], *refs[8:]
    for k in range(8):
        values = blocks[k][...].astype(F32)
        centred = values - jnp.mean(values, axis=-1, keepdims=True)
        spread = jnp.mean(centred * centred, axis=-1, keepdims=True)
        unit[128 * k : 128 * k + 128, :] = (centred * lax.rsqrt(spread + NORM_EPS)).astype(BF)
    for k in range(4):
        here = slice(256 * k, 256 * k + 256)
        proj[here, :] = (dot(unit[here, :], wide[...]) + bias[:1, :]).astype(BF)


def up_kernel(at, unit, up, bias, active, slope):
    for k in range(4):
        here = slice(256 * k, 256 * k + 256)
        middle = dot(unit[here, :], up[...]) + bias[:1, :]
        share = 0.5 * (1.0 + lax.erf(middle * (1.0 / math.sqrt(2.0))))
        density = jnp.exp(-0.5 * middle * middle) * (1.0 / math.sqrt(2.0 * math.pi))
        active[here, :] = (middle * share).astype(BF)
        slope[here, :] = (share + middle * density).astype(BF)


def attend_kernel(where_ref, proj, cosine, low, high, begin, mixed, *kept):
    attend(where_ref, proj, (cosine, low, high, begin), mixed, *kept)


def project_kernel(at, active, mixed, down, dense_parts, *refs):
    blocks, dense = refs[:8], refs[8]
    for k in range(8):
        dense[:, 128 * k : 128 * k + 128] = dense_parts[k]
    for k in (2, 1, 3, 0):
        here = slice(256 * k, 256 * k + 256)
        out = dot(active[here, :], down[...]) + dot(mixed[here, :], dense[...])
        blocks[2 * k][...] = out[:128].astype(BF)
        blocks[2 * k + 1][...] = out[128:].astype(BF)


def back_front_kernel(at, *refs):
    blocks, down_turned, dense_parts, slope, grad_middle, grad_mixed, dense_turned = refs[:8], *refs[8:]
    for k in range(8):
        dense_turned[128 * k : 128 * k + 128, :] = jnp.transpose(dense_parts[k])
    for k in range(8):
        here = slice(128 * k, 128 * k + 128)
        rows = blocks[k][...]
        grad_middle[here, :] = (dot(rows, down_turned[...]) * slope[here, :].astype(F32)).astype(BF)
        grad_mixed[here, :] = dot(rows, dense_turned[...]).astype(BF)


def back_attend_kernel(where_ref, grad_mixed, grad_middle, wide_turned, up_turned, cosine, low, high, begin, *refs):
    kept, blocks, grad_proj, (do_ref, dq_ref, dk_ref, dv_ref) = refs[:5], refs[5:13], refs[13], refs[14:]
    for m in range(LENGTH // UNIT):
        do_ref[pl.ds(m * UNIT, UNIT), :] = grad_mixed[unit_rows(where_ref, m), :]
    attend_back(where_ref, (cosine, low, high, begin), kept, do_ref, grad_proj, dq_ref, dk_ref, dv_ref)
    for k in (2, 1, 3, 0):
        here = slice(256 * k, 256 * k + 256)
        out = dot(grad_proj[here, :], wide_turned[...]) + dot(grad_middle[here, :], up_turned[...])
        blocks[2 * k][...] = out[:128].astype(BF)
        blocks[2 * k + 1][...] = out[128:].astype(BF)


def shard_at(at, step, beside):
    return 2 * ((at[Y] + step) % 4) + (at[ZL] + beside) % 2


def weight_terms(at, unit, grads, outward=None, order=None):
    extent = sum(grad.shape[1] for grad in grads)
    start = 640 if outward else 0
    arrays = (unit, *grads)
    scratch = []
    counts = {None: (1, 8), "y": (4, 2), "z": (2, 4)}[order]
    shapes = [((counts[1], 144, start + extent), BF)] * counts[0]
    if outward:
        active, mixed, rows, grad_middle = outward
        arrays = (*arrays, active, mixed, grad_middle, *rows)
        scratch = [pltpu.VMEM((512, 1024), F32), pltpu.VMEM((128, 1024), F32)]

    def body(at, unit, *refs):
        grad_refs, refs = refs[: len(grads)], refs[len(grads) :]
        if outward:
            (active, mixed, grad_middle), rows, refs = refs[:3], refs[3:11], refs[11:]
        outs, refs = refs[: len(shapes)], refs[len(shapes) :]
        places = []
        for step in range(4):
            for beside in range(2):
                if order == "y":
                    places.append((outs[step].at[beside], shard_at(at, step, beside)))
                elif order == "z":
                    places.append((outs[beside].at[step], shard_at(at, step, beside)))
                else:
                    places.append((outs[0].at[2 * step + beside], 2 * step + beside))
        if outward:
            down, dense = refs
            sums = jnp.zeros((1, 128), F32)
            for k in range(8):
                here = slice(128 * k, 128 * k + 128)
                block = rows[k][...]
                more_down = dot_left(active[here, :], block)
                more_dense = dot_left(mixed[here, :], block)
                if k == 0:
                    down[...] = more_down
                    dense[...] = more_dense
                else:
                    down[...] += more_down
                    dense[...] += more_dense
                sums = sums + jnp.sum(rows[k][:, lanes(128 * at[PART])].astype(F32), axis=0, keepdims=True)
            sums_up = jnp.sum(grad_middle[...].astype(F32), axis=0, keepdims=True)
            for place, shard in places:
                piece = down[pl.ds(pl.multiple_of(64 * shard, 64), 64), :].astype(BF)
                place[:64, :512] = piece[:, :512]
                place[64:128, :512] = piece[:, 512:]
                place[:128, 512:640] = dense[:, lanes(128 * shard)].astype(BF)
                place[128:, :128] = jnp.broadcast_to(sums, (16, 128)).astype(BF)
                place[128:, 128:640] = jnp.broadcast_to(sums_up, (16, 512)).astype(BF)
        at_column = start
        for grad in grad_refs:
            columns = grad.shape[1]
            here = slice(at_column, at_column + columns)
            sums = jnp.sum(grad[...].astype(F32), axis=0, keepdims=True)
            for place, shard in places:
                terms = dot_left(unit[:, lanes(128 * shard)], grad[...])
                place[:128, here] = terms.astype(BF)
                place[128:, here] = jnp.broadcast_to(sums, (16, columns)).astype(BF)
            at_column += columns

    outs = run(body, at, arrays, shapes, scratch, flops=2 * 1024 * 1024 * (extent + start))
    return outs if order else outs[0]


def final_kernel(at, *refs):
    firsts, seconds = refs[:2], refs[2:10]
    qkv, up, gain_one, shift_one, gain_two, shift_two = refs[10:16]
    grad_qkv, grad_up, grad_down, grad_dense = refs[16:20]
    bias_qk, bias_v, bias_up, bias_out, gain_a, shift_a, gain_b, shift_b = refs[20:28]
    sums, sums_qkv, sums_up, sums_out, sems = refs[28:]
    x, core, shard = at[X], at[CORE], at[SHARD]

    @pl.when(core == 0)
    def _():
        copies = [pltpu.make_async_copy(firsts[k], sums.at[k], sems.at[k]) for k in range(2)]
        for copy in copies:
            copy.start()
        for copy in copies:
            copy.wait()

    @pl.when(core == 1)
    def _():
        copies = []
        for k in range(2):
            for r in range(4):
                target = sums.at[k, (x + r) % 4]
                copies.append(pltpu.make_async_copy(seconds[4 * k + r], target, sems.at[len(copies)]))
        for copy in copies:
            copy.start()
        for copy in copies:
            copy.wait()

    def whole(beside, r, columns):
        return sums[beside, r, :128, columns].astype(F32)

    def below(beside, r, columns):
        return sums[beside, r, 128:, columns].astype(F32)

    gain_col, shift_col = column(gain_one[...].astype(F32)), column(shift_one[...].astype(F32))
    gain_col_two, shift_col_two = column(gain_two[...].astype(F32)), column(shift_two[...].astype(F32))
    totals = [jnp.zeros((128, 128), F32) for _ in range(4)]
    for r in range(4):
        column_no = r
        for half in range(2):
            beside = (core + half) % 2
            part = 2 * column_no + half
            for k in range(3):
                cols = slice(1152 + 128 * k, 1280 + 128 * k)
                raw = whole(beside, r, cols)
                total = below(beside, r, cols)[:1]
                place = lanes(1024 * k + 128 * part)
                weight = qkv[:, place].astype(F32)
                grad_qkv[:, place] = gain_col * raw + shift_col * total
                sums_qkv[pl.ds(8 * k + part, 1), :] = total
                totals[0] += weight * raw
                totals[1] += weight * total
            grad_down[pl.ds(pl.multiple_of(64 * part, 64), 64), :512] = sums[beside, r, :64, :512].astype(F32)
            grad_down[pl.ds(pl.multiple_of(64 * part, 64), 64), 512:] = sums[beside, r, 64:128, :512].astype(F32)
            grad_dense[:, lanes(128 * part)] = whole(beside, r, slice(512, 640))
            sums_out[pl.ds(part, 1), :] = below(beside, r, slice(0, 128))[:1]
        zero, one = core % 2, (core + 1) % 2
        for k in range(4):
            cols = slice(640 + 128 * k, 768 + 128 * k)
            beneath = slice(128 + 128 * k, 256 + 128 * k)
            raws = half_tiles(whole(zero, r, cols), whole(one, r, cols))
            adds = half_tiles(below(zero, r, beneath), below(one, r, beneath))
            for odd in range(2):
                raw, total = raws[odd], adds[odd][:1]
                place = lanes(1024 * k + 512 * odd + 128 * column_no)
                weight = up[:, place].astype(F32)
                grad_up[:, place] = gain_col_two * raw + shift_col_two * total
                sums_up[pl.ds(8 * k + 4 * odd + column_no, 1), :] = total
                totals[2] += weight * raw
                totals[3] += weight * total
    for out, total in zip((gain_a, shift_a, gain_b, shift_b), totals):
        out[...] = jnp.sum(jnp.transpose(total), axis=0, keepdims=True)
    for k in range(2):
        bias_qk[:, 128 * k : 128 * k + 128] = sums_qkv[pl.ds(2 * shard + k, 1), :]
    bias_v[...] = sums_qkv[pl.ds(16 + shard, 1), :]
    for k in range(4):
        bias_up[:, 128 * k : 128 * k + 128] = sums_up[pl.ds(4 * shard + k, 1), :]
    bias_out[...] = sums_out[pl.ds(shard, 1), :]


def added(*blocks):
    total = blocks[0].astype(F32)
    for block in blocks[1:]:
        total = total + block.astype(F32)
    return total


def gather_rows(mine):
    own = [mine] + [along_x(mine, -r) for r in (1, 2, 3)]
    other = [across_cores(block) for block in own]
    return [rows for pair in zip(own, other) for rows in pair]


def joined_cores(blocks):
    joined = {r: added(blocks[2 * r], across_cores(blocks[2 * r + 1])) for r in (2, 1, 3, 0)}
    return [joined[0]] + [joined[r].astype(BF) for r in (1, 2, 3)]


def joined_chips(joined):
    return added(joined[0], *(along_x(joined[r], r) for r in (1, 2, 3)))


def summed(blocks):
    return jnp.sum(blocks.astype(F32), axis=0)


def normalized(rows):
    values = rows.astype(F32)
    centre = jnp.mean(values, axis=-1, keepdims=True)
    centred = values - centre
    spread = jnp.mean(centred * centred, axis=-1, keepdims=True)
    scale = lax.rsqrt(spread + NORM_EPS)
    return centred * scale, scale


def norm_back(grad, rows):
    unit, scale = normalized(rows)
    mean_grad = jnp.mean(grad, axis=-1, keepdims=True)
    mean_both = jnp.mean(grad * unit, axis=-1, keepdims=True)
    return scale * (grad - mean_grad - unit * mean_both)


def shards(
    tokens, positions, w_qkv, b_qkv, w_dense, b_dense, w_up, b_up, w_down, b_down,
    norm1_gain, norm1_shift, norm2_gain, norm2_shift, cotangent,
):
    core, x, zh, y, zl = (lax.axis_index(axis) for axis in AXES)
    shard = 2 * y + zl
    part = 2 * x + core
    first_core = core == 0
    anywhere, vmem = pl.BlockSpec(memory_space=pl.ANY), pl.BlockSpec(memory_space=pltpu.VMEM)

    bias_rows = [16 * ((8 * k + part) // 3) + (8 * k + part) % 3 for k in range(3)]
    at = jnp.stack([x, core, zh, y, zl, part, shard] + bias_rows).astype(jnp.int32)
    unit_no = jnp.arange(16, dtype=jnp.int32)
    where = (
        ((unit_no // 4 - x) % 4) * 4
        + jnp.bitwise_xor(unit_no % 2, core) * 2
        + jnp.bitwise_xor((unit_no // 2) % 2, zh)
    ).astype(jnp.int32)

    def own_rows(array):
        own = lax.dynamic_slice_in_dim(pick(array, zh), core * UNIT, UNIT, 0)
        lent = lax.dynamic_slice_in_dim(pick(array, 1 - zh), core * UNIT, UNIT, 0)
        return jnp.concatenate([own, across_high(lent)], axis=0)

    own_tokens = own_rows(tokens)

    sliced = run(
        slice_kernel,
        at,
        (
            w_qkv[0], w_up[0], w_down[0], w_dense[0], b_qkv, b_up, b_dense, b_down,
            norm1_gain, norm1_shift, norm2_gain, norm2_shift,
        ),
        [((144, 512), BF)] * 2 + [((128, 1024), BF)] * 2,
        [
            pltpu.VMEM((3, 128, 256), BF),
            pltpu.VMEM((8, 128, 128), BF),
            pltpu.VMEM((128, 1024), BF),
            pltpu.VMEM((128, 256), BF),
            pltpu.VMEM((1, 384), BF),
            pltpu.VMEM((7, 1, 128), BF),
            pltpu.VMEM((16, 128), F32),
            pltpu.SemaphoreType.DMA((21,)),
        ],
        spaces=[pl.BlockSpec(memory_space=pltpu.HBM)] * 12,
    )
    qkv_theirs, rest_theirs = across_cores(sliced[1]), across_cores(sliced[3])
    qkv, qkv_two = jnp.where(first_core, sliced[0], qkv_theirs), jnp.where(first_core, qkv_theirs, sliced[0])
    qkv = jnp.concatenate([qkv, qkv_two[:, 384:]], axis=1)
    rest = jnp.where(first_core, sliced[2], rest_theirs)
    rest_two = jnp.where(first_core, rest_theirs, sliced[2])
    wide_two = jnp.concatenate([qkv_two[:, :384], jnp.pad(rest_two[:, :512], ((0, 16), (0, 0)))], axis=1)
    down_two = rest_two[:, 512:]

    half = ROT // 2
    frequency = 1.0 / 10000.0 ** (jnp.arange(half).astype(F32) * 2.0 / ROT)
    frequency = jnp.concatenate([jnp.tile(frequency, HEAD // half)] * 2)[None, :]
    tables = run(
        tables_kernel,
        at,
        (lax.dynamic_slice_in_dim(positions, zh, 1, 0), frequency),
        [((LENGTH, 128), F32)] * 3 + [((LENGTH, 128), jnp.int32)],
    )

    def front(rows, wide, bias):
        return run(
            norm_kernel, at, (*rows, wide, bias), [((1024, 1024), BF), ((1024, 384), BF)], flops=1_000_000_000
        )

    def front_up(unit, up, bias):
        return run(up_kernel, at, (unit, up, bias), [((1024, 512), BF)] * 2, flops=1_000_000_000)

    def attention(proj):
        outs = run(
            attend_kernel,
            where,
            (proj, *tables),
            [((1024, 128), BF)] * 5 + [((1024, 128), F32)],
            flops=4_000_000_000,
        )
        return outs[0], outs[1:]

    def project(active, mixed, down, dense):
        return run(
            project_kernel,
            at,
            (active, mixed, down, dense),
            [((128, 1024), BF)] * 8,
            [pltpu.VMEM((128, 1024), BF)],
            flops=1_500_000_000,
        )

    def back_front(rows, down_turned, dense, slope):
        return run(
            back_front_kernel,
            at,
            (*rows, down_turned, dense, slope),
            [((1024, 512), BF), ((1024, 128), BF)],
            [pltpu.VMEM((1024, 128), BF)],
            flops=1_500_000_000,
        )

    def back_attend(grad_mixed, grad_middle, qkv_turned, up_turned, kept):
        outs = run(
            back_attend_kernel,
            where,
            (grad_mixed, grad_middle, qkv_turned, up_turned, *tables, *kept),
            [((128, 1024), BF)] * 8 + [((1024, 384), BF)],
            [pltpu.VMEM((1024, 128), BF)] + [pltpu.VMEM((1024, 128), F32)] * 3,
            flops=6_000_000_000,
        )
        return outs[:8], outs[8]

    qkvs = from_all(after(qkv, own_tokens), SHARDS)
    rows_one = gather_rows(own_tokens)
    qkv_one, qkv_turned_one, qkv_bias, bias_out_one, vectors = run(prepare_qkv_kernel, at, (qkvs,), QKV)
    dense = jnp.stack([qkvs[:, :128, 384:512], qkvs[:, :128, 512:]], axis=1)
    dense = swapped(after(dense, rows_one[2::2]), ("x", "core"))
    dense_one, dense_two = dense[:, 0], dense[:, 1]
    rests = from_all(after(rest, dense_one, dense_two), SHARDS)
    unit_one, proj = front(rows_one, qkv_one, qkv_bias)
    mixed_one, kept_one = attention(proj)
    rests, wide_two = after((rests, wide_two), mixed_one)

    up_one, up_turned_one, up_bias, down_one, down_turned_one = run(
        prepare_rest_kernel, at, (rests, vectors), UP + DOWN
    )
    active_one, slope_one = front_up(unit_one, up_one, up_bias)
    wides = from_all(after(wide_two, rests), SHARDS)
    blocks = project(active_one, mixed_one, down_one, dense_one)
    joined = joined_cores(blocks)
    hidden_one = own_tokens.astype(F32) + joined_chips(joined) + bias_out_one[:1, :]
    hidden_one = hidden_one.astype(BF)
    rows_two = gather_rows(hidden_one)
    downs = from_all(after(down_two, wides), SHARDS)
    own_cotangent = own_rows(after(cotangent, rows_two[2::2]))
    qkv_two, qkv_turned_two, qkv_bias, bias_out_two, _, up_two, up_turned_two, up_bias = run(
        prepare_wide_kernel, at, (wides,), QKV + UP
    )

    grad_own = [own_cotangent] + [along_x(own_cotangent, -r) for r in (1, 2, 3)]
    unit_two, proj = front(rows_two, qkv_two, qkv_bias)
    mixed_two, kept_two = attention(proj)
    active_two, slope_two = front_up(unit_two, up_two, up_bias)
    grad_own = after(grad_own, active_two, mixed_two)
    grad_rows = [rows for block in grad_own for rows in (block, across_cores(block))]
    down_two, down_turned_two = run(prepare_down_kernel, at, (downs,), DOWN)

    grad_middle, grad_mixed = back_front(grad_rows, down_turned_two, dense_two, slope_two)
    blocks, grad_proj = back_attend(grad_mixed, grad_middle, qkv_turned_two, up_turned_two, kept_two)
    joined = joined_cores(blocks)
    unit_late = after(unit_two, joined)
    out_sums = weight_terms(at, unit_late, (), (active_two, mixed_two, grad_rows, grad_middle))
    wide_sums = weight_terms(at, unit_late, (grad_middle, grad_proj))
    joined[0] = after(joined[0], out_sums, wide_sums)
    out_sums = swapped(out_sums, SHARDS)
    grad_two = own_cotangent.astype(F32) + norm_back(joined_chips(joined), hidden_one)
    grad_mid = grad_two.astype(BF)
    grad_rows = gather_rows(grad_mid)
    grad_rows, out_sums, wide_sums = barrier(grad_rows, out_sums, wide_sums)

    wide_sums = swapped(wide_sums, SHARDS)
    grad_middle, grad_mixed = back_front(grad_rows, down_turned_one, dense_one, slope_one)
    early_sums = weight_terms(at, unit_one, (grad_middle,), (active_one, mixed_one, grad_rows, grad_middle))
    blocks, grad_proj = back_attend(grad_mixed, grad_middle, qkv_turned_one, up_turned_one, kept_one)
    blocks, grad_proj, wide_sums, early_sums = barrier(blocks, grad_proj, wide_sums, early_sums)

    def turned_dense(total):
        dense = jnp.concatenate([transposed(total[:128, 512:640]), total[128:, 512:640]], axis=0)
        return jnp.concatenate([total[:, :512], dense, total[:, 640:]], axis=1)

    def to_keeper(parts, layer):
        return route(parts, lambda c, x, zh, y, zl: (layer, x, zh, y, zl) if c != layer else None)

    early_sums = swapped(early_sums, SHARDS)
    joined = joined_cores(blocks)
    late_sums = weight_terms(at, unit_one, (grad_proj,))
    grad_one = grad_mid.astype(F32) + norm_back(joined_chips(joined), own_tokens)
    grad_low = grad_one.astype(BF)
    joined = joined_cores(project(after(active_two, late_sums), mixed_two, down_two, dense_two))
    hidden_two = hidden_one.astype(F32) + joined_chips(joined) + bias_out_two[:1, :]
    hidden_two = hidden_two.astype(BF)
    second = turned_dense(jnp.concatenate([summed(out_sums), summed(wide_sums)], axis=1).astype(BF))
    second_high = across_high(second)
    early_sums, late_sums, grad_low, hidden_two, second, second_high = barrier(
        early_sums, late_sums, grad_low, hidden_two, second, second_high
    )
    late_sums = swapped(late_sums, SHARDS)
    second = added(second, second_high).astype(BF)
    second = [second] + [along_x(second, -r) for r in (1, 2, 3)]
    early = summed(early_sums).astype(BF)
    early_high = across_high(early)
    grad_beside, hidden_beside = across_cores(grad_low), across_cores(hidden_two)
    late_sums, second, early, early_high, grad_beside, hidden_beside = barrier(
        late_sums, second, early, early_high, grad_beside, hidden_beside
    )
    late = summed(late_sums).astype(BF)
    late = added(late, across_high(late)).astype(BF)
    early = turned_dense(added(early, early_high).astype(BF))
    late, early, second = barrier(late, early, second)
    first = from_all(jnp.concatenate([early, late], axis=1), ("x",))
    second_sums = second + [to_keeper(block, 1) for block in second]

    def placed(pairs):
        local, lent = [], []
        for own, beside in pairs:
            low = jnp.where(first_core, own, beside)
            high = jnp.where(first_core, beside, own)
            local.append(jnp.concatenate([low[:UNIT], high[:UNIT]], axis=0))
            lent.append(jnp.concatenate([low[UNIT:], high[UNIT:]], axis=0))
        local, lent = jnp.stack(local), across_high(jnp.stack(lent))
        return jnp.stack([jnp.where(zh == 0, local, lent), jnp.where(zh == 0, lent, local)], axis=1)

    outputs = placed(
        [
            (jnp.where(first_core, hidden_one, hidden_two), jnp.where(first_core, rows_two[1], hidden_beside)),
            (jnp.where(first_core, grad_low, grad_mid), jnp.where(first_core, grad_beside, grad_rows[1])),
        ]
    )
    hidden, in_grads = outputs[0], outputs[1].astype(F32)
    first, second_sums, in_grads = barrier(first, second_sums, in_grads)
    first_sums = [first, to_keeper(first, 0)]

    outs = run(
        final_kernel,
        at,
        (
            *first_sums, *second_sums,
            w_qkv[0], w_up[0], norm1_gain, norm1_shift, norm2_gain, norm2_shift,
        ),
        [((128, 3072), F32), ((128, 4096), F32), ((512, 1024), F32), ((128, 1024), F32)]
        + [((1, 256), F32), ((1, 128), F32), ((1, 512), F32)]
        + [((1, 128), F32)] * 5,
        [
            pltpu.VMEM((2, 4, 144, 1536), BF),
            pltpu.VMEM((24, 128), F32),
            pltpu.VMEM((32, 128), F32),
            pltpu.VMEM((8, 128), F32),
            pltpu.SemaphoreType.DMA((8,)),
        ],
        spaces=[anywhere] * 10 + [vmem] * 6,
    )
    grad_qkv, grad_up, grad_down, grad_dense, bias_qk, bias_v, bias_up, bias_out, *norms = outs
    return (
        hidden[None], in_grads[None], grad_qkv[None], bias_qk, bias_v, grad_dense[None], bias_out,
        grad_up[None], bias_up, grad_down[None], bias_out, *norms,
    )


def solution(mesh):
    mesh = Mesh(mesh.devices.reshape(2, 4, 2, 4, 2), AXES)
    rows = P("core", SHARDS, None)
    vector = P("core", SHARDS)
    tokens = P(SHARDS, ("x", "z_hi"), None)
    layered = P("core", SHARDS, ("x", "z_hi"), None)
    in_specs = (
        tokens, P(SHARDS, None),
        rows, vector, rows, vector, rows, vector, rows, vector, vector, vector, vector, vector,
        tokens,
    )
    out_specs = (
        layered, layered,
        rows, vector, vector, rows, vector, rows, vector, rows, vector, vector, vector, vector, vector,
    )
    return jax.shard_map(shards, mesh=mesh, in_specs=in_specs, out_specs=out_specs, check_vma=False)
```

```python
import math

import jax
import jax.numpy as jnp
from jax import lax
from jax.experimental import pallas as pl
from jax.experimental.pallas import tpu as pltpu
from jax.sharding import Mesh
from jax.sharding import PartitionSpec as P

HEAD = 64
ROT = 16
NORM_EPS = 1e-05
BF = jnp.bfloat16
F32 = jnp.float32
AXES = ("core", "x", "z_hi", "y", "z_lo")
SHARDS = ("y", "z_lo")
LENGTH = 1024
WIDTH = 1024
QROWS = 256
UNIT = 64


def place_of(index):
    return index // 64, (index // 16) % 4, (index // 8) % 2, (index // 2) % 4, index % 2


def index_of(core, x, zh, y, zl):
    return core * 64 + x * 16 + zh * 8 + 2 * y + zl


def route(block, target):
    targets = [target(*place_of(i)) for i in range(128)]
    pairs = [(i, index_of(*place)) for i, place in enumerate(targets) if place is not None]
    return lax.ppermute(block, AXES, pairs)


def from_all(block, axes):
    count = math.prod(lax.axis_size(axis) for axis in axes)
    return swapped(jnp.broadcast_to(block[None], (count, *block.shape)), axes)


def swapped(blocks, axes):
    return lax.all_to_all(blocks, axes, split_axis=0, concat_axis=0, tiled=True)


def along_x(block, step):
    return route(block, lambda c, x, zh, y, zl: (c, (x + step) % 4, zh, y, zl))


def along_y(block, step):
    return route(block, lambda c, x, zh, y, zl: (c, x, zh, (y + step) % 4, zl))


def across_low(block):
    return route(block, lambda c, x, zh, y, zl: (c, x, zh, y, 1 - zl))


def across_cores(block):
    return route(block, lambda c, x, zh, y, zl: (1 - c, x, zh, y, zl))


def across_high(block):
    return route(block, lambda c, x, zh, y, zl: (c, x, 1 - zh, y, zl))


def transposed(block):
    return route(block, lambda c, x, zh, y, zl: (zl, y, zh, x, c))


def pick(array, index, axis=0):
    return lax.dynamic_index_in_dim(array, index, axis, keepdims=False)


def dot(left, right):
    return jnp.dot(left, right, preferred_element_type=F32)


def dot_left(left, right):
    return lax.dot_general(left, right, (((0,), (0,)), ((), ())), preferred_element_type=F32)


def dot_right(left, right):
    return lax.dot_general(left, right, (((1,), (1,)), ((), ())), preferred_element_type=F32)


def head_lanes(rows, head):
    lanes = lax.broadcasted_iota(jnp.int32, (rows, 2 * HEAD), 1)
    return (lanes >= head * HEAD) & (lanes < (head + 1) * HEAD)


def turned(values, cosine, sine_low, sine_high):
    return (
        values * cosine
        + pltpu.roll(values, ROT // 2, 1) * sine_low
        + pltpu.roll(values, 2 * HEAD - ROT // 2, 1) * sine_high
    )


def masked_scores(query, keys, begin, block, reach):
    scores = dot_right(query, keys)
    rows = block * QROWS + lax.broadcasted_iota(jnp.int32, (QROWS, reach), 0)
    columns = lax.broadcasted_iota(jnp.int32, (QROWS, reach), 1)
    seen = (columns <= rows) & (columns >= begin)
    return jnp.where(seen, scores, -1e30)


def unit_rows(where_ref, m):
    return pl.ds(pl.multiple_of(where_ref[WHERE + m] * UNIT, UNIT), UNIT)


def attend(where_ref, proj_ref, tables, mixed_ref, q_ref, k_ref, v_ref, o_ref, lse_ref):
    cos_ref, low_ref, high_ref, begin_ref = tables
    for m in range(LENGTH // UNIT):
        here = pl.ds(m * UNIT, UNIT)
        proj = proj_ref[unit_rows(where_ref, m), :]
        cosine, low, high = cos_ref[here, :], low_ref[here, :], high_ref[here, :]
        query = turned(proj[:, :128].astype(F32), cosine, low, high)
        q_ref[here, :] = (query.astype(BF).astype(F32) * (1.0 / math.sqrt(HEAD))).astype(BF)
        k_ref[here, :] = turned(proj[:, 128:256].astype(F32), cosine, low, high).astype(BF)
        v_ref[here, :] = proj[:, 256:]
    for block in range(LENGTH // QROWS):
        rows = pl.ds(block * QROWS, QROWS)
        reach = (block + 1) * QROWS
        keys, values = k_ref[:reach, :], v_ref[:reach, :]
        query = q_ref[rows, :]
        begin = begin_ref[rows, :1]
        outs, logs = [], []
        for head in range(2):
            own = head_lanes(QROWS, head)
            scores = masked_scores(jnp.where(own, query, jnp.zeros_like(query)), keys, begin, block, reach)
            highest = jnp.max(scores, axis=-1, keepdims=True)
            exponent = jnp.exp(scores - highest)
            total = jnp.sum(exponent, axis=-1, keepdims=True)
            probs = (exponent * (1.0 / total)).astype(BF)
            outs.append(dot(probs, values))
            logs.append(highest + jnp.log(total))
        first = head_lanes(QROWS, 0)
        o_ref[rows, :] = jnp.where(first, outs[0], outs[1]).astype(BF)
        lse_ref[rows, :] = jnp.where(first, logs[0], logs[1])
    for m in range(LENGTH // UNIT):
        mixed_ref[unit_rows(where_ref, m), :] = o_ref[pl.ds(m * UNIT, UNIT), :]


def attend_back(where_ref, tables, kept, do_ref, out_ref, dq_ref, dk_ref, dv_ref):
    cos_ref, low_ref, high_ref, begin_ref = tables
    q_ref, k_ref, v_ref, o_ref, lse_ref = kept
    for block in reversed(range(LENGTH // QROWS)):
        rows = pl.ds(block * QROWS, QROWS)
        reach = (block + 1) * QROWS
        keys, values = k_ref[:reach, :], v_ref[:reach, :]
        query, upstream, mixed = q_ref[rows, :], do_ref[rows, :], o_ref[rows, :].astype(F32)
        begin = begin_ref[rows, :1]
        grads = []
        for head in range(2):
            own = head_lanes(QROWS, head)
            query_own = jnp.where(own, query, jnp.zeros_like(query))
            up_own = jnp.where(own, upstream, jnp.zeros_like(upstream))
            scores = masked_scores(query_own, keys, begin, block, reach)
            probs = jnp.exp(scores - lse_ref[rows, head * HEAD : head * HEAD + 1])
            centre = jnp.sum(up_own.astype(F32) * mixed, axis=-1, keepdims=True)
            moved = (probs * (dot_right(up_own, values) - centre)).astype(BF)
            grads.append(dot(moved, keys))
            dk = dot_left(moved, query_own)
            dv = dot_left(probs.astype(BF), up_own)
            if block == LENGTH // QROWS - 1 and head == 0:
                dk_ref[...] = dk
                dv_ref[...] = dv
            else:
                dk_ref[:reach, :] += dk
                dv_ref[:reach, :] += dv
        first = head_lanes(QROWS, 0)
        dq_ref[rows, :] = jnp.where(first, grads[0], grads[1]) * (1.0 / math.sqrt(HEAD))
    for m in range(LENGTH // UNIT):
        here = pl.ds(m * UNIT, UNIT)
        there = unit_rows(where_ref, m)
        cosine, low, high = cos_ref[here, :], -low_ref[here, :], -high_ref[here, :]
        out_ref[there, :128] = turned(dq_ref[here, :], cosine, low, high).astype(BF)
        out_ref[there, 128:256] = turned(dk_ref[here, :], cosine, low, high).astype(BF)
        out_ref[there, 256:384] = dv_ref[here, :].astype(BF)


def barrier(*values):
    flat, tree = jax.tree.flatten(values)
    anywhere = pl.BlockSpec(memory_space=pl.ANY)
    flat = pl.pallas_call(
        lambda *refs: None,
        out_shape=[jax.ShapeDtypeStruct(value.shape, value.dtype) for value in flat],
        in_specs=[anywhere] * len(flat),
        out_specs=[anywhere] * len(flat),
        input_output_aliases={k: k for k in range(len(flat))},
    )(*flat)
    return jax.tree.unflatten(tree, flat)


def after(values, *others):
    flat, tree = jax.tree.flatten(values)
    others = jax.tree.leaves(others)
    anywhere = pl.BlockSpec(memory_space=pl.ANY)
    flat = pl.pallas_call(
        lambda *refs: None,
        out_shape=[jax.ShapeDtypeStruct(value.shape, value.dtype) for value in flat],
        in_specs=[anywhere] * (len(flat) + len(others)),
        out_specs=[anywhere] * len(flat),
        input_output_aliases={k: k for k in range(len(flat))},
    )(*flat, *others)
    return jax.tree.unflatten(tree, flat)


def run(body, scalars, arrays, outs, scratch=(), flops=0, spaces=None, others=()):
    vmem, anywhere = pl.BlockSpec(memory_space=pltpu.VMEM), pl.BlockSpec(memory_space=pl.ANY)
    others = jax.tree.leaves(others)
    count = 1 + len(arrays)
    return pl.pallas_call(
        lambda *refs: body(*refs[:count], *refs[count + len(others) :]),
        out_shape=[jax.ShapeDtypeStruct(*out) for out in outs],
        in_specs=[pl.BlockSpec(memory_space=pltpu.SMEM)]
        + (spaces or [vmem] * len(arrays))
        + [anywhere] * len(others),
        out_specs=[vmem] * len(outs),
        scratch_shapes=list(scratch),
        compiler_params=pltpu.CompilerParams(vmem_limit_bytes=60 * 1024 * 1024),
        cost_estimate=pl.CostEstimate(flops=flops, bytes_accessed=4_000_000, transcendentals=0),
    )(scalars, *arrays, *others)


X, CORE, ZH, Y, ZL, PART, SHARD, BIAS, WHERE = 0, 1, 2, 3, 4, 5, 6, 7, 10


def lanes(start, extent=128):
    return pl.ds(pl.multiple_of(start, extent), extent)


def low_half(rows):
    return lax.broadcasted_iota(jnp.int32, (rows, 128), 1) < 64


def half_tiles(first, second):
    low = low_half(first.shape[0])
    return (
        jnp.where(low, first, pltpu.roll(second, 64, 1)),
        jnp.where(low, pltpu.roll(first, 64, 1), second),
    )


def block_rows(number, extent):
    return pl.ds(pl.multiple_of(extent * number, extent), extent)


def column(row):
    return jnp.transpose(jnp.broadcast_to(row, (128, 128)))


def slice_kernel(
    at, qkv_all, up_all, down_all, dense_all, bias_qkv_all, bias_up_all, bias_dense, bias_down, gain_one, shift_one,
    gain_two, shift_two,
    qkv_self, qkv_other, rest_self, rest_other,
    qkv, up, down, dense, bias_qkv, small, rows, sems,
):
    x, core = at[X], at[CORE]
    copies = [(up_all.at[:, lanes(512 * k + 128 * x)], up.at[k]) for k in range(8)]
    copies += [(qkv_all.at[:, lanes(1024 * k + 256 * x, 256)], qkv.at[k]) for k in range(3)]
    copies.append((down_all.at[pl.ds(pl.multiple_of(128 * x, 128), 128), :], down))
    copies.append((dense_all.at[:, lanes(256 * x, 256)], dense))
    copies.append((bias_qkv_all, bias_qkv))
    copies.append((bias_up_all.at[:, lanes(128 * x)], small.at[0]))
    for k, vector in enumerate((bias_dense, bias_down, gain_one, shift_one, gain_two, shift_two)):
        copies.append((vector, small.at[1 + k]))
    copies = [pltpu.make_async_copy(*pair, sems.at[k]) for k, pair in enumerate(copies)]
    for copy in copies:
        copy.start()
    for copy in copies:
        copy.wait()
    for k in range(4):
        zero, one = half_tiles(up[2 * k].astype(F32), up[2 * k + 1].astype(F32))
        here = slice(128 * k, 128 * k + 128)
        rest_self[:, here] = jnp.where(core == 0, zero, one).astype(BF)
        rest_other[:, here] = jnp.where(core == 0, one, zero).astype(BF)
    for k in range(3):
        first, second = qkv[k, :, :128], qkv[k, :, 128:]
        here = slice(128 * k, 128 * k + 128)
        qkv_self[:128, here] = jnp.where(core == 0, first, second)
        qkv_other[:128, here] = jnp.where(core == 0, second, first)
    for k in range(2):
        first, second = down[:64, 512 * k : 512 * k + 512], down[64:, 512 * k : 512 * k + 512]
        rest_self[64 * k : 64 * k + 64, 512:] = jnp.where(core == 0, first, second)
        rest_other[64 * k : 64 * k + 64, 512:] = jnp.where(core == 0, second, first)
    first, second = dense[:, :128], dense[:, 128:]
    qkv_self[:128, 384:] = jnp.where(core == 0, first, second)
    qkv_other[:128, 384:] = jnp.where(core == 0, second, first)
    rows[...] = jnp.zeros_like(rows)
    for k in range(3):
        rows[k : k + 1, :] = bias_qkv[:, 128 * k : 128 * k + 128].astype(F32)
    for k in range(7):
        rows[3 + k : 4 + k, :] = small[k].astype(F32)
    plain = rows[...]
    number = lax.broadcasted_iota(jnp.int32, (16, 128), 0)
    moved = jnp.where(number == 3, pltpu.roll(plain, 64, 1), plain)
    for out, upper in ((qkv_self, core), (qkv_other, 1 - core)):
        out[128:, :128] = jnp.where(upper == 0, plain, moved).astype(BF)
        out[128:, 128:] = jnp.zeros((16, 384), BF)


def tables_kernel(at, places, frequency, cos_ref, low_ref, high_ref, begin_ref):
    place = jnp.transpose(jnp.broadcast_to(places[...].astype(F32), (128, LENGTH)))
    lane = lax.broadcasted_iota(jnp.int32, (LENGTH, 128), 1) % HEAD
    angles = place * frequency[...]
    sine = jnp.sin(angles)
    cos_ref[...] = jnp.where(lane < ROT, jnp.cos(angles), 1.0)
    low_ref[...] = jnp.where((lane >= ROT // 2) & (lane < ROT), sine, 0.0)
    high_ref[...] = jnp.where(lane < ROT // 2, -sine, 0.0)
    row = lax.broadcasted_iota(jnp.int32, (LENGTH, 128), 0)
    begin_ref[...] = row - place.astype(jnp.int32)


def prepare_qkv(at, blocks, wide, wide_turned, bias, bias_out, rows):
    bias[...] = jnp.zeros_like(bias)
    for shard, message in blocks:
        vectors = message[128:, :128].astype(F32)
        rows[16 * shard : 16 * shard + 16, :] = vectors
        here = slice(128 * shard, 128 * shard + 128)
        scale = column(vectors[6:7, :])
        for k in range(0, 384, 128):
            wide[here, k : k + 128] = (message[:128, k : k + 128].astype(F32) * scale).astype(BF)
        shift = jnp.broadcast_to(vectors[7:8, :], (8, 128)).astype(BF)
        bias[:, :384] += dot(shift, message[:128, :384])
    for k in range(3):
        bias[:, 128 * k : 128 * k + 128] += jnp.broadcast_to(rows[pl.ds(at[BIAS + k], 1), :], (8, 128))
    for shard in range(8):
        total = rows[16 * shard + 4 : 16 * shard + 5, :] + rows[16 * shard + 5 : 16 * shard + 6, :]
        bias_out[:, 128 * shard : 128 * shard + 128] = jnp.broadcast_to(total, (8, 128))
    wide_turned[...] = jnp.transpose(wide[...])


def prepare_up(at, blocks, rows, up, up_turned, bias):
    bias[...] = jnp.zeros_like(bias)
    for shard, message in blocks:
        vectors = rows[16 * shard : 16 * shard + 16, :]
        here = slice(128 * shard, 128 * shard + 128)
        scale = column(vectors[8:9, :])
        for k in range(0, 512, 128):
            up[here, k : k + 128] = (message[:128, k : k + 128].astype(F32) * scale).astype(BF)
        shift = jnp.broadcast_to(vectors[9:10, :], (8, 128)).astype(BF)
        bias[...] += dot(shift, message[:128, :512])
    for k in range(4):
        first = jnp.broadcast_to(rows[32 * k + 3 : 32 * k + 4, :], (8, 128))
        second = jnp.broadcast_to(rows[32 * k + 19 : 32 * k + 20, :], (8, 128))
        bias[:, 128 * k : 128 * k + 128] += half_tiles(first, second)[0]
    up_turned[...] = jnp.transpose(up[...])


def prepare_down(blocks, down, down_turned):
    for k, halves in enumerate(blocks):
        down[64 * k : 64 * k + 64, :512] = halves[:64, :]
        down[64 * k : 64 * k + 64, 512:] = halves[64:128, :]
    down_turned[...] = jnp.transpose(down[...])


def project_rows(blocks, qkv, bias, unit, proj):
    for k in range(8):
        values = blocks[k][...].astype(F32)
        centred = values - jnp.mean(values, axis=-1, keepdims=True)
        spread = jnp.mean(centred * centred, axis=-1, keepdims=True)
        unit[128 * k : 128 * k + 128, :] = (centred * lax.rsqrt(spread + NORM_EPS)).astype(BF)
    for k in range(4):
        here = slice(256 * k, 256 * k + 256)
        proj[here, :] = (dot(unit[here, :], qkv[...]) + bias[:1, :]).astype(BF)


def activate(unit, up, bias, active, slope):
    for k in range(4):
        here = slice(256 * k, 256 * k + 256)
        middle = dot(unit[here, :], up[...]) + bias[:1, :]
        share = 0.5 * (1.0 + lax.erf(middle * (1.0 / math.sqrt(2.0))))
        density = jnp.exp(-0.5 * middle * middle) * (1.0 / math.sqrt(2.0 * math.pi))
        active[here, :] = (middle * share).astype(BF)
        slope[here, :] = (share + middle * density).astype(BF)


def attend_first_kernel(at, *refs):
    blocks, messages, tables, outs = refs[:8], refs[8], refs[9:13], refs[13:]
    qkv_turned, bias_out, vectors, unit, mixed, *kept = outs[:10]
    qkv, bias, proj = outs[10:]
    prepare_qkv(at, [(k, messages.at[k]) for k in range(8)], qkv, qkv_turned, bias, bias_out, vectors)
    project_rows(blocks, qkv, bias, unit, proj)
    attend(at, proj, tables, mixed, *kept)


def attend_second_kernel(at, *refs):
    blocks, messages, tables, outs = refs[:8], refs[8], refs[9:13], refs[13:]
    qkv_turned, bias_out, up_turned, active, slope, unit, mixed, *kept = outs[:12]
    qkv, bias, proj, vectors, up, up_bias = outs[12:]
    prepare_qkv(at, [(k, messages.at[k]) for k in range(8)], qkv, qkv_turned, bias, bias_out, vectors)
    prepare_up(at, [(k, messages.at[k, :, 384:]) for k in range(8)], vectors, up, up_turned, up_bias)
    project_rows(blocks, qkv, bias, unit, proj)
    activate(unit, up, up_bias, active, slope)
    attend(at, proj, tables, mixed, *kept)


def dense_parts_of(at, parts, layer):
    for r in range(4):
        for beside in range(2):
            part = 2 * ((at[X] + 4 - r) % 4) + (at[CORE] + beside) % 2
            yield part, parts[beside, r, :, 128 * layer : 128 * layer + 128]


def project(at, layer, active, mixed, down, dense_parts, dense, blocks):
    for part, columns in dense_parts_of(at, dense_parts, layer):
        dense[:, lanes(128 * part)] = columns
    for k in (2, 1, 3, 0):
        here = slice(256 * k, 256 * k + 256)
        out = dot(active[here, :], down[...]) + dot(mixed[here, :], dense[...])
        blocks[2 * k][...] = out[:128].astype(BF)
        blocks[2 * k + 1][...] = out[128:].astype(BF)


def rest_first_kernel(at, messages, vectors, unit, mixed, dense_parts, up_turned, down_turned, active, slope, *refs):
    blocks, (up, bias, down, dense) = refs[:8], refs[8:]
    prepare_up(at, [(k, messages.at[k]) for k in range(8)], vectors, up, up_turned, bias)
    prepare_down([messages.at[k, :, 512:] for k in range(8)], down, down_turned)
    activate(unit, up, bias, active, slope)
    project(at, 0, active, mixed, down, dense_parts, dense, blocks)


def project_kernel(at, active, mixed, down, dense_parts, *refs):
    project(at, 1, active, mixed, down, dense_parts, refs[8], refs[:8])


def pull_back(at, layer, blocks, down_turned, dense_parts, slope, grad_middle, grad_mixed, dense_turned):
    for part, columns in dense_parts_of(at, dense_parts, layer):
        dense_turned[block_rows(part, 128), :] = jnp.transpose(columns)
    for k in range(8):
        here = slice(128 * k, 128 * k + 128)
        rows = blocks[k][...]
        grad_middle[here, :] = (dot(rows, down_turned[...]) * slope[here, :].astype(F32)).astype(BF)
        grad_mixed[here, :] = dot(rows, dense_turned[...]).astype(BF)


def back_second_kernel(at, *refs):
    rows, (messages, dense_parts, slope), qkv_turned, up_turned = refs[:8], refs[8:11], refs[11], refs[12]
    tables, kept, blocks = refs[13:17], refs[17:22], refs[22:30]
    grad_proj, grad_middle, down, down_turned, dense_turned, grad_mixed, *scratch = refs[30:]
    prepare_down([messages.at[k] for k in range(8)], down, down_turned)
    pull_back(at, 1, rows, down_turned, dense_parts, slope, grad_middle, grad_mixed, dense_turned)
    back_attend_kernel(
        at, grad_mixed, grad_middle, qkv_turned, up_turned, *tables, *kept, *blocks, grad_proj, *scratch
    )


def back_attend_kernel(where_ref, grad_mixed, grad_middle, wide_turned, up_turned, cosine, low, high, begin, *refs):
    kept, blocks, grad_proj, (do_ref, dq_ref, dk_ref, dv_ref) = refs[:5], refs[5:13], refs[13], refs[14:]
    for m in range(LENGTH // UNIT):
        do_ref[pl.ds(m * UNIT, UNIT), :] = grad_mixed[unit_rows(where_ref, m), :]
    attend_back(where_ref, (cosine, low, high, begin), kept, do_ref, grad_proj, dq_ref, dk_ref, dv_ref)
    for k in (2, 1, 3, 0):
        here = slice(256 * k, 256 * k + 256)
        out = dot(grad_proj[here, :], wide_turned[...]) + dot(grad_middle[here, :], up_turned[...])
        blocks[2 * k][...] = out[:128].astype(BF)
        blocks[2 * k + 1][...] = out[128:].astype(BF)


def weight_terms(at, unit, grads, outward=None, pulled=None, others=()):
    extent = 512 if pulled else sum(grad.shape[1] for grad in grads)
    start = 640 if outward else 0
    arrays, scratch, outs = (unit, *grads), [], [((8, 144, start + extent), BF)]
    if outward:
        active, mixed, rows, *grad_middle = outward
        arrays = (*arrays, active, mixed, *rows, *grad_middle)
        scratch = [pltpu.VMEM((512, 1024), F32), pltpu.VMEM((128, 1024), F32)]
    if pulled:
        arrays = (*arrays, *pulled)
        outs += [((1024, 512), BF), ((1024, 128), BF)]
        scratch.append(pltpu.VMEM((1024, 128), BF))

    def body(at, unit, *refs):
        grad_refs, refs = refs[: len(grads)], refs[len(grads) :]
        if pulled:
            (active, mixed), rows, refs = refs[:2], refs[2:10], refs[10:]
            (down_turned, dense_parts, slope), (out, grad_middle, grad_mixed) = refs[:3], refs[3:6]
            down, dense, dense_turned = refs[6:]
            pull_back(at, 0, rows, down_turned, dense_parts, slope, grad_middle, grad_mixed, dense_turned)
            grad_refs = (grad_middle,)
        elif outward:
            (active, mixed), rows, grad_middle, out, (down, dense) = refs[:2], refs[2:10], refs[10], refs[11], refs[12:]
        else:
            out = refs[0]
        if outward:
            sums = jnp.zeros((1, 128), F32)
            for k in range(8):
                here = slice(128 * k, 128 * k + 128)
                block = rows[k][...]
                more_down = dot_left(active[here, :], block)
                more_dense = dot_left(mixed[here, :], block)
                if k == 0:
                    down[...] = more_down
                    dense[...] = more_dense
                else:
                    down[...] += more_down
                    dense[...] += more_dense
                sums = sums + jnp.sum(rows[k][:, lanes(128 * at[PART])].astype(F32), axis=0, keepdims=True)
            sums_up = jnp.sum(grad_middle[...].astype(F32), axis=0, keepdims=True)
            for shard in range(8):
                for half in range(2):
                    piece = down[64 * shard : 64 * shard + 64, 512 * half : 512 * half + 512]
                    out[shard, 64 * half : 64 * half + 64, :512] = piece.astype(BF)
                out[shard, :128, 512:640] = dense[:, 128 * shard : 128 * shard + 128].astype(BF)
                out[shard, 128:, :128] = jnp.broadcast_to(sums, (16, 128)).astype(BF)
                out[shard, 128:, 128:640] = jnp.broadcast_to(sums_up, (16, 512)).astype(BF)
        at_column = start
        for grad in grad_refs:
            columns = grad.shape[1]
            here = slice(at_column, at_column + columns)
            sums = jnp.sum(grad[...].astype(F32), axis=0, keepdims=True)
            for shard in range(8):
                terms = dot_left(unit[:, 128 * shard : 128 * shard + 128], grad[...])
                out[shard, :128, here] = terms.astype(BF)
                out[shard, 128:, here] = jnp.broadcast_to(sums, (16, columns)).astype(BF)
            at_column += columns

    outs = run(body, at, arrays, outs, scratch, flops=2 * 1024 * 1024 * (extent + start), others=others)
    return outs if pulled else outs[0]


def final_kernel(at, *refs):
    sources = refs[:8], refs[8:16]
    qkv, up, gain_one, shift_one, gain_two, shift_two = refs[16:22]
    grad_qkv, grad_up, grad_down, grad_dense = refs[22:26]
    bias_qk, bias_v, bias_up, bias_out, gain_a, shift_a, gain_b, shift_b = refs[26:34]
    sums, sums_qkv, sums_up, sums_out, sems = refs[34:]
    x, core, shard = at[X], at[CORE], at[SHARD]
    for layer in range(2):

        @pl.when(core == layer)
        def _():
            copies = []
            for k in range(8):
                target = sums.at[k // 4, (x + k % 4) % 4]
                copies.append(pltpu.make_async_copy(sources[layer][k], target, sems.at[k]))
            for copy in copies:
                copy.start()
            for copy in copies:
                copy.wait()

    def whole(beside, r, columns):
        return sums[beside, r, :128, columns].astype(F32)

    def below(beside, r, columns):
        return sums[beside, r, 128:, columns].astype(F32)

    gain_col, shift_col = column(gain_one[...].astype(F32)), column(shift_one[...].astype(F32))
    gain_col_two, shift_col_two = column(gain_two[...].astype(F32)), column(shift_two[...].astype(F32))
    totals = [jnp.zeros((128, 128), F32) for _ in range(4)]
    for r in range(4):
        column_no = r
        for half in range(2):
            beside = (core + half) % 2
            part = 2 * column_no + half
            for k in range(3):
                cols = slice(1152 + 128 * k, 1280 + 128 * k)
                raw = whole(beside, r, cols)
                total = below(beside, r, cols)[:1]
                place = lanes(1024 * k + 128 * part)
                weight = qkv[:, place].astype(F32)
                grad_qkv[:, place] = gain_col * raw + shift_col * total
                sums_qkv[pl.ds(8 * k + part, 1), :] = total
                totals[0] += weight * raw
                totals[1] += weight * total
            grad_down[pl.ds(pl.multiple_of(64 * part, 64), 64), :512] = sums[beside, r, :64, :512].astype(F32)
            grad_down[pl.ds(pl.multiple_of(64 * part, 64), 64), 512:] = sums[beside, r, 64:128, :512].astype(F32)
            grad_dense[:, lanes(128 * part)] = whole(beside, r, slice(512, 640))
            sums_out[pl.ds(part, 1), :] = below(beside, r, slice(0, 128))[:1]
        zero, one = core % 2, (core + 1) % 2
        for k in range(4):
            cols = slice(640 + 128 * k, 768 + 128 * k)
            beneath = slice(128 + 128 * k, 256 + 128 * k)
            raws = half_tiles(whole(zero, r, cols), whole(one, r, cols))
            adds = half_tiles(below(zero, r, beneath), below(one, r, beneath))
            for odd in range(2):
                raw, total = raws[odd], adds[odd][:1]
                place = lanes(1024 * k + 512 * odd + 128 * column_no)
                weight = up[:, place].astype(F32)
                grad_up[:, place] = gain_col_two * raw + shift_col_two * total
                sums_up[pl.ds(8 * k + 4 * odd + column_no, 1), :] = total
                totals[2] += weight * raw
                totals[3] += weight * total
    for out, total in zip((gain_a, shift_a, gain_b, shift_b), totals):
        out[...] = jnp.sum(jnp.transpose(total), axis=0, keepdims=True)
    for k in range(2):
        bias_qk[:, 128 * k : 128 * k + 128] = sums_qkv[pl.ds(2 * shard + k, 1), :]
    bias_v[...] = sums_qkv[pl.ds(16 + shard, 1), :]
    for k in range(4):
        bias_up[:, 128 * k : 128 * k + 128] = sums_up[pl.ds(4 * shard + k, 1), :]
    bias_out[...] = sums_out[pl.ds(shard, 1), :]


def added(*blocks):
    total = blocks[0].astype(F32)
    for block in blocks[1:]:
        total = total + block.astype(F32)
    return total


def gather_rows(mine):
    own = [mine] + [along_x(mine, -r) for r in (1, 2, 3)]
    other = [across_cores(block) for block in own]
    return [rows for pair in zip(own, other) for rows in pair]


def joined_cores(blocks):
    joined = {r: added(blocks[2 * r], across_cores(blocks[2 * r + 1])) for r in (2, 1, 3, 0)}
    return [joined[0]] + [joined[r].astype(BF) for r in (1, 2, 3)]


def joined_chips(joined):
    return added(joined[0], *(along_x(joined[r], r) for r in (1, 2, 3)))


def summed(blocks):
    return jnp.sum(blocks.astype(F32), axis=0)


def normalized(rows):
    values = rows.astype(F32)
    centre = jnp.mean(values, axis=-1, keepdims=True)
    centred = values - centre
    spread = jnp.mean(centred * centred, axis=-1, keepdims=True)
    scale = lax.rsqrt(spread + NORM_EPS)
    return centred * scale, scale


def norm_back(grad, rows):
    unit, scale = normalized(rows)
    mean_grad = jnp.mean(grad, axis=-1, keepdims=True)
    mean_both = jnp.mean(grad * unit, axis=-1, keepdims=True)
    return scale * (grad - mean_grad - unit * mean_both)


def shards(
    tokens, positions, w_qkv, b_qkv, w_dense, b_dense, w_up, b_up, w_down, b_down,
    norm1_gain, norm1_shift, norm2_gain, norm2_shift, cotangent,
):
    core, x, zh, y, zl = (lax.axis_index(axis) for axis in AXES)
    shard = 2 * y + zl
    part = 2 * x + core
    first_core = core == 0
    anywhere, vmem = pl.BlockSpec(memory_space=pl.ANY), pl.BlockSpec(memory_space=pltpu.VMEM)

    bias_rows = [16 * ((8 * k + part) // 3) + (8 * k + part) % 3 for k in range(3)]
    at = jnp.stack([x, core, zh, y, zl, part, shard] + bias_rows).astype(jnp.int32)
    unit_no = jnp.arange(16, dtype=jnp.int32)
    where = (
        ((unit_no // 4 - x) % 4) * 4
        + jnp.bitwise_xor(unit_no % 2, core) * 2
        + jnp.bitwise_xor((unit_no // 2) % 2, zh)
    ).astype(jnp.int32)
    at = jnp.concatenate([at, where])

    own, lent = [], []
    for array in (tokens, cotangent):
        own.append(lax.dynamic_slice_in_dim(pick(array, zh), core * UNIT, UNIT, 0))
        lent.append(lax.dynamic_slice_in_dim(pick(array, 1 - zh), core * UNIT, UNIT, 0))
    lent = across_high(jnp.stack(lent))
    own_tokens = jnp.concatenate([own[0], lent[0]], axis=0)
    own_cotangent = jnp.concatenate([own[1], lent[1]], axis=0)

    sliced = run(
        slice_kernel,
        at,
        (
            w_qkv[0], w_up[0], w_down[0], w_dense[0], b_qkv, b_up, b_dense, b_down,
            norm1_gain, norm1_shift, norm2_gain, norm2_shift,
        ),
        [((144, 512), BF)] * 2 + [((128, 1024), BF)] * 2,
        [
            pltpu.VMEM((3, 128, 256), BF),
            pltpu.VMEM((8, 128, 128), BF),
            pltpu.VMEM((128, 1024), BF),
            pltpu.VMEM((128, 256), BF),
            pltpu.VMEM((1, 384), BF),
            pltpu.VMEM((7, 1, 128), BF),
            pltpu.VMEM((16, 128), F32),
            pltpu.SemaphoreType.DMA((21,)),
        ],
        spaces=[pl.BlockSpec(memory_space=pltpu.HBM)] * 12,
    )
    qkv_theirs, rest_theirs = across_cores(sliced[1]), across_cores(sliced[3])
    qkv, qkv_two = jnp.where(first_core, sliced[0], qkv_theirs), jnp.where(first_core, qkv_theirs, sliced[0])
    qkv = jnp.concatenate([qkv, qkv_two[:, 384:]], axis=1)
    rest = jnp.where(first_core, sliced[2], rest_theirs)
    rest_two = jnp.where(first_core, rest_theirs, sliced[2])
    wide_two = jnp.concatenate([qkv_two[:, :384], jnp.pad(rest_two[:, :512], ((0, 16), (0, 0)))], axis=1)
    down_two = rest_two[:, 512:]

    half = ROT // 2
    frequency = 1.0 / 10000.0 ** (jnp.arange(half).astype(F32) * 2.0 / ROT)
    frequency = jnp.concatenate([jnp.tile(frequency, HEAD // half)] * 2)[None, :]
    tables = run(
        tables_kernel,
        at,
        (lax.dynamic_slice_in_dim(positions, zh, 1, 0), frequency),
        [((LENGTH, 128), F32)] * 3 + [((LENGTH, 128), jnp.int32)],
    )

    big, head = ((1024, 1024), BF), ((1024, 128), BF)
    kept_outs = [head] * 4 + [((1024, 128), F32)]
    qkv_scratch = [pltpu.VMEM((1024, 384), BF), pltpu.VMEM((8, 384), F32), pltpu.VMEM((1024, 384), BF)]
    grad_scratch = [pltpu.VMEM((1024, 128), BF)] + [pltpu.VMEM((1024, 128), F32)] * 3
    hidden_outs = [((1024, 512), BF)] * 2
    block_outs = [((128, 1024), BF)] * 8
    qkv_outs = [((384, 1024), BF), ((8, 1024), F32)]

    def back_attend(grad_mixed, grad_middle, qkv_turned, up_turned, kept):
        outs = run(
            back_attend_kernel,
            at,
            (grad_mixed, grad_middle, qkv_turned, up_turned, *tables, *kept),
            [((128, 1024), BF)] * 8 + [((1024, 384), BF)],
            grad_scratch,
            flops=6_000_000_000,
        )
        return outs[:8], outs[8]

    qkvs = from_all(after(qkv, own_tokens), SHARDS)
    rows_one = gather_rows(own_tokens)
    rests = from_all(after(rest, qkvs, rows_one[2::2]), SHARDS)
    held = [lax.dynamic_slice(qkvs, (2 * ((x + r) % 4), 0, 384), (2, 128, 256)) for r in range(4)]
    held = [held[0]] + [along_x(held[r], r) for r in (1, 2, 3)]
    dense = jnp.stack([pick(block, core) for block in held])
    dense = jnp.stack([dense, across_cores(jnp.stack([pick(block, 1 - core) for block in held]))])
    qkv_turned_one, bias_out_one, vectors, unit_one, mixed_one, *kept_one = run(
        attend_first_kernel,
        at,
        (*rows_one, qkvs, *tables),
        qkv_outs + [((128, 128), F32), big, head] + kept_outs,
        qkv_scratch,
        flops=5_000_000_000,
    )
    rests, wide_two, dense = after((rests, wide_two, dense), mixed_one)

    wides = from_all(after(wide_two, rests), SHARDS)
    up_turned_one, down_turned_one, active_one, slope_one, *blocks = run(
        rest_first_kernel,
        at,
        (rests, vectors, unit_one, mixed_one, dense),
        [((512, 1024), BF), ((1024, 512), BF)] + hidden_outs + block_outs,
        [
            pltpu.VMEM((1024, 512), BF),
            pltpu.VMEM((8, 512), F32),
            pltpu.VMEM((512, 1024), BF),
            pltpu.VMEM((128, 1024), BF),
        ],
        flops=3_000_000_000,
    )
    joined = joined_cores(blocks)
    hidden_one = own_tokens.astype(F32) + joined_chips(joined) + bias_out_one[:1, :]
    hidden_one = hidden_one.astype(BF)
    rows_two = gather_rows(hidden_one)
    downs = from_all(after(down_two, wides), SHARDS)
    own_cotangent = after(own_cotangent, rows_two[2::2])

    grad_own = [own_cotangent] + [along_x(own_cotangent, -r) for r in (1, 2, 3)]
    qkv_turned_two, bias_out_two, up_turned_two, active_two, slope_two, unit_two, mixed_two, *kept_two = run(
        attend_second_kernel,
        at,
        (*rows_two, wides, *tables),
        qkv_outs + [((512, 1024), BF)] + hidden_outs + [big, head] + kept_outs,
        qkv_scratch
        + [pltpu.VMEM((128, 128), F32), pltpu.VMEM((1024, 512), BF), pltpu.VMEM((8, 512), F32)],
        flops=8_000_000_000,
    )
    grad_own = after(grad_own, mixed_two)
    grad_rows = [rows for block in grad_own for rows in (block, across_cores(block))]

    *blocks, grad_proj, grad_middle, down_two = run(
        back_second_kernel,
        at,
        (*grad_rows, downs, dense, slope_two, qkv_turned_two, up_turned_two, *tables, *kept_two),
        block_outs + [((1024, 384), BF), ((1024, 512), BF), ((512, 1024), BF)],
        [pltpu.VMEM((1024, 512), BF), pltpu.VMEM((1024, 128), BF), pltpu.VMEM((1024, 128), BF)] + grad_scratch,
        flops=8_000_000_000,
    )
    joined = joined_cores(blocks)
    out_sums = weight_terms(
        at, unit_two, (), (active_two, mixed_two, grad_rows, grad_middle), others=joined
    )
    joined[0] = after(joined[0], out_sums)
    out_sums = swapped(out_sums, SHARDS)
    grad_two = grad_rows[0].astype(F32) + norm_back(joined_chips(joined), hidden_one)
    grad_mid = grad_two.astype(BF)
    wide_sums = weight_terms(at, unit_two, (grad_middle, grad_proj), others=[grad_mid])
    grad_rows = gather_rows(grad_mid)
    grad_rows, out_sums, wide_sums = barrier(grad_rows, out_sums, wide_sums)
    grad_mid = grad_rows[0]

    wide_sums = swapped(wide_sums, SHARDS)
    early_sums, grad_middle, grad_mixed = weight_terms(
        at, unit_one, (), (active_one, mixed_one, grad_rows), (down_turned_one, dense, slope_one)
    )
    blocks, grad_proj = back_attend(grad_mixed, grad_middle, qkv_turned_one, up_turned_one, kept_one)
    blocks_hidden = run(
        project_kernel,
        at,
        (active_two, mixed_two, down_two, dense),
        block_outs,
        [pltpu.VMEM((128, 1024), BF)],
        flops=1_500_000_000,
        others=[grad_proj],
    )
    joined_hidden = joined_cores(blocks_hidden)
    blocks, grad_proj, out_sums, wide_sums, early_sums, joined_hidden = barrier(
        blocks, grad_proj, out_sums, wide_sums, early_sums, joined_hidden
    )

    def turned_dense(total):
        dense = jnp.concatenate([transposed(total[:128, 512:640]), total[128:, 512:640]], axis=0)
        return jnp.concatenate([total[:, :512], dense, total[:, 640:]], axis=1)

    def to_keeper(parts, layer):
        return route(parts, lambda c, x, zh, y, zl: (layer, x, zh, y, zl) if c != layer else None)

    early_sums = swapped(early_sums, SHARDS)
    joined = joined_cores(blocks)
    late_sums = weight_terms(at, unit_one, (grad_proj,), others=joined[1:])
    grad_one = grad_mid.astype(F32) + norm_back(joined_chips(joined), own_tokens)
    grad_low = grad_one.astype(BF)
    out_sums, wide_sums = after((out_sums, wide_sums), joined[1:])
    hidden_two = hidden_one.astype(F32) + joined_chips(joined_hidden) + bias_out_two[:1, :]
    hidden_two = hidden_two.astype(BF)
    second = turned_dense(jnp.concatenate([summed(out_sums), summed(wide_sums)], axis=1).astype(BF))
    second_high = across_high(second)
    early_sums, late_sums, grad_low, hidden_two, second, second_high = barrier(
        early_sums, late_sums, grad_low, hidden_two, second, second_high
    )
    late_sums = swapped(late_sums, SHARDS)
    second = added(second, second_high).astype(BF)
    second = [second] + [along_x(second, -r) for r in (1, 2, 3)]
    early = turned_dense(summed(after(early_sums, second[1])).astype(BF))
    grad_beside, hidden_beside = across_cores(grad_low), across_cores(hidden_two)
    late_sums, second, early, grad_beside, hidden_beside = barrier(late_sums, second, early, grad_beside, hidden_beside)
    first = jnp.concatenate([early, summed(late_sums).astype(BF)], axis=1)
    first = added(first, across_high(first)).astype(BF)
    first = [first] + [along_x(first, -r) for r in (1, 2, 3)]
    first_sums = first + [to_keeper(block, 0) for block in first]
    second_sums = second + [to_keeper(block, 1) for block in second]

    def placed(pairs):
        local, lent = [], []
        for own, beside in pairs:
            low = jnp.where(first_core, own, beside)
            high = jnp.where(first_core, beside, own)
            local.append(jnp.concatenate([low[:UNIT], high[:UNIT]], axis=0))
            lent.append(jnp.concatenate([low[UNIT:], high[UNIT:]], axis=0))
        local, lent = jnp.stack(local), across_high(jnp.stack(lent))
        return jnp.stack([jnp.where(zh == 0, local, lent), jnp.where(zh == 0, lent, local)], axis=1)

    outputs = placed(
        [
            (jnp.where(first_core, hidden_one, hidden_two), jnp.where(first_core, rows_two[1], hidden_beside)),
            (jnp.where(first_core, grad_low, grad_mid), jnp.where(first_core, grad_beside, grad_rows[1])),
        ]
    )
    hidden, in_grads = outputs[0], outputs[1].astype(F32)
    outs = run(
        final_kernel,
        at,
        (
            *first_sums, *second_sums,
            w_qkv[0], w_up[0], norm1_gain, norm1_shift, norm2_gain, norm2_shift,
        ),
        [((128, 3072), F32), ((128, 4096), F32), ((512, 1024), F32), ((128, 1024), F32)]
        + [((1, 256), F32), ((1, 128), F32), ((1, 512), F32)]
        + [((1, 128), F32)] * 5,
        [
            pltpu.VMEM((2, 4, 144, 1536), BF),
            pltpu.VMEM((24, 128), F32),
            pltpu.VMEM((32, 128), F32),
            pltpu.VMEM((8, 128), F32),
            pltpu.SemaphoreType.DMA((8,)),
        ],
        spaces=[anywhere] * 16 + [vmem] * 6,
    )
    grad_qkv, grad_up, grad_down, grad_dense, bias_qk, bias_v, bias_up, bias_out, *norms = outs
    return (
        hidden[None], in_grads[None], grad_qkv[None], bias_qk, bias_v, grad_dense[None], bias_out,
        grad_up[None], bias_up, grad_down[None], bias_out, *norms,
    )


def solution(mesh):
    mesh = Mesh(mesh.devices.reshape(2, 4, 2, 4, 2), AXES)
    rows = P("core", SHARDS, None)
    vector = P("core", SHARDS)
    tokens = P(SHARDS, ("x", "z_hi"), None)
    layered = P("core", SHARDS, ("x", "z_hi"), None)
    in_specs = (
        tokens, P(SHARDS, None),
        rows, vector, rows, vector, rows, vector, rows, vector, vector, vector, vector, vector,
        tokens,
    )
    out_specs = (
        layered, layered,
        rows, vector, vector, rows, vector, rows, vector, rows, vector, vector, vector, vector, vector,
    )
    return jax.shard_map(shards, mesh=mesh, in_specs=in_specs, out_specs=out_specs, check_vma=False)
```

```python
import math

import jax
import jax.numpy as jnp
from jax import lax
from jax.experimental import pallas as pl
from jax.experimental.pallas import tpu as pltpu
from jax.sharding import Mesh
from jax.sharding import PartitionSpec as P

HEAD = 64
ROT = 16
NORM_EPS = 1e-05
BF = jnp.bfloat16
F32 = jnp.float32
AXES = ("core", "x", "z_hi", "y", "z_lo")
SHARDS = ("y", "z_lo")
LENGTH = 1024
WIDTH = 1024
QROWS = 256
UNIT = 64


def place_of(index):
    return index // 64, (index // 16) % 4, (index // 8) % 2, (index // 2) % 4, index % 2


def index_of(core, x, zh, y, zl):
    return core * 64 + x * 16 + zh * 8 + 2 * y + zl


def route(block, target):
    targets = [target(*place_of(i)) for i in range(128)]
    pairs = [(i, index_of(*place)) for i, place in enumerate(targets) if place is not None]
    return lax.ppermute(block, AXES, pairs)


def from_all(block, axes):
    count = math.prod(lax.axis_size(axis) for axis in axes)
    return swapped(jnp.broadcast_to(block[None], (count, *block.shape)), axes)


def swapped(blocks, axes):
    return lax.all_to_all(blocks, axes, split_axis=0, concat_axis=0, tiled=True)


def along_x(block, step):
    return route(block, lambda c, x, zh, y, zl: (c, (x + step) % 4, zh, y, zl))


def along_y(block, step):
    return route(block, lambda c, x, zh, y, zl: (c, x, zh, (y + step) % 4, zl))


def across_low(block):
    return route(block, lambda c, x, zh, y, zl: (c, x, zh, y, 1 - zl))


def across_cores(block):
    return route(block, lambda c, x, zh, y, zl: (1 - c, x, zh, y, zl))


def across_high(block):
    return route(block, lambda c, x, zh, y, zl: (c, x, 1 - zh, y, zl))


def transposed(block):
    return route(block, lambda c, x, zh, y, zl: (zl, y, zh, x, c))


def pick(array, index, axis=0):
    return lax.dynamic_index_in_dim(array, index, axis, keepdims=False)


def dot(left, right):
    return jnp.dot(left, right, preferred_element_type=F32)


def dot_left(left, right):
    return lax.dot_general(left, right, (((0,), (0,)), ((), ())), preferred_element_type=F32)


def dot_right(left, right):
    return lax.dot_general(left, right, (((1,), (1,)), ((), ())), preferred_element_type=F32)


def head_lanes(rows, head):
    lanes = lax.broadcasted_iota(jnp.int32, (rows, 2 * HEAD), 1)
    return (lanes >= head * HEAD) & (lanes < (head + 1) * HEAD)


def turned(values, cosine, sine_low, sine_high):
    return (
        values * cosine
        + pltpu.roll(values, ROT // 2, 1) * sine_low
        + pltpu.roll(values, 2 * HEAD - ROT // 2, 1) * sine_high
    )


def masked_scores(query, keys, begin, block, reach):
    scores = dot_right(query, keys)
    rows = block * QROWS + lax.broadcasted_iota(jnp.int32, (QROWS, reach), 0)
    columns = lax.broadcasted_iota(jnp.int32, (QROWS, reach), 1)
    seen = (columns <= rows) & (columns >= begin)
    return jnp.where(seen, scores, -1e30)


def unit_rows(where_ref, m):
    return pl.ds(pl.multiple_of(where_ref[WHERE + m] * UNIT, UNIT), UNIT)


def attend(where_ref, proj_ref, tables, mixed_ref, q_ref, k_ref, v_ref, o_ref, lse_ref):
    cos_ref, low_ref, high_ref, begin_ref = tables
    for m in range(LENGTH // UNIT):
        here = pl.ds(m * UNIT, UNIT)
        proj = proj_ref[unit_rows(where_ref, m), :]
        cosine, low, high = cos_ref[here, :], low_ref[here, :], high_ref[here, :]
        query = turned(proj[:, :128].astype(F32), cosine, low, high)
        q_ref[here, :] = (query.astype(BF).astype(F32) * (1.0 / math.sqrt(HEAD))).astype(BF)
        k_ref[here, :] = turned(proj[:, 128:256].astype(F32), cosine, low, high).astype(BF)
        v_ref[here, :] = proj[:, 256:]
    for block in range(LENGTH // QROWS):
        rows = pl.ds(block * QROWS, QROWS)
        reach = (block + 1) * QROWS
        keys, values = k_ref[:reach, :], v_ref[:reach, :]
        query = q_ref[rows, :]
        begin = begin_ref[rows, :1]
        outs, logs = [], []
        for head in range(2):
            own = head_lanes(QROWS, head)
            scores = masked_scores(jnp.where(own, query, jnp.zeros_like(query)), keys, begin, block, reach)
            highest = jnp.max(scores, axis=-1, keepdims=True)
            exponent = jnp.exp(scores - highest)
            total = jnp.sum(exponent, axis=-1, keepdims=True)
            probs = (exponent * (1.0 / total)).astype(BF)
            outs.append(dot(probs, values))
            logs.append(highest + jnp.log(total))
        first = head_lanes(QROWS, 0)
        o_ref[rows, :] = jnp.where(first, outs[0], outs[1]).astype(BF)
        lse_ref[rows, :] = jnp.where(first, logs[0], logs[1])
    for m in range(LENGTH // UNIT):
        mixed_ref[unit_rows(where_ref, m), :] = o_ref[pl.ds(m * UNIT, UNIT), :]


def attend_back(where_ref, tables, kept, do_ref, out_ref, dq_ref, dk_ref, dv_ref):
    cos_ref, low_ref, high_ref, begin_ref = tables
    q_ref, k_ref, v_ref, o_ref, lse_ref = kept
    for block in reversed(range(LENGTH // QROWS)):
        rows = pl.ds(block * QROWS, QROWS)
        reach = (block + 1) * QROWS
        keys, values = k_ref[:reach, :], v_ref[:reach, :]
        query, upstream, mixed = q_ref[rows, :], do_ref[rows, :], o_ref[rows, :].astype(F32)
        begin = begin_ref[rows, :1]
        grads = []
        for head in range(2):
            own = head_lanes(QROWS, head)
            query_own = jnp.where(own, query, jnp.zeros_like(query))
            up_own = jnp.where(own, upstream, jnp.zeros_like(upstream))
            scores = masked_scores(query_own, keys, begin, block, reach)
            probs = jnp.exp(scores - lse_ref[rows, head * HEAD : head * HEAD + 1])
            centre = jnp.sum(up_own.astype(F32) * mixed, axis=-1, keepdims=True)
            moved = (probs * (dot_right(up_own, values) - centre)).astype(BF)
            grads.append(dot(moved, keys))
            dk = dot_left(moved, query_own)
            dv = dot_left(probs.astype(BF), up_own)
            if block == LENGTH // QROWS - 1 and head == 0:
                dk_ref[...] = dk
                dv_ref[...] = dv
            else:
                dk_ref[:reach, :] += dk
                dv_ref[:reach, :] += dv
        first = head_lanes(QROWS, 0)
        dq_ref[rows, :] = jnp.where(first, grads[0], grads[1]) * (1.0 / math.sqrt(HEAD))
    for m in range(LENGTH // UNIT):
        here = pl.ds(m * UNIT, UNIT)
        there = unit_rows(where_ref, m)
        cosine, low, high = cos_ref[here, :], -low_ref[here, :], -high_ref[here, :]
        out_ref[there, :128] = turned(dq_ref[here, :], cosine, low, high).astype(BF)
        out_ref[there, 128:256] = turned(dk_ref[here, :], cosine, low, high).astype(BF)
        out_ref[there, 256:384] = dv_ref[here, :].astype(BF)


def barrier(*values):
    flat, tree = jax.tree.flatten(values)
    anywhere = pl.BlockSpec(memory_space=pl.ANY)
    flat = pl.pallas_call(
        lambda *refs: None,
        out_shape=[jax.ShapeDtypeStruct(value.shape, value.dtype) for value in flat],
        in_specs=[anywhere] * len(flat),
        out_specs=[anywhere] * len(flat),
        input_output_aliases={k: k for k in range(len(flat))},
    )(*flat)
    return jax.tree.unflatten(tree, flat)


def after(values, *others):
    flat, tree = jax.tree.flatten(values)
    others = jax.tree.leaves(others)
    anywhere = pl.BlockSpec(memory_space=pl.ANY)
    flat = pl.pallas_call(
        lambda *refs: None,
        out_shape=[jax.ShapeDtypeStruct(value.shape, value.dtype) for value in flat],
        in_specs=[anywhere] * (len(flat) + len(others)),
        out_specs=[anywhere] * len(flat),
        input_output_aliases={k: k for k in range(len(flat))},
    )(*flat, *others)
    return jax.tree.unflatten(tree, flat)


def run(body, scalars, arrays, outs, scratch=(), flops=0, spaces=None, others=()):
    vmem, anywhere = pl.BlockSpec(memory_space=pltpu.VMEM), pl.BlockSpec(memory_space=pl.ANY)
    others = jax.tree.leaves(others)
    count = 1 + len(arrays)
    return pl.pallas_call(
        lambda *refs: body(*refs[:count], *refs[count + len(others) :]),
        out_shape=[jax.ShapeDtypeStruct(*out) for out in outs],
        in_specs=[pl.BlockSpec(memory_space=pltpu.SMEM)]
        + (spaces or [vmem] * len(arrays))
        + [anywhere] * len(others),
        out_specs=[vmem] * len(outs),
        scratch_shapes=list(scratch),
        compiler_params=pltpu.CompilerParams(vmem_limit_bytes=60 * 1024 * 1024),
        cost_estimate=pl.CostEstimate(flops=flops, bytes_accessed=4_000_000, transcendentals=0),
    )(scalars, *arrays, *others)


X, CORE, ZH, Y, ZL, PART, SHARD, BIAS, WHERE = 0, 1, 2, 3, 4, 5, 6, 7, 10


def lanes(start, extent=128):
    return pl.ds(pl.multiple_of(start, extent), extent)


def low_half(rows):
    return lax.broadcasted_iota(jnp.int32, (rows, 128), 1) < 64


def half_tiles(first, second):
    low = low_half(first.shape[0])
    return (
        jnp.where(low, first, pltpu.roll(second, 64, 1)),
        jnp.where(low, pltpu.roll(first, 64, 1), second),
    )


def block_rows(number, extent):
    return pl.ds(pl.multiple_of(extent * number, extent), extent)


def column(row):
    return jnp.transpose(jnp.broadcast_to(row, (128, 128)))


def slice_kernel(
    at, qkv_all, up_all, down_all, dense_all, bias_qkv_all, bias_up_all, bias_dense, bias_down, gain_one, shift_one,
    gain_two, shift_two,
    qkv_self, qkv_other, rest_self, rest_other,
    qkv, up, down, dense, bias_qkv, small, rows, sems,
):
    x, core = at[X], at[CORE]
    copies = [(up_all.at[:, lanes(512 * k + 128 * x)], up.at[k]) for k in range(8)]
    copies += [(qkv_all.at[:, lanes(1024 * k + 256 * x, 256)], qkv.at[k]) for k in range(3)]
    copies.append((down_all.at[pl.ds(pl.multiple_of(128 * x, 128), 128), :], down))
    copies.append((dense_all.at[:, lanes(256 * x, 256)], dense))
    copies.append((bias_qkv_all, bias_qkv))
    copies.append((bias_up_all.at[:, lanes(128 * x)], small.at[0]))
    for k, vector in enumerate((bias_dense, bias_down, gain_one, shift_one, gain_two, shift_two)):
        copies.append((vector, small.at[1 + k]))
    copies = [pltpu.make_async_copy(*pair, sems.at[k]) for k, pair in enumerate(copies)]
    for copy in copies:
        copy.start()
    for copy in copies:
        copy.wait()
    for k in range(4):
        zero, one = half_tiles(up[2 * k].astype(F32), up[2 * k + 1].astype(F32))
        here = slice(128 * k, 128 * k + 128)
        rest_self[:, here] = jnp.where(core == 0, zero, one).astype(BF)
        rest_other[:, here] = jnp.where(core == 0, one, zero).astype(BF)
    for k in range(3):
        first, second = qkv[k, :, :128], qkv[k, :, 128:]
        here = slice(128 * k, 128 * k + 128)
        qkv_self[:128, here] = jnp.where(core == 0, first, second)
        qkv_other[:128, here] = jnp.where(core == 0, second, first)
    for k in range(2):
        first, second = down[:64, 512 * k : 512 * k + 512], down[64:, 512 * k : 512 * k + 512]
        rest_self[64 * k : 64 * k + 64, 512:] = jnp.where(core == 0, first, second)
        rest_other[64 * k : 64 * k + 64, 512:] = jnp.where(core == 0, second, first)
    first, second = dense[:, :128], dense[:, 128:]
    qkv_self[:128, 384:] = jnp.where(core == 0, first, second)
    qkv_other[:128, 384:] = jnp.where(core == 0, second, first)
    rows[...] = jnp.zeros_like(rows)
    for k in range(3):
        rows[k : k + 1, :] = bias_qkv[:, 128 * k : 128 * k + 128].astype(F32)
    for k in range(7):
        rows[3 + k : 4 + k, :] = small[k].astype(F32)
    plain = rows[...]
    number = lax.broadcasted_iota(jnp.int32, (16, 128), 0)
    moved = jnp.where(number == 3, pltpu.roll(plain, 64, 1), plain)
    for out, upper in ((qkv_self, core), (qkv_other, 1 - core)):
        out[128:, :128] = jnp.where(upper == 0, plain, moved).astype(BF)
        out[128:, 128:] = jnp.zeros((16, 384), BF)


def tables_kernel(at, places, frequency, cos_ref, low_ref, high_ref, begin_ref):
    place = jnp.transpose(jnp.broadcast_to(places[...].astype(F32), (128, LENGTH)))
    lane = lax.broadcasted_iota(jnp.int32, (LENGTH, 128), 1) % HEAD
    angles = place * frequency[...]
    sine = jnp.sin(angles)
    cos_ref[...] = jnp.where(lane < ROT, jnp.cos(angles), 1.0)
    low_ref[...] = jnp.where((lane >= ROT // 2) & (lane < ROT), sine, 0.0)
    high_ref[...] = jnp.where(lane < ROT // 2, -sine, 0.0)
    row = lax.broadcasted_iota(jnp.int32, (LENGTH, 128), 0)
    begin_ref[...] = row - place.astype(jnp.int32)


def prepare_qkv(at, blocks, wide, wide_turned, bias, bias_out, rows):
    bias[...] = jnp.zeros_like(bias)
    for shard, message in blocks:
        vectors = message[128:, :128].astype(F32)
        rows[16 * shard : 16 * shard + 16, :] = vectors
        here = slice(128 * shard, 128 * shard + 128)
        scale = column(vectors[6:7, :])
        for k in range(0, 384, 128):
            wide[here, k : k + 128] = (message[:128, k : k + 128].astype(F32) * scale).astype(BF)
        shift = jnp.broadcast_to(vectors[7:8, :], (8, 128)).astype(BF)
        bias[:, :384] += dot(shift, message[:128, :384])
    for k in range(3):
        bias[:, 128 * k : 128 * k + 128] += jnp.broadcast_to(rows[pl.ds(at[BIAS + k], 1), :], (8, 128))
    for shard in range(8):
        total = rows[16 * shard + 4 : 16 * shard + 5, :] + rows[16 * shard + 5 : 16 * shard + 6, :]
        bias_out[:, 128 * shard : 128 * shard + 128] = jnp.broadcast_to(total, (8, 128))
    wide_turned[...] = jnp.transpose(wide[...])


def prepare_up(at, blocks, rows, up, up_turned, bias):
    bias[...] = jnp.zeros_like(bias)
    for shard, message in blocks:
        vectors = rows[16 * shard : 16 * shard + 16, :]
        here = slice(128 * shard, 128 * shard + 128)
        scale = column(vectors[8:9, :])
        for k in range(0, 512, 128):
            up[here, k : k + 128] = (message[:128, k : k + 128].astype(F32) * scale).astype(BF)
        shift = jnp.broadcast_to(vectors[9:10, :], (8, 128)).astype(BF)
        bias[...] += dot(shift, message[:128, :512])
    for k in range(4):
        first = jnp.broadcast_to(rows[32 * k + 3 : 32 * k + 4, :], (8, 128))
        second = jnp.broadcast_to(rows[32 * k + 19 : 32 * k + 20, :], (8, 128))
        bias[:, 128 * k : 128 * k + 128] += half_tiles(first, second)[0]
    up_turned[...] = jnp.transpose(up[...])


def prepare_down(blocks, down, down_turned):
    for k, halves in enumerate(blocks):
        down[64 * k : 64 * k + 64, :512] = halves[:64, :]
        down[64 * k : 64 * k + 64, 512:] = halves[64:128, :]
    down_turned[...] = jnp.transpose(down[...])


def project_rows(blocks, qkv, bias, unit, proj):
    for k in range(8):
        values = blocks[k][...].astype(F32)
        centred = values - jnp.mean(values, axis=-1, keepdims=True)
        spread = jnp.mean(centred * centred, axis=-1, keepdims=True)
        unit[128 * k : 128 * k + 128, :] = (centred * lax.rsqrt(spread + NORM_EPS)).astype(BF)
    for k in range(4):
        here = slice(256 * k, 256 * k + 256)
        proj[here, :] = (dot(unit[here, :], qkv[...]) + bias[:1, :]).astype(BF)


def activate(unit, up, bias, active, slope):
    for k in range(4):
        here = slice(256 * k, 256 * k + 256)
        middle = dot(unit[here, :], up[...]) + bias[:1, :]
        share = 0.5 * (1.0 + lax.erf(middle * (1.0 / math.sqrt(2.0))))
        density = jnp.exp(-0.5 * middle * middle) * (1.0 / math.sqrt(2.0 * math.pi))
        active[here, :] = (middle * share).astype(BF)
        slope[here, :] = (share + middle * density).astype(BF)


def attend_first_kernel(at, *refs):
    blocks, messages, tables, outs = refs[:8], refs[8], refs[9:13], refs[13:]
    qkv_turned, bias_out, vectors, unit, mixed, *kept = outs[:10]
    qkv, bias, proj = outs[10:]
    prepare_qkv(at, [(k, messages.at[k]) for k in range(8)], qkv, qkv_turned, bias, bias_out, vectors)
    project_rows(blocks, qkv, bias, unit, proj)
    attend(at, proj, tables, mixed, *kept)


def attend_second_kernel(at, *refs):
    blocks, messages, tables, outs = refs[:8], refs[8], refs[9:13], refs[13:]
    qkv_turned, bias_out, up_turned, active, slope, unit, mixed, *kept = outs[:12]
    qkv, bias, proj, vectors, up, up_bias = outs[12:]
    prepare_qkv(at, [(k, messages.at[k]) for k in range(8)], qkv, qkv_turned, bias, bias_out, vectors)
    prepare_up(at, [(k, messages.at[k, :, 384:]) for k in range(8)], vectors, up, up_turned, up_bias)
    project_rows(blocks, qkv, bias, unit, proj)
    activate(unit, up, up_bias, active, slope)
    attend(at, proj, tables, mixed, *kept)


def dense_parts_of(at, parts, layer):
    for r in range(4):
        for beside in range(2):
            part = 2 * ((at[X] + 4 - r) % 4) + (at[CORE] + beside) % 2
            yield part, parts[beside, r, :, 128 * layer : 128 * layer + 128]


def project(at, layer, active, mixed, down, dense_parts, dense, blocks):
    for part, columns in dense_parts_of(at, dense_parts, layer):
        dense[:, lanes(128 * part)] = columns
    for k in (2, 1, 3, 0):
        here = slice(256 * k, 256 * k + 256)
        out = dot(active[here, :], down[...]) + dot(mixed[here, :], dense[...])
        blocks[2 * k][...] = out[:128].astype(BF)
        blocks[2 * k + 1][...] = out[128:].astype(BF)


def rest_first_kernel(at, messages, vectors, unit, mixed, dense_parts, up_turned, down_turned, active, slope, *refs):
    blocks, (up, bias, down, dense) = refs[:8], refs[8:]
    prepare_up(at, [(k, messages.at[k]) for k in range(8)], vectors, up, up_turned, bias)
    prepare_down([messages.at[k, :, 512:] for k in range(8)], down, down_turned)
    activate(unit, up, bias, active, slope)
    project(at, 0, active, mixed, down, dense_parts, dense, blocks)


def project_kernel(at, active, mixed, down, dense_parts, *refs):
    project(at, 1, active, mixed, down, dense_parts, refs[8], refs[:8])


def pull_back(at, layer, blocks, down_turned, dense_parts, slope, grad_middle, grad_mixed, dense_turned, together):
    for k in range(8):
        together[128 * k : 128 * k + 128, :] = blocks[k][...]
    for part, columns in dense_parts_of(at, dense_parts, layer):
        dense_turned[block_rows(part, 128), :] = jnp.transpose(columns)
    for k in range(4):
        here = slice(256 * k, 256 * k + 256)
        rows = together[here, :]
        grad_middle[here, :] = (dot(rows, down_turned[...]) * slope[here, :].astype(F32)).astype(BF)
        grad_mixed[here, :] = dot(rows, dense_turned[...]).astype(BF)


def back_second_kernel(at, *refs):
    rows, (messages, dense_parts, slope), qkv_turned, up_turned = refs[:8], refs[8:11], refs[11], refs[12]
    tables, kept, blocks = refs[13:17], refs[17:22], refs[22:30]
    grad_proj, grad_middle, down, down_turned, dense_turned, grad_mixed, together, *scratch = refs[30:]
    prepare_down([messages.at[k] for k in range(8)], down, down_turned)
    pull_back(at, 1, rows, down_turned, dense_parts, slope, grad_middle, grad_mixed, dense_turned, together)
    back_attend_kernel(
        at, grad_mixed, grad_middle, qkv_turned, up_turned, *tables, *kept, *blocks, grad_proj, *scratch
    )


def back_attend_kernel(where_ref, grad_mixed, grad_middle, wide_turned, up_turned, cosine, low, high, begin, *refs):
    kept, blocks, grad_proj, (do_ref, dq_ref, dk_ref, dv_ref) = refs[:5], refs[5:13], refs[13], refs[14:]
    for m in range(LENGTH // UNIT):
        do_ref[pl.ds(m * UNIT, UNIT), :] = grad_mixed[unit_rows(where_ref, m), :]
    attend_back(where_ref, (cosine, low, high, begin), kept, do_ref, grad_proj, dq_ref, dk_ref, dv_ref)
    for k in (2, 1, 3, 0):
        here = slice(256 * k, 256 * k + 256)
        out = dot(grad_proj[here, :], wide_turned[...]) + dot(grad_middle[here, :], up_turned[...])
        blocks[2 * k][...] = out[:128].astype(BF)
        blocks[2 * k + 1][...] = out[128:].astype(BF)


def weight_terms(at, unit, grads, outward=None, pulled=None, others=()):
    extent = 512 if pulled else sum(grad.shape[1] for grad in grads)
    start = 640 if outward else 0
    arrays, scratch, outs = (unit, *grads), [], [((8, 144, start + extent), BF)]
    if outward:
        active, mixed, rows, *grad_middle = outward
        arrays = (*arrays, active, mixed, *rows, *grad_middle)
        scratch = [pltpu.VMEM((1024, 1024), BF)]
    if pulled:
        arrays = (*arrays, *pulled)
        outs += [((1024, 512), BF), ((1024, 128), BF)]
        scratch.append(pltpu.VMEM((1024, 128), BF))

    def body(at, unit, *refs):
        grad_refs, refs = refs[: len(grads)], refs[len(grads) :]
        if pulled:
            (active, mixed), rows, refs = refs[:2], refs[2:10], refs[10:]
            (down_turned, dense_parts, slope), (out, grad_middle, grad_mixed) = refs[:3], refs[3:6]
            together, dense_turned = refs[6:]
            pull_back(
                at, 0, rows, down_turned, dense_parts, slope, grad_middle, grad_mixed, dense_turned, together
            )
            grad_refs = (grad_middle,)
        elif outward:
            (active, mixed), rows, grad_middle, out, together = refs[:2], refs[2:10], *refs[10:]
            for k in range(8):
                together[128 * k : 128 * k + 128, :] = rows[k][...]
        else:
            out = refs[0]
        if outward:
            sums = jnp.sum(together[:, lanes(128 * at[PART])].astype(F32), axis=0, keepdims=True)
            sums_up = jnp.sum(grad_middle[...].astype(F32), axis=0, keepdims=True)
            dense = dot_left(mixed[...], together[...]).astype(BF)
            for shard in range(8):
                if shard % 4 == 0:
                    down = dot_left(active[:, 64 * shard : 64 * shard + 256], together[...]).astype(BF)
                for half in range(2):
                    piece = down[64 * (shard % 4) : 64 * (shard % 4) + 64, 512 * half : 512 * half + 512]
                    out[shard, 64 * half : 64 * half + 64, :512] = piece
                out[shard, :128, 512:640] = dense[:, 128 * shard : 128 * shard + 128]
                out[shard, 128:, :128] = jnp.broadcast_to(sums, (16, 128)).astype(BF)
                out[shard, 128:, 128:640] = jnp.broadcast_to(sums_up, (16, 512)).astype(BF)
        at_column = start
        for grad in grad_refs:
            columns = grad.shape[1]
            here = slice(at_column, at_column + columns)
            sums = jnp.sum(grad[...].astype(F32), axis=0, keepdims=True)
            for shard in range(8):
                if shard % 2 == 0:
                    terms = dot_left(unit[:, 128 * shard : 128 * shard + 256], grad[...]).astype(BF)
                out[shard, :128, here] = terms[128 * (shard % 2) : 128 * (shard % 2) + 128, :]
                out[shard, 128:, here] = jnp.broadcast_to(sums, (16, columns)).astype(BF)
            at_column += columns

    outs = run(body, at, arrays, outs, scratch, flops=2 * 1024 * 1024 * (extent + start), others=others)
    return outs if pulled else outs[0]


def final_kernel(at, *refs):
    sources = refs[:8], refs[8:16]
    qkv, up, gain_one, shift_one, gain_two, shift_two = refs[16:22]
    grad_qkv, grad_up, grad_down, grad_dense = refs[22:26]
    bias_qk, bias_v, bias_up, bias_out, gain_a, shift_a, gain_b, shift_b = refs[26:34]
    sums, sums_qkv, sums_up, sums_out, sems = refs[34:]
    x, core, shard = at[X], at[CORE], at[SHARD]
    for layer in range(2):

        @pl.when(core == layer)
        def _():
            copies = []
            for k in range(8):
                target = sums.at[k // 4, (x + k % 4) % 4]
                copies.append(pltpu.make_async_copy(sources[layer][k], target, sems.at[k]))
            for copy in copies:
                copy.start()
            for copy in copies:
                copy.wait()

    def whole(beside, r, columns):
        return sums[beside, r, :128, columns].astype(F32)

    def below(beside, r, columns):
        return sums[beside, r, 128:, columns].astype(F32)

    gain_col, shift_col = column(gain_one[...].astype(F32)), column(shift_one[...].astype(F32))
    gain_col_two, shift_col_two = column(gain_two[...].astype(F32)), column(shift_two[...].astype(F32))
    totals = [jnp.zeros((128, 128), F32) for _ in range(4)]
    for r in range(4):
        column_no = r
        for half in range(2):
            beside = (core + half) % 2
            part = 2 * column_no + half
            for k in range(3):
                cols = slice(1152 + 128 * k, 1280 + 128 * k)
                raw = whole(beside, r, cols)
                total = below(beside, r, cols)[:1]
                place = lanes(1024 * k + 128 * part)
                weight = qkv[:, place].astype(F32)
                grad_qkv[:, place] = gain_col * raw + shift_col * total
                sums_qkv[pl.ds(8 * k + part, 1), :] = total
                totals[0] += weight * raw
                totals[1] += weight * total
            grad_down[pl.ds(pl.multiple_of(64 * part, 64), 64), :512] = sums[beside, r, :64, :512].astype(F32)
            grad_down[pl.ds(pl.multiple_of(64 * part, 64), 64), 512:] = sums[beside, r, 64:128, :512].astype(F32)
            grad_dense[:, lanes(128 * part)] = whole(beside, r, slice(512, 640))
            sums_out[pl.ds(part, 1), :] = below(beside, r, slice(0, 128))[:1]
        zero, one = core % 2, (core + 1) % 2
        for k in range(4):
            cols = slice(640 + 128 * k, 768 + 128 * k)
            beneath = slice(128 + 128 * k, 256 + 128 * k)
            raws = half_tiles(whole(zero, r, cols), whole(one, r, cols))
            adds = half_tiles(below(zero, r, beneath), below(one, r, beneath))
            for odd in range(2):
                raw, total = raws[odd], adds[odd][:1]
                place = lanes(1024 * k + 512 * odd + 128 * column_no)
                weight = up[:, place].astype(F32)
                grad_up[:, place] = gain_col_two * raw + shift_col_two * total
                sums_up[pl.ds(8 * k + 4 * odd + column_no, 1), :] = total
                totals[2] += weight * raw
                totals[3] += weight * total
    for out, total in zip((gain_a, shift_a, gain_b, shift_b), totals):
        out[...] = jnp.sum(jnp.transpose(total), axis=0, keepdims=True)
    for k in range(2):
        bias_qk[:, 128 * k : 128 * k + 128] = sums_qkv[pl.ds(2 * shard + k, 1), :]
    bias_v[...] = sums_qkv[pl.ds(16 + shard, 1), :]
    for k in range(4):
        bias_up[:, 128 * k : 128 * k + 128] = sums_up[pl.ds(4 * shard + k, 1), :]
    bias_out[...] = sums_out[pl.ds(shard, 1), :]


def added(*blocks):
    total = blocks[0].astype(F32)
    for block in blocks[1:]:
        total = total + block.astype(F32)
    return total


def gather_rows(mine):
    own = [mine] + [along_x(mine, -r) for r in (1, 2, 3)]
    other = [across_cores(block) for block in own]
    return [rows for pair in zip(own, other) for rows in pair]


def joined_cores(blocks):
    joined = {r: added(blocks[2 * r], across_cores(blocks[2 * r + 1])) for r in (2, 1, 3, 0)}
    return [joined[0]] + [joined[r].astype(BF) for r in (1, 2, 3)]


def joined_chips(joined):
    return added(joined[0], *(along_x(joined[r], r) for r in (1, 2, 3)))


def summed(blocks):
    return jnp.sum(blocks.astype(F32), axis=0)


def normalized(rows):
    values = rows.astype(F32)
    centre = jnp.mean(values, axis=-1, keepdims=True)
    centred = values - centre
    spread = jnp.mean(centred * centred, axis=-1, keepdims=True)
    scale = lax.rsqrt(spread + NORM_EPS)
    return centred * scale, scale


def norm_back(grad, rows):
    unit, scale = normalized(rows)
    mean_grad = jnp.mean(grad, axis=-1, keepdims=True)
    mean_both = jnp.mean(grad * unit, axis=-1, keepdims=True)
    return scale * (grad - mean_grad - unit * mean_both)


def shards(
    tokens, positions, w_qkv, b_qkv, w_dense, b_dense, w_up, b_up, w_down, b_down,
    norm1_gain, norm1_shift, norm2_gain, norm2_shift, cotangent,
):
    core, x, zh, y, zl = (lax.axis_index(axis) for axis in AXES)
    shard = 2 * y + zl
    part = 2 * x + core
    first_core = core == 0
    anywhere, vmem = pl.BlockSpec(memory_space=pl.ANY), pl.BlockSpec(memory_space=pltpu.VMEM)

    bias_rows = [16 * ((8 * k + part) // 3) + (8 * k + part) % 3 for k in range(3)]
    at = jnp.stack([x, core, zh, y, zl, part, shard] + bias_rows).astype(jnp.int32)
    unit_no = jnp.arange(16, dtype=jnp.int32)
    where = (
        ((unit_no // 4 - x) % 4) * 4
        + jnp.bitwise_xor(unit_no % 2, core) * 2
        + jnp.bitwise_xor((unit_no // 2) % 2, zh)
    ).astype(jnp.int32)
    at = jnp.concatenate([at, where])

    own, lent = [], []
    for array in (tokens, cotangent):
        own.append(lax.dynamic_slice_in_dim(pick(array, zh), core * UNIT, UNIT, 0))
        lent.append(lax.dynamic_slice_in_dim(pick(array, 1 - zh), core * UNIT, UNIT, 0))
    lent = across_high(jnp.stack(lent))
    own_tokens = jnp.concatenate([own[0], lent[0]], axis=0)
    own_cotangent = jnp.concatenate([own[1], lent[1]], axis=0)

    sliced = run(
        slice_kernel,
        at,
        (
            w_qkv[0], w_up[0], w_down[0], w_dense[0], b_qkv, b_up, b_dense, b_down,
            norm1_gain, norm1_shift, norm2_gain, norm2_shift,
        ),
        [((144, 512), BF)] * 2 + [((128, 1024), BF)] * 2,
        [
            pltpu.VMEM((3, 128, 256), BF),
            pltpu.VMEM((8, 128, 128), BF),
            pltpu.VMEM((128, 1024), BF),
            pltpu.VMEM((128, 256), BF),
            pltpu.VMEM((1, 384), BF),
            pltpu.VMEM((7, 1, 128), BF),
            pltpu.VMEM((16, 128), F32),
            pltpu.SemaphoreType.DMA((21,)),
        ],
        spaces=[pl.BlockSpec(memory_space=pltpu.HBM)] * 12,
    )
    qkv_theirs, rest_theirs = across_cores(sliced[1]), across_cores(sliced[3])
    qkv, qkv_two = jnp.where(first_core, sliced[0], qkv_theirs), jnp.where(first_core, qkv_theirs, sliced[0])
    qkv = jnp.concatenate([qkv, qkv_two[:, 384:]], axis=1)
    rest = jnp.where(first_core, sliced[2], rest_theirs)
    rest_two = jnp.where(first_core, rest_theirs, sliced[2])
    wide_two = jnp.concatenate([qkv_two[:, :384], jnp.pad(rest_two[:, :512], ((0, 16), (0, 0)))], axis=1)
    down_two = rest_two[:, 512:]

    half = ROT // 2
    frequency = 1.0 / 10000.0 ** (jnp.arange(half).astype(F32) * 2.0 / ROT)
    frequency = jnp.concatenate([jnp.tile(frequency, HEAD // half)] * 2)[None, :]
    tables = run(
        tables_kernel,
        at,
        (lax.dynamic_slice_in_dim(positions, zh, 1, 0), frequency),
        [((LENGTH, 128), F32)] * 3 + [((LENGTH, 128), jnp.int32)],
    )

    big, head = ((1024, 1024), BF), ((1024, 128), BF)
    kept_outs = [head] * 4 + [((1024, 128), F32)]
    qkv_scratch = [pltpu.VMEM((1024, 384), BF), pltpu.VMEM((8, 384), F32), pltpu.VMEM((1024, 384), BF)]
    grad_scratch = [pltpu.VMEM((1024, 128), BF)] + [pltpu.VMEM((1024, 128), F32)] * 3
    hidden_outs = [((1024, 512), BF)] * 2
    block_outs = [((128, 1024), BF)] * 8
    qkv_outs = [((384, 1024), BF), ((8, 1024), F32)]

    def back_attend(grad_mixed, grad_middle, qkv_turned, up_turned, kept):
        outs = run(
            back_attend_kernel,
            at,
            (grad_mixed, grad_middle, qkv_turned, up_turned, *tables, *kept),
            [((128, 1024), BF)] * 8 + [((1024, 384), BF)],
            grad_scratch,
            flops=6_000_000_000,
        )
        return outs[:8], outs[8]

    qkvs = from_all(after(qkv, own_tokens), SHARDS)
    rows_one = gather_rows(own_tokens)
    rests = from_all(after(rest, qkvs, rows_one[2::2]), SHARDS)
    held = [lax.dynamic_slice(qkvs, (2 * ((x + r) % 4), 0, 384), (2, 128, 256)) for r in range(4)]
    held = [held[0]] + [along_x(held[r], r) for r in (1, 2, 3)]
    dense = jnp.stack([pick(block, core) for block in held])
    dense = jnp.stack([dense, across_cores(jnp.stack([pick(block, 1 - core) for block in held]))])
    qkv_turned_one, bias_out_one, vectors, unit_one, mixed_one, *kept_one = run(
        attend_first_kernel,
        at,
        (*rows_one, qkvs, *tables),
        qkv_outs + [((128, 128), F32), big, head] + kept_outs,
        qkv_scratch,
        flops=5_000_000_000,
    )
    rests, wide_two, dense = after((rests, wide_two, dense), mixed_one)

    wides = from_all(after(wide_two, rests), SHARDS)
    up_turned_one, down_turned_one, active_one, slope_one, *blocks = run(
        rest_first_kernel,
        at,
        (rests, vectors, unit_one, mixed_one, dense),
        [((512, 1024), BF), ((1024, 512), BF)] + hidden_outs + block_outs,
        [
            pltpu.VMEM((1024, 512), BF),
            pltpu.VMEM((8, 512), F32),
            pltpu.VMEM((512, 1024), BF),
            pltpu.VMEM((128, 1024), BF),
        ],
        flops=3_000_000_000,
    )
    joined = joined_cores(blocks)
    hidden_one = own_tokens.astype(F32) + joined_chips(joined) + bias_out_one[:1, :]
    hidden_one = hidden_one.astype(BF)
    rows_two = gather_rows(hidden_one)
    downs = from_all(after(down_two, wides), SHARDS)
    own_cotangent = after(own_cotangent, rows_two[2::2])

    grad_own = [own_cotangent] + [along_x(own_cotangent, -r) for r in (1, 2, 3)]
    qkv_turned_two, bias_out_two, up_turned_two, active_two, slope_two, unit_two, mixed_two, *kept_two = run(
        attend_second_kernel,
        at,
        (*rows_two, wides, *tables),
        qkv_outs + [((512, 1024), BF)] + hidden_outs + [big, head] + kept_outs,
        qkv_scratch
        + [pltpu.VMEM((128, 128), F32), pltpu.VMEM((1024, 512), BF), pltpu.VMEM((8, 512), F32)],
        flops=8_000_000_000,
    )
    grad_own = after(grad_own, mixed_two)
    grad_rows = [rows for block in grad_own for rows in (block, across_cores(block))]

    *blocks, grad_proj, grad_middle, down_two = run(
        back_second_kernel,
        at,
        (*grad_rows, downs, dense, slope_two, qkv_turned_two, up_turned_two, *tables, *kept_two),
        block_outs + [((1024, 384), BF), ((1024, 512), BF), ((512, 1024), BF)],
        [pltpu.VMEM((1024, 512), BF)] + [pltpu.VMEM((1024, 128), BF)] * 2 + [pltpu.VMEM((1024, 1024), BF)] + grad_scratch,
        flops=8_000_000_000,
    )
    joined = joined_cores(blocks)
    out_sums = weight_terms(
        at, unit_two, (), (active_two, mixed_two, grad_rows, grad_middle), others=joined
    )
    joined[0] = after(joined[0], out_sums)
    out_sums = swapped(out_sums, SHARDS)
    grad_two = grad_rows[0].astype(F32) + norm_back(joined_chips(joined), hidden_one)
    grad_mid = grad_two.astype(BF)
    wide_sums = weight_terms(at, unit_two, (grad_middle, grad_proj), others=[grad_mid])
    grad_rows = gather_rows(grad_mid)
    grad_rows, out_sums, wide_sums = barrier(grad_rows, out_sums, wide_sums)
    grad_mid = grad_rows[0]

    wide_sums = swapped(wide_sums, SHARDS)
    early_sums, grad_middle, grad_mixed = weight_terms(
        at, unit_one, (), (active_one, mixed_one, grad_rows), (down_turned_one, dense, slope_one)
    )
    blocks, grad_proj = back_attend(grad_mixed, grad_middle, qkv_turned_one, up_turned_one, kept_one)
    blocks_hidden = run(
        project_kernel,
        at,
        (active_two, mixed_two, down_two, dense),
        block_outs,
        [pltpu.VMEM((128, 1024), BF)],
        flops=1_500_000_000,
        others=[grad_proj],
    )
    joined_hidden = joined_cores(blocks_hidden)
    blocks, grad_proj, out_sums, wide_sums, early_sums, joined_hidden = barrier(
        blocks, grad_proj, out_sums, wide_sums, early_sums, joined_hidden
    )

    def turned_dense(total):
        dense = jnp.concatenate([transposed(total[:128, 512:640]), total[128:, 512:640]], axis=0)
        return jnp.concatenate([total[:, :512], dense, total[:, 640:]], axis=1)

    def to_keeper(parts, layer):
        return route(parts, lambda c, x, zh, y, zl: (layer, x, zh, y, zl) if c != layer else None)

    early_sums = swapped(early_sums, SHARDS)
    joined = joined_cores(blocks)
    late_sums = weight_terms(at, unit_one, (grad_proj,), others=joined[1:])
    grad_one = grad_mid.astype(F32) + norm_back(joined_chips(joined), own_tokens)
    grad_low = grad_one.astype(BF)
    out_sums, wide_sums = after((out_sums, wide_sums), joined[1:])
    hidden_two = hidden_one.astype(F32) + joined_chips(joined_hidden) + bias_out_two[:1, :]
    hidden_two = hidden_two.astype(BF)
    second = turned_dense(jnp.concatenate([summed(out_sums), summed(wide_sums)], axis=1).astype(BF))
    second_high = across_high(second)
    early_sums, late_sums, grad_low, hidden_two, second, second_high = barrier(
        early_sums, late_sums, grad_low, hidden_two, second, second_high
    )
    late_sums = swapped(late_sums, SHARDS)
    second = added(second, second_high).astype(BF)
    second = [second] + [along_x(second, -r) for r in (1, 2, 3)]
    early = turned_dense(summed(after(early_sums, second[1])).astype(BF))
    grad_beside, hidden_beside = across_cores(grad_low), across_cores(hidden_two)
    late_sums, second, early, grad_beside, hidden_beside = barrier(late_sums, second, early, grad_beside, hidden_beside)
    first = jnp.concatenate([early, summed(late_sums).astype(BF)], axis=1)
    first = added(first, across_high(first)).astype(BF)
    first = [first] + [along_x(first, -r) for r in (1, 2, 3)]
    first_sums = first + [to_keeper(block, 0) for block in first]
    second_sums = second + [to_keeper(block, 1) for block in second]

    def placed(pairs):
        local, lent = [], []
        for own, beside in pairs:
            low = jnp.where(first_core, own, beside)
            high = jnp.where(first_core, beside, own)
            local.append(jnp.concatenate([low[:UNIT], high[:UNIT]], axis=0))
            lent.append(jnp.concatenate([low[UNIT:], high[UNIT:]], axis=0))
        local, lent = jnp.stack(local), across_high(jnp.stack(lent))
        return jnp.stack([jnp.where(zh == 0, local, lent), jnp.where(zh == 0, lent, local)], axis=1)

    outputs = placed(
        [
            (jnp.where(first_core, hidden_one, hidden_two), jnp.where(first_core, rows_two[1], hidden_beside)),
            (jnp.where(first_core, grad_low, grad_mid), jnp.where(first_core, grad_beside, grad_rows[1])),
        ]
    )
    hidden, in_grads = outputs[0], outputs[1].astype(F32)
    outs = run(
        final_kernel,
        at,
        (
            *first_sums, *second_sums,
            w_qkv[0], w_up[0], norm1_gain, norm1_shift, norm2_gain, norm2_shift,
        ),
        [((128, 3072), F32), ((128, 4096), F32), ((512, 1024), F32), ((128, 1024), F32)]
        + [((1, 256), F32), ((1, 128), F32), ((1, 512), F32)]
        + [((1, 128), F32)] * 5,
        [
            pltpu.VMEM((2, 4, 144, 1536), BF),
            pltpu.VMEM((24, 128), F32),
            pltpu.VMEM((32, 128), F32),
            pltpu.VMEM((8, 128), F32),
            pltpu.SemaphoreType.DMA((8,)),
        ],
        spaces=[anywhere] * 16 + [vmem] * 6,
    )
    grad_qkv, grad_up, grad_down, grad_dense, bias_qk, bias_v, bias_up, bias_out, *norms = outs
    return (
        hidden[None], in_grads[None], grad_qkv[None], bias_qk, bias_v, grad_dense[None], bias_out,
        grad_up[None], bias_up, grad_down[None], bias_out, *norms,
    )


def solution(mesh):
    mesh = Mesh(mesh.devices.reshape(2, 4, 2, 4, 2), AXES)
    rows = P("core", SHARDS, None)
    vector = P("core", SHARDS)
    tokens = P(SHARDS, ("x", "z_hi"), None)
    layered = P("core", SHARDS, ("x", "z_hi"), None)
    in_specs = (
        tokens, P(SHARDS, None),
        rows, vector, rows, vector, rows, vector, rows, vector, vector, vector, vector, vector,
        tokens,
    )
    out_specs = (
        layered, layered,
        rows, vector, vector, rows, vector, rows, vector, rows, vector, vector, vector, vector, vector,
    )
    return jax.shard_map(shards, mesh=mesh, in_specs=in_specs, out_specs=out_specs, check_vma=False)
```

```python
import math

import jax
import jax.numpy as jnp
from jax import lax
from jax.experimental import pallas as pl
from jax.experimental.pallas import tpu as pltpu
from jax.sharding import Mesh
from jax.sharding import PartitionSpec as P

HEAD = 64
ROT = 16
NORM_EPS = 1e-05
BF = jnp.bfloat16
F32 = jnp.float32
AXES = ("core", "x", "z_hi", "y", "z_lo")
SHARDS = ("y", "z_lo")
LENGTH = 1024
WIDTH = 1024
QROWS = 256
UNIT = 64


def place_of(index):
    return index // 64, (index // 16) % 4, (index // 8) % 2, (index // 2) % 4, index % 2


def index_of(core, x, zh, y, zl):
    return core * 64 + x * 16 + zh * 8 + 2 * y + zl


def route(block, target):
    targets = [target(*place_of(i)) for i in range(128)]
    pairs = [(i, index_of(*place)) for i, place in enumerate(targets) if place is not None]
    return lax.ppermute(block, AXES, pairs)


def from_all(block, axes):
    count = math.prod(lax.axis_size(axis) for axis in axes)
    return swapped(jnp.broadcast_to(block[None], (count, *block.shape)), axes)


def swapped(blocks, axes):
    return lax.all_to_all(blocks, axes, split_axis=0, concat_axis=0, tiled=True)


def along_x(block, step):
    return route(block, lambda c, x, zh, y, zl: (c, (x + step) % 4, zh, y, zl))


def along_y(block, step):
    return route(block, lambda c, x, zh, y, zl: (c, x, zh, (y + step) % 4, zl))


def across_low(block):
    return route(block, lambda c, x, zh, y, zl: (c, x, zh, y, 1 - zl))


def across_cores(block):
    return route(block, lambda c, x, zh, y, zl: (1 - c, x, zh, y, zl))


def across_high(block):
    return route(block, lambda c, x, zh, y, zl: (c, x, 1 - zh, y, zl))


def transposed(block):
    return route(block, lambda c, x, zh, y, zl: (zl, y, zh, x, c))


def pick(array, index, axis=0):
    return lax.dynamic_index_in_dim(array, index, axis, keepdims=False)


def dot(left, right):
    return jnp.dot(left, right, preferred_element_type=F32)


def dot_left(left, right):
    return lax.dot_general(left, right, (((0,), (0,)), ((), ())), preferred_element_type=F32)


def dot_right(left, right):
    return lax.dot_general(left, right, (((1,), (1,)), ((), ())), preferred_element_type=F32)


def head_lanes(rows, head):
    lanes = lax.broadcasted_iota(jnp.int32, (rows, 2 * HEAD), 1)
    return (lanes >= head * HEAD) & (lanes < (head + 1) * HEAD)


def turned(values, cosine, sine_low, sine_high):
    return (
        values * cosine
        + pltpu.roll(values, ROT // 2, 1) * sine_low
        + pltpu.roll(values, 2 * HEAD - ROT // 2, 1) * sine_high
    )


def visible(begin, block, reach):
    rows = block * QROWS + lax.broadcasted_iota(jnp.int32, (QROWS, reach), 0)
    columns = lax.broadcasted_iota(jnp.int32, (QROWS, reach), 1)
    return (columns <= rows) & (columns >= begin)


def unit_rows(where_ref, m):
    return pl.ds(pl.multiple_of(where_ref[WHERE + m] * UNIT, UNIT), UNIT)


def attend(where_ref, proj_ref, tables, mixed_ref, q_ref, k_ref, v_ref, o_ref, lse_ref):
    cos_ref, low_ref, high_ref, begin_ref = tables
    for m in range(LENGTH // UNIT):
        here = pl.ds(m * UNIT, UNIT)
        proj = proj_ref[unit_rows(where_ref, m), :]
        cosine, low, high = cos_ref[here, :], low_ref[here, :], high_ref[here, :]
        query = turned(proj[:, :128].astype(F32), cosine, low, high)
        q_ref[here, :] = (query.astype(BF).astype(F32) * (1.0 / math.sqrt(HEAD))).astype(BF)
        k_ref[here, :] = turned(proj[:, 128:256].astype(F32), cosine, low, high).astype(BF)
        v_ref[here, :] = proj[:, 256:]
    for block in range(LENGTH // QROWS):
        rows = pl.ds(block * QROWS, QROWS)
        reach = (block + 1) * QROWS
        keys, values = k_ref[:reach, :], v_ref[:reach, :]
        query = q_ref[rows, :]
        seen = visible(begin_ref[rows, :1], block, reach)
        outs, logs = [], []
        for head in range(2):
            own = head_lanes(QROWS, head)
            scores = dot_right(jnp.where(own, query, jnp.zeros_like(query)), keys)
            scores = jnp.where(seen, scores, -1e30)
            highest = jnp.max(scores, axis=-1, keepdims=True)
            exponent = jnp.exp(scores - highest)
            total = jnp.sum(exponent, axis=-1, keepdims=True)
            outs.append(dot(exponent.astype(BF), values) * (1.0 / total))
            logs.append(highest + jnp.log(total))
        first = head_lanes(QROWS, 0)
        o_ref[rows, :] = jnp.where(first, outs[0], outs[1]).astype(BF)
        lse_ref[rows, :] = jnp.where(first, logs[0], logs[1])
    for m in range(LENGTH // UNIT):
        mixed_ref[unit_rows(where_ref, m), :] = o_ref[pl.ds(m * UNIT, UNIT), :]


def attend_back(where_ref, tables, kept, do_ref, out_ref, dq_ref, dk_ref, dv_ref):
    cos_ref, low_ref, high_ref, begin_ref = tables
    q_ref, k_ref, v_ref, o_ref, lse_ref = kept
    for block in reversed(range(LENGTH // QROWS)):
        rows = pl.ds(block * QROWS, QROWS)
        reach = (block + 1) * QROWS
        keys, values = k_ref[:reach, :], v_ref[:reach, :]
        query, upstream, mixed = q_ref[rows, :], do_ref[rows, :], o_ref[rows, :].astype(F32)
        seen = visible(begin_ref[rows, :1], block, reach)
        grads = []
        for head in range(2):
            own = head_lanes(QROWS, head)
            query_own = jnp.where(own, query, jnp.zeros_like(query))
            up_own = jnp.where(own, upstream, jnp.zeros_like(upstream))
            scores = jnp.where(seen, dot_right(query_own, keys), -1e30)
            probs = jnp.exp(scores - lse_ref[rows, head * HEAD : head * HEAD + 1])
            centre = jnp.sum(up_own.astype(F32) * mixed, axis=-1, keepdims=True)
            moved = (probs * (dot_right(up_own, values) - centre)).astype(BF)
            grads.append(dot(moved, keys))
            dk = dot_left(moved, query_own)
            dv = dot_left(probs.astype(BF), up_own)
            if block == LENGTH // QROWS - 1 and head == 0:
                dk_ref[...] = dk
                dv_ref[...] = dv
            else:
                dk_ref[:reach, :] += dk
                dv_ref[:reach, :] += dv
        first = head_lanes(QROWS, 0)
        dq_ref[rows, :] = jnp.where(first, grads[0], grads[1]) * (1.0 / math.sqrt(HEAD))
    for m in range(LENGTH // UNIT):
        here = pl.ds(m * UNIT, UNIT)
        there = unit_rows(where_ref, m)
        cosine, low, high = cos_ref[here, :], -low_ref[here, :], -high_ref[here, :]
        out_ref[there, :128] = turned(dq_ref[here, :], cosine, low, high).astype(BF)
        out_ref[there, 128:256] = turned(dk_ref[here, :], cosine, low, high).astype(BF)
        out_ref[there, 256:384] = dv_ref[here, :].astype(BF)


def barrier(*values):
    flat, tree = jax.tree.flatten(values)
    anywhere = pl.BlockSpec(memory_space=pl.ANY)
    flat = pl.pallas_call(
        lambda *refs: None,
        out_shape=[jax.ShapeDtypeStruct(value.shape, value.dtype) for value in flat],
        in_specs=[anywhere] * len(flat),
        out_specs=[anywhere] * len(flat),
        input_output_aliases={k: k for k in range(len(flat))},
    )(*flat)
    return jax.tree.unflatten(tree, flat)


def after(values, *others):
    flat, tree = jax.tree.flatten(values)
    others = jax.tree.leaves(others)
    anywhere = pl.BlockSpec(memory_space=pl.ANY)
    flat = pl.pallas_call(
        lambda *refs: None,
        out_shape=[jax.ShapeDtypeStruct(value.shape, value.dtype) for value in flat],
        in_specs=[anywhere] * (len(flat) + len(others)),
        out_specs=[anywhere] * len(flat),
        input_output_aliases={k: k for k in range(len(flat))},
    )(*flat, *others)
    return jax.tree.unflatten(tree, flat)


def run(body, scalars, arrays, outs, scratch=(), flops=0, spaces=None, others=()):
    vmem, anywhere = pl.BlockSpec(memory_space=pltpu.VMEM), pl.BlockSpec(memory_space=pl.ANY)
    others = jax.tree.leaves(others)
    count = 1 + len(arrays)
    return pl.pallas_call(
        lambda *refs: body(*refs[:count], *refs[count + len(others) :]),
        out_shape=[jax.ShapeDtypeStruct(*out) for out in outs],
        in_specs=[pl.BlockSpec(memory_space=pltpu.SMEM)]
        + (spaces or [vmem] * len(arrays))
        + [anywhere] * len(others),
        out_specs=[vmem] * len(outs),
        scratch_shapes=list(scratch),
        compiler_params=pltpu.CompilerParams(vmem_limit_bytes=60 * 1024 * 1024),
        cost_estimate=pl.CostEstimate(flops=flops, bytes_accessed=4_000_000, transcendentals=0),
    )(scalars, *arrays, *others)


X, CORE, ZH, Y, ZL, PART, SHARD, BIAS, WHERE = 0, 1, 2, 3, 4, 5, 6, 7, 10


def lanes(start, extent=128):
    return pl.ds(pl.multiple_of(start, extent), extent)


def low_half(rows):
    return lax.broadcasted_iota(jnp.int32, (rows, 128), 1) < 64


def half_tiles(first, second):
    low = low_half(first.shape[0])
    return (
        jnp.where(low, first, pltpu.roll(second, 64, 1)),
        jnp.where(low, pltpu.roll(first, 64, 1), second),
    )


def block_rows(number, extent):
    return pl.ds(pl.multiple_of(extent * number, extent), extent)


def column(row):
    return jnp.transpose(jnp.broadcast_to(row, (128, 128)))


def slice_kernel(
    at, qkv_all, up_all, down_all, dense_all, bias_qkv_all, bias_up_all, bias_dense, bias_down, gain_one, shift_one,
    gain_two, shift_two,
    qkv_self, qkv_other, rest_self, rest_other,
    qkv, up, down, dense, bias_qkv, small, rows, sems,
):
    x, core = at[X], at[CORE]
    copies = [(up_all.at[:, lanes(512 * k + 128 * x)], up.at[k]) for k in range(8)]
    copies += [(qkv_all.at[:, lanes(1024 * k + 256 * x, 256)], qkv.at[k]) for k in range(3)]
    copies.append((down_all.at[pl.ds(pl.multiple_of(128 * x, 128), 128), :], down))
    copies.append((dense_all.at[:, lanes(256 * x, 256)], dense))
    copies.append((bias_qkv_all, bias_qkv))
    copies.append((bias_up_all.at[:, lanes(128 * x)], small.at[0]))
    for k, vector in enumerate((bias_dense, bias_down, gain_one, shift_one, gain_two, shift_two)):
        copies.append((vector, small.at[1 + k]))
    copies = [pltpu.make_async_copy(*pair, sems.at[k]) for k, pair in enumerate(copies)]
    for copy in copies:
        copy.start()
    for copy in copies:
        copy.wait()
    for k in range(4):
        zero, one = half_tiles(up[2 * k].astype(F32), up[2 * k + 1].astype(F32))
        here = slice(128 * k, 128 * k + 128)
        rest_self[:, here] = jnp.where(core == 0, zero, one).astype(BF)
        rest_other[:, here] = jnp.where(core == 0, one, zero).astype(BF)
    for k in range(3):
        first, second = qkv[k, :, :128], qkv[k, :, 128:]
        here = slice(128 * k, 128 * k + 128)
        qkv_self[:128, here] = jnp.where(core == 0, first, second)
        qkv_other[:128, here] = jnp.where(core == 0, second, first)
    for k in range(2):
        first, second = down[:64, 512 * k : 512 * k + 512], down[64:, 512 * k : 512 * k + 512]
        rest_self[64 * k : 64 * k + 64, 512:] = jnp.where(core == 0, first, second)
        rest_other[64 * k : 64 * k + 64, 512:] = jnp.where(core == 0, second, first)
    first, second = dense[:, :128], dense[:, 128:]
    qkv_self[:128, 384:] = jnp.where(core == 0, first, second)
    qkv_other[:128, 384:] = jnp.where(core == 0, second, first)
    rows[...] = jnp.zeros_like(rows)
    for k in range(3):
        rows[k : k + 1, :] = bias_qkv[:, 128 * k : 128 * k + 128].astype(F32)
    for k in range(7):
        rows[3 + k : 4 + k, :] = small[k].astype(F32)
    plain = rows[...]
    number = lax.broadcasted_iota(jnp.int32, (16, 128), 0)
    moved = jnp.where(number == 3, pltpu.roll(plain, 64, 1), plain)
    for out, upper in ((qkv_self, core), (qkv_other, 1 - core)):
        out[128:, :128] = jnp.where(upper == 0, plain, moved).astype(BF)
        out[128:, 128:] = jnp.zeros((16, 384), BF)


def tables_kernel(at, places, frequency, cos_ref, low_ref, high_ref, begin_ref):
    place = jnp.transpose(jnp.broadcast_to(places[...].astype(F32), (128, LENGTH)))
    lane = lax.broadcasted_iota(jnp.int32, (LENGTH, 128), 1) % HEAD
    angles = place * frequency[...]
    sine = jnp.sin(angles)
    cos_ref[...] = jnp.where(lane < ROT, jnp.cos(angles), 1.0)
    low_ref[...] = jnp.where((lane >= ROT // 2) & (lane < ROT), sine, 0.0)
    high_ref[...] = jnp.where(lane < ROT // 2, -sine, 0.0)
    row = lax.broadcasted_iota(jnp.int32, (LENGTH, 128), 0)
    begin_ref[...] = row - place.astype(jnp.int32)


def prepare_qkv(at, blocks, wide, wide_turned, bias, bias_out, rows):
    bias[...] = jnp.zeros_like(bias)
    for shard, message in blocks:
        vectors = message[128:, :128].astype(F32)
        rows[16 * shard : 16 * shard + 16, :] = vectors
        here = slice(128 * shard, 128 * shard + 128)
        scale = column(vectors[6:7, :])
        for k in range(0, 384, 128):
            wide[here, k : k + 128] = (message[:128, k : k + 128].astype(F32) * scale).astype(BF)
        shift = jnp.broadcast_to(vectors[7:8, :], (8, 128)).astype(BF)
        bias[:, :384] += dot(shift, message[:128, :384])
    for k in range(3):
        bias[:, 128 * k : 128 * k + 128] += jnp.broadcast_to(rows[pl.ds(at[BIAS + k], 1), :], (8, 128))
    for shard in range(8):
        total = rows[16 * shard + 4 : 16 * shard + 5, :] + rows[16 * shard + 5 : 16 * shard + 6, :]
        bias_out[:, 128 * shard : 128 * shard + 128] = jnp.broadcast_to(total, (8, 128))
    wide_turned[...] = jnp.transpose(wide[...])


def prepare_up(at, blocks, rows, up, up_turned, bias):
    bias[...] = jnp.zeros_like(bias)
    for shard, message in blocks:
        vectors = rows[16 * shard : 16 * shard + 16, :]
        here = slice(128 * shard, 128 * shard + 128)
        scale = column(vectors[8:9, :])
        for k in range(0, 512, 128):
            up[here, k : k + 128] = (message[:128, k : k + 128].astype(F32) * scale).astype(BF)
        shift = jnp.broadcast_to(vectors[9:10, :], (8, 128)).astype(BF)
        bias[...] += dot(shift, message[:128, :512])
    for k in range(4):
        first = jnp.broadcast_to(rows[32 * k + 3 : 32 * k + 4, :], (8, 128))
        second = jnp.broadcast_to(rows[32 * k + 19 : 32 * k + 20, :], (8, 128))
        bias[:, 128 * k : 128 * k + 128] += half_tiles(first, second)[0]
    up_turned[...] = jnp.transpose(up[...])


def prepare_down(blocks, down, down_turned):
    for k, halves in enumerate(blocks):
        down[64 * k : 64 * k + 64, :512] = halves[:64, :]
        down[64 * k : 64 * k + 64, 512:] = halves[64:128, :]
    down_turned[...] = jnp.transpose(down[...])


def project_rows(blocks, qkv, bias, unit, proj):
    for k in range(8):
        values = blocks[k][...].astype(F32)
        centred = values - jnp.mean(values, axis=-1, keepdims=True)
        spread = jnp.mean(centred * centred, axis=-1, keepdims=True)
        unit[128 * k : 128 * k + 128, :] = (centred * lax.rsqrt(spread + NORM_EPS)).astype(BF)
    for k in range(4):
        here = slice(256 * k, 256 * k + 256)
        proj[here, :] = (dot(unit[here, :], qkv[...]) + bias[:1, :]).astype(BF)


def activate(unit, up, bias, active, slope):
    for k in range(4):
        here = slice(256 * k, 256 * k + 256)
        middle = dot(unit[here, :], up[...]) + bias[:1, :]
        share = 0.5 * (1.0 + lax.erf(middle * (1.0 / math.sqrt(2.0))))
        density = jnp.exp(-0.5 * middle * middle) * (1.0 / math.sqrt(2.0 * math.pi))
        active[here, :] = (middle * share).astype(BF)
        slope[here, :] = (share + middle * density).astype(BF)


def attend_first_kernel(at, *refs):
    blocks, messages, tables, outs = refs[:8], refs[8], refs[9:13], refs[13:]
    qkv_turned, bias_out, vectors, unit, mixed, *kept = outs[:10]
    qkv, bias, proj = outs[10:]
    prepare_qkv(at, [(k, messages.at[k]) for k in range(8)], qkv, qkv_turned, bias, bias_out, vectors)
    project_rows(blocks, qkv, bias, unit, proj)
    attend(at, proj, tables, mixed, *kept)


def attend_second_kernel(at, *refs):
    blocks, messages, tables, outs = refs[:8], refs[8], refs[9:13], refs[13:]
    qkv_turned, bias_out, up_turned, active, slope, unit, mixed, *kept = outs[:12]
    qkv, bias, proj, vectors, up, up_bias = outs[12:]
    prepare_qkv(at, [(k, messages.at[k]) for k in range(8)], qkv, qkv_turned, bias, bias_out, vectors)
    prepare_up(at, [(k, messages.at[k, :, 384:]) for k in range(8)], vectors, up, up_turned, up_bias)
    project_rows(blocks, qkv, bias, unit, proj)
    activate(unit, up, up_bias, active, slope)
    attend(at, proj, tables, mixed, *kept)


def dense_parts_of(at, parts, layer):
    for r in range(4):
        for beside in range(2):
            part = 2 * ((at[X] + 4 - r) % 4) + (at[CORE] + beside) % 2
            yield part, parts[beside, r, :, 128 * layer : 128 * layer + 128]


def project(at, layer, active, mixed, down, dense_parts, dense, blocks):
    for part, columns in dense_parts_of(at, dense_parts, layer):
        dense[:, lanes(128 * part)] = columns
    for k in (2, 1, 3, 0):
        here = slice(256 * k, 256 * k + 256)
        out = dot(active[here, :], down[...]) + dot(mixed[here, :], dense[...])
        blocks[2 * k][...] = out[:128].astype(BF)
        blocks[2 * k + 1][...] = out[128:].astype(BF)


def rest_first_kernel(at, messages, vectors, unit, mixed, dense_parts, up_turned, down_turned, active, slope, *refs):
    blocks, (up, bias, down, dense) = refs[:8], refs[8:]
    prepare_up(at, [(k, messages.at[k]) for k in range(8)], vectors, up, up_turned, bias)
    prepare_down([messages.at[k, :, 512:] for k in range(8)], down, down_turned)
    activate(unit, up, bias, active, slope)
    project(at, 0, active, mixed, down, dense_parts, dense, blocks)


def project_kernel(at, active, mixed, down, dense_parts, *refs):
    project(at, 1, active, mixed, down, dense_parts, refs[8], refs[:8])


def pull_back(at, layer, blocks, down_turned, dense_parts, slope, grad_middle, grad_mixed, dense_turned, together):
    for k in range(8):
        together[128 * k : 128 * k + 128, :] = blocks[k][...]
    for part, columns in dense_parts_of(at, dense_parts, layer):
        dense_turned[block_rows(part, 128), :] = jnp.transpose(columns)
    for k in range(4):
        here = slice(256 * k, 256 * k + 256)
        rows = together[here, :]
        grad_middle[here, :] = (dot(rows, down_turned[...]) * slope[here, :].astype(F32)).astype(BF)
        grad_mixed[here, :] = dot(rows, dense_turned[...]).astype(BF)


def back_second_kernel(at, *refs):
    rows, (messages, dense_parts, slope), qkv_turned, up_turned = refs[:8], refs[8:11], refs[11], refs[12]
    tables, kept, blocks = refs[13:17], refs[17:22], refs[22:30]
    grad_proj, grad_middle, down, down_turned, dense_turned, grad_mixed, together, *scratch = refs[30:]
    prepare_down([messages.at[k] for k in range(8)], down, down_turned)
    pull_back(at, 1, rows, down_turned, dense_parts, slope, grad_middle, grad_mixed, dense_turned, together)
    back_attend_kernel(
        at, grad_mixed, grad_middle, qkv_turned, up_turned, *tables, *kept, *blocks, grad_proj, *scratch
    )


def back_attend_kernel(where_ref, grad_mixed, grad_middle, wide_turned, up_turned, cosine, low, high, begin, *refs):
    kept, blocks, grad_proj, (do_ref, dq_ref, dk_ref, dv_ref) = refs[:5], refs[5:13], refs[13], refs[14:]
    for m in range(LENGTH // UNIT):
        do_ref[pl.ds(m * UNIT, UNIT), :] = grad_mixed[unit_rows(where_ref, m), :]
    attend_back(where_ref, (cosine, low, high, begin), kept, do_ref, grad_proj, dq_ref, dk_ref, dv_ref)
    for k in (2, 1, 3, 0):
        here = slice(256 * k, 256 * k + 256)
        out = dot(grad_proj[here, :], wide_turned[...]) + dot(grad_middle[here, :], up_turned[...])
        blocks[2 * k][...] = out[:128].astype(BF)
        blocks[2 * k + 1][...] = out[128:].astype(BF)


def weight_terms(at, unit, grads, outward=None, pulled=None, others=()):
    extent = 512 if pulled else sum(grad.shape[1] for grad in grads)
    start = 640 if outward else 0
    arrays, scratch, outs = (unit, *grads), [], [((8, 144, start + extent), BF)]
    if outward:
        active, mixed, rows, *grad_middle = outward
        arrays = (*arrays, active, mixed, *rows, *grad_middle)
        scratch = [pltpu.VMEM((1024, 1024), BF)]
    if pulled:
        arrays = (*arrays, *pulled)
        outs += [((1024, 512), BF), ((1024, 128), BF)]
        scratch.append(pltpu.VMEM((1024, 128), BF))

    def body(at, unit, *refs):
        grad_refs, refs = refs[: len(grads)], refs[len(grads) :]
        if pulled:
            (active, mixed), rows, refs = refs[:2], refs[2:10], refs[10:]
            (down_turned, dense_parts, slope), (out, grad_middle, grad_mixed) = refs[:3], refs[3:6]
            together, dense_turned = refs[6:]
            pull_back(
                at, 0, rows, down_turned, dense_parts, slope, grad_middle, grad_mixed, dense_turned, together
            )
            grad_refs = (grad_middle,)
        elif outward:
            (active, mixed), rows, grad_middle, out, together = refs[:2], refs[2:10], *refs[10:]
            for k in range(8):
                together[128 * k : 128 * k + 128, :] = rows[k][...]
        else:
            out = refs[0]
        if outward:
            sums = jnp.sum(together[:, lanes(128 * at[PART])].astype(F32), axis=0, keepdims=True)
            sums_up = jnp.sum(grad_middle[...].astype(F32), axis=0, keepdims=True)
            dense = dot_left(mixed[...], together[...]).astype(BF)
            for shard in range(8):
                if shard % 4 == 0:
                    down = dot_left(active[:, 64 * shard : 64 * shard + 256], together[...]).astype(BF)
                for half in range(2):
                    piece = down[64 * (shard % 4) : 64 * (shard % 4) + 64, 512 * half : 512 * half + 512]
                    out[shard, 64 * half : 64 * half + 64, :512] = piece
                out[shard, :128, 512:640] = dense[:, 128 * shard : 128 * shard + 128]
                out[shard, 128:, :128] = jnp.broadcast_to(sums, (16, 128)).astype(BF)
                out[shard, 128:, 128:640] = jnp.broadcast_to(sums_up, (16, 512)).astype(BF)
        at_column = start
        for grad in grad_refs:
            columns = grad.shape[1]
            here = slice(at_column, at_column + columns)
            sums = jnp.sum(grad[...].astype(F32), axis=0, keepdims=True)
            for shard in range(8):
                if shard % 2 == 0:
                    terms = dot_left(unit[:, 128 * shard : 128 * shard + 256], grad[...]).astype(BF)
                out[shard, :128, here] = terms[128 * (shard % 2) : 128 * (shard % 2) + 128, :]
                out[shard, 128:, here] = jnp.broadcast_to(sums, (16, columns)).astype(BF)
            at_column += columns

    outs = run(body, at, arrays, outs, scratch, flops=2 * 1024 * 1024 * (extent + start), others=others)
    return outs if pulled else outs[0]


def final_kernel(at, *refs):
    sources = refs[:8], refs[8:16]
    qkv, up, gain_one, shift_one, gain_two, shift_two = refs[16:22]
    grad_qkv, grad_up, grad_down, grad_dense = refs[22:26]
    bias_qk, bias_v, bias_up, bias_out, gain_a, shift_a, gain_b, shift_b = refs[26:34]
    sums, sums_qkv, sums_up, sums_out, sems = refs[34:]
    x, core, shard = at[X], at[CORE], at[SHARD]
    for layer in range(2):

        @pl.when(core == layer)
        def _():
            copies = []
            for k in range(8):
                target = sums.at[k // 4, (x + k % 4) % 4]
                copies.append(pltpu.make_async_copy(sources[layer][k], target, sems.at[k]))
            for copy in copies:
                copy.start()
            for copy in copies:
                copy.wait()

    def whole(beside, r, columns):
        return sums[beside, r, :128, columns].astype(F32)

    def below(beside, r, columns):
        return sums[beside, r, 128:, columns].astype(F32)

    gain_col, shift_col = column(gain_one[...].astype(F32)), column(shift_one[...].astype(F32))
    gain_col_two, shift_col_two = column(gain_two[...].astype(F32)), column(shift_two[...].astype(F32))
    totals = [jnp.zeros((128, 128), F32) for _ in range(4)]
    for r in range(4):
        column_no = r
        for half in range(2):
            beside = (core + half) % 2
            part = 2 * column_no + half
            for k in range(3):
                cols = slice(1152 + 128 * k, 1280 + 128 * k)
                raw = whole(beside, r, cols)
                total = below(beside, r, cols)[:1]
                place = lanes(1024 * k + 128 * part)
                weight = qkv[:, place].astype(F32)
                grad_qkv[:, place] = gain_col * raw + shift_col * total
                sums_qkv[pl.ds(8 * k + part, 1), :] = total
                totals[0] += weight * raw
                totals[1] += weight * total
            grad_down[pl.ds(pl.multiple_of(64 * part, 64), 64), :512] = sums[beside, r, :64, :512].astype(F32)
            grad_down[pl.ds(pl.multiple_of(64 * part, 64), 64), 512:] = sums[beside, r, 64:128, :512].astype(F32)
            grad_dense[:, lanes(128 * part)] = whole(beside, r, slice(512, 640))
            sums_out[pl.ds(part, 1), :] = below(beside, r, slice(0, 128))[:1]
        zero, one = core % 2, (core + 1) % 2
        for k in range(4):
            cols = slice(640 + 128 * k, 768 + 128 * k)
            beneath = slice(128 + 128 * k, 256 + 128 * k)
            raws = half_tiles(whole(zero, r, cols), whole(one, r, cols))
            adds = half_tiles(below(zero, r, beneath), below(one, r, beneath))
            for odd in range(2):
                raw, total = raws[odd], adds[odd][:1]
                place = lanes(1024 * k + 512 * odd + 128 * column_no)
                weight = up[:, place].astype(F32)
                grad_up[:, place] = gain_col_two * raw + shift_col_two * total
                sums_up[pl.ds(8 * k + 4 * odd + column_no, 1), :] = total
                totals[2] += weight * raw
                totals[3] += weight * total
    for out, total in zip((gain_a, shift_a, gain_b, shift_b), totals):
        out[...] = jnp.sum(jnp.transpose(total), axis=0, keepdims=True)
    for k in range(2):
        bias_qk[:, 128 * k : 128 * k + 128] = sums_qkv[pl.ds(2 * shard + k, 1), :]
    bias_v[...] = sums_qkv[pl.ds(16 + shard, 1), :]
    for k in range(4):
        bias_up[:, 128 * k : 128 * k + 128] = sums_up[pl.ds(4 * shard + k, 1), :]
    bias_out[...] = sums_out[pl.ds(shard, 1), :]


def added(*blocks):
    total = blocks[0].astype(F32)
    for block in blocks[1:]:
        total = total + block.astype(F32)
    return total


def gather_rows(mine):
    own = [mine] + [along_x(mine, -r) for r in (1, 2, 3)]
    other = [across_cores(block) for block in own]
    return [rows for pair in zip(own, other) for rows in pair]


def joined_cores(blocks):
    joined = {r: added(blocks[2 * r], across_cores(blocks[2 * r + 1])) for r in (2, 1, 3, 0)}
    return [joined[0]] + [joined[r].astype(BF) for r in (1, 2, 3)]


def joined_chips(joined):
    return added(joined[0], *(along_x(joined[r], r) for r in (1, 2, 3)))


def summed(blocks):
    return jnp.sum(blocks.astype(F32), axis=0)


def normalized(rows):
    values = rows.astype(F32)
    centre = jnp.mean(values, axis=-1, keepdims=True)
    centred = values - centre
    spread = jnp.mean(centred * centred, axis=-1, keepdims=True)
    scale = lax.rsqrt(spread + NORM_EPS)
    return centred * scale, scale


def norm_back(grad, rows):
    unit, scale = normalized(rows)
    mean_grad = jnp.mean(grad, axis=-1, keepdims=True)
    mean_both = jnp.mean(grad * unit, axis=-1, keepdims=True)
    return scale * (grad - mean_grad - unit * mean_both)


def shards(
    tokens, positions, w_qkv, b_qkv, w_dense, b_dense, w_up, b_up, w_down, b_down,
    norm1_gain, norm1_shift, norm2_gain, norm2_shift, cotangent,
):
    core, x, zh, y, zl = (lax.axis_index(axis) for axis in AXES)
    shard = 2 * y + zl
    part = 2 * x + core
    first_core = core == 0
    anywhere, vmem = pl.BlockSpec(memory_space=pl.ANY), pl.BlockSpec(memory_space=pltpu.VMEM)

    bias_rows = [16 * ((8 * k + part) // 3) + (8 * k + part) % 3 for k in range(3)]
    at = jnp.stack([x, core, zh, y, zl, part, shard] + bias_rows).astype(jnp.int32)
    unit_no = jnp.arange(16, dtype=jnp.int32)
    where = (
        ((unit_no // 4 - x) % 4) * 4
        + jnp.bitwise_xor(unit_no % 2, core) * 2
        + jnp.bitwise_xor((unit_no // 2) % 2, zh)
    ).astype(jnp.int32)
    at = jnp.concatenate([at, where])

    own, lent = [], []
    for array in (tokens, cotangent):
        own.append(lax.dynamic_slice_in_dim(pick(array, zh), core * UNIT, UNIT, 0))
        lent.append(lax.dynamic_slice_in_dim(pick(array, 1 - zh), core * UNIT, UNIT, 0))
    lent = across_high(jnp.stack(lent))
    own_tokens = jnp.concatenate([own[0], lent[0]], axis=0)
    own_cotangent = jnp.concatenate([own[1], lent[1]], axis=0)

    sliced = run(
        slice_kernel,
        at,
        (
            w_qkv[0], w_up[0], w_down[0], w_dense[0], b_qkv, b_up, b_dense, b_down,
            norm1_gain, norm1_shift, norm2_gain, norm2_shift,
        ),
        [((144, 512), BF)] * 2 + [((128, 1024), BF)] * 2,
        [
            pltpu.VMEM((3, 128, 256), BF),
            pltpu.VMEM((8, 128, 128), BF),
            pltpu.VMEM((128, 1024), BF),
            pltpu.VMEM((128, 256), BF),
            pltpu.VMEM((1, 384), BF),
            pltpu.VMEM((7, 1, 128), BF),
            pltpu.VMEM((16, 128), F32),
            pltpu.SemaphoreType.DMA((21,)),
        ],
        spaces=[pl.BlockSpec(memory_space=pltpu.HBM)] * 12,
    )
    qkv_theirs, rest_theirs = across_cores(sliced[1]), across_cores(sliced[3])
    qkv, qkv_two = jnp.where(first_core, sliced[0], qkv_theirs), jnp.where(first_core, qkv_theirs, sliced[0])
    qkv = jnp.concatenate([qkv, qkv_two[:, 384:]], axis=1)
    rest = jnp.where(first_core, sliced[2], rest_theirs)
    rest_two = jnp.where(first_core, rest_theirs, sliced[2])
    wide_two = jnp.concatenate([qkv_two[:, :384], jnp.pad(rest_two[:, :512], ((0, 16), (0, 0)))], axis=1)
    down_two = rest_two[:, 512:]

    half = ROT // 2
    frequency = 1.0 / 10000.0 ** (jnp.arange(half).astype(F32) * 2.0 / ROT)
    frequency = jnp.concatenate([jnp.tile(frequency, HEAD // half)] * 2)[None, :]
    tables = run(
        tables_kernel,
        at,
        (lax.dynamic_slice_in_dim(positions, zh, 1, 0), frequency),
        [((LENGTH, 128), F32)] * 3 + [((LENGTH, 128), jnp.int32)],
    )

    big, head = ((1024, 1024), BF), ((1024, 128), BF)
    kept_outs = [head] * 4 + [((1024, 128), F32)]
    qkv_scratch = [pltpu.VMEM((1024, 384), BF), pltpu.VMEM((8, 384), F32), pltpu.VMEM((1024, 384), BF)]
    grad_scratch = [pltpu.VMEM((1024, 128), BF)] + [pltpu.VMEM((1024, 128), F32)] * 3
    hidden_outs = [((1024, 512), BF)] * 2
    block_outs = [((128, 1024), BF)] * 8
    qkv_outs = [((384, 1024), BF), ((8, 1024), F32)]

    def back_attend(grad_mixed, grad_middle, qkv_turned, up_turned, kept):
        outs = run(
            back_attend_kernel,
            at,
            (grad_mixed, grad_middle, qkv_turned, up_turned, *tables, *kept),
            [((128, 1024), BF)] * 8 + [((1024, 384), BF)],
            grad_scratch,
            flops=6_000_000_000,
        )
        return outs[:8], outs[8]

    qkvs = from_all(after(qkv, own_tokens), SHARDS)
    rows_one = gather_rows(own_tokens)
    rests = from_all(after(rest, qkvs, rows_one[2::2]), SHARDS)
    held = [lax.dynamic_slice(qkvs, (2 * ((x + r) % 4), 0, 384), (2, 128, 256)) for r in range(4)]
    held = [held[0]] + [along_x(held[r], r) for r in (1, 2, 3)]
    dense = jnp.stack([pick(block, core) for block in held])
    dense = jnp.stack([dense, across_cores(jnp.stack([pick(block, 1 - core) for block in held]))])
    qkv_turned_one, bias_out_one, vectors, unit_one, mixed_one, *kept_one = run(
        attend_first_kernel,
        at,
        (*rows_one, qkvs, *tables),
        qkv_outs + [((128, 128), F32), big, head] + kept_outs,
        qkv_scratch,
        flops=5_000_000_000,
    )
    rests, wide_two, dense = after((rests, wide_two, dense), mixed_one)

    wides = from_all(after(wide_two, rests), SHARDS)
    up_turned_one, down_turned_one, active_one, slope_one, *blocks = run(
        rest_first_kernel,
        at,
        (rests, vectors, unit_one, mixed_one, dense),
        [((512, 1024), BF), ((1024, 512), BF)] + hidden_outs + block_outs,
        [
            pltpu.VMEM((1024, 512), BF),
            pltpu.VMEM((8, 512), F32),
            pltpu.VMEM((512, 1024), BF),
            pltpu.VMEM((128, 1024), BF),
        ],
        flops=3_000_000_000,
    )
    joined = joined_cores(blocks)
    hidden_one = own_tokens.astype(F32) + joined_chips(joined) + bias_out_one[:1, :]
    hidden_one = hidden_one.astype(BF)
    rows_two = gather_rows(hidden_one)
    downs = from_all(after(down_two, wides), SHARDS)
    own_cotangent = after(own_cotangent, rows_two[2::2])

    grad_own = [own_cotangent] + [along_x(own_cotangent, -r) for r in (1, 2, 3)]
    qkv_turned_two, bias_out_two, up_turned_two, active_two, slope_two, unit_two, mixed_two, *kept_two = run(
        attend_second_kernel,
        at,
        (*rows_two, wides, *tables),
        qkv_outs + [((512, 1024), BF)] + hidden_outs + [big, head] + kept_outs,
        qkv_scratch
        + [pltpu.VMEM((128, 128), F32), pltpu.VMEM((1024, 512), BF), pltpu.VMEM((8, 512), F32)],
        flops=8_000_000_000,
    )
    grad_own = after(grad_own, mixed_two)
    grad_rows = [rows for block in grad_own for rows in (block, across_cores(block))]

    *blocks, grad_proj, grad_middle, down_two = run(
        back_second_kernel,
        at,
        (*grad_rows, downs, dense, slope_two, qkv_turned_two, up_turned_two, *tables, *kept_two),
        block_outs + [((1024, 384), BF), ((1024, 512), BF), ((512, 1024), BF)],
        [pltpu.VMEM((1024, 512), BF)] + [pltpu.VMEM((1024, 128), BF)] * 2 + [pltpu.VMEM((1024, 1024), BF)] + grad_scratch,
        flops=8_000_000_000,
    )
    joined = joined_cores(blocks)
    out_sums = weight_terms(
        at, unit_two, (), (active_two, mixed_two, grad_rows, grad_middle), others=joined
    )
    joined[0] = after(joined[0], out_sums)
    out_sums = swapped(out_sums, SHARDS)
    grad_two = grad_rows[0].astype(F32) + norm_back(joined_chips(joined), hidden_one)
    grad_mid = grad_two.astype(BF)
    wide_sums = weight_terms(at, unit_two, (grad_middle, grad_proj), others=[grad_mid])
    grad_rows = gather_rows(grad_mid)
    grad_rows, out_sums, wide_sums = barrier(grad_rows, out_sums, wide_sums)
    grad_mid = grad_rows[0]

    wide_sums = swapped(wide_sums, SHARDS)
    early_sums, grad_middle, grad_mixed = weight_terms(
        at, unit_one, (), (active_one, mixed_one, grad_rows), (down_turned_one, dense, slope_one)
    )
    blocks, grad_proj = back_attend(grad_mixed, grad_middle, qkv_turned_one, up_turned_one, kept_one)
    blocks_hidden = run(
        project_kernel,
        at,
        (active_two, mixed_two, down_two, dense),
        block_outs,
        [pltpu.VMEM((128, 1024), BF)],
        flops=1_500_000_000,
        others=[grad_proj],
    )
    joined_hidden = joined_cores(blocks_hidden)
    blocks, grad_proj, out_sums, wide_sums, early_sums, joined_hidden = barrier(
        blocks, grad_proj, out_sums, wide_sums, early_sums, joined_hidden
    )

    def turned_dense(total):
        dense = jnp.concatenate([transposed(total[:128, 512:640]), total[128:, 512:640]], axis=0)
        return jnp.concatenate([total[:, :512], dense, total[:, 640:]], axis=1)

    def to_keeper(parts, layer):
        return route(parts, lambda c, x, zh, y, zl: (layer, x, zh, y, zl) if c != layer else None)

    early_sums = swapped(early_sums, SHARDS)
    joined = joined_cores(blocks)
    late_sums = weight_terms(at, unit_one, (grad_proj,), others=joined[1:])
    grad_one = grad_mid.astype(F32) + norm_back(joined_chips(joined), own_tokens)
    grad_low = grad_one.astype(BF)
    out_sums, wide_sums = after((out_sums, wide_sums), joined[1:])
    hidden_two = hidden_one.astype(F32) + joined_chips(joined_hidden) + bias_out_two[:1, :]
    hidden_two = hidden_two.astype(BF)
    second = turned_dense(jnp.concatenate([summed(out_sums), summed(wide_sums)], axis=1).astype(BF))
    second_high = across_high(second)
    early_sums, late_sums, grad_low, hidden_two, second, second_high = barrier(
        early_sums, late_sums, grad_low, hidden_two, second, second_high
    )
    late_sums = swapped(late_sums, SHARDS)
    second = added(second, second_high).astype(BF)
    second = [second] + [along_x(second, -r) for r in (1, 2, 3)]
    early = turned_dense(summed(after(early_sums, second[1])).astype(BF))
    grad_beside, hidden_beside = across_cores(grad_low), across_cores(hidden_two)
    late_sums, second, early, grad_beside, hidden_beside = barrier(late_sums, second, early, grad_beside, hidden_beside)
    first = jnp.concatenate([early, summed(late_sums).astype(BF)], axis=1)
    first = added(first, across_high(first)).astype(BF)
    first = [first] + [along_x(first, -r) for r in (1, 2, 3)]
    first_sums = first + [to_keeper(block, 0) for block in first]
    second_sums = second + [to_keeper(block, 1) for block in second]

    def placed(pairs):
        local, lent = [], []
        for own, beside in pairs:
            low = jnp.where(first_core, own, beside)
            high = jnp.where(first_core, beside, own)
            local.append(jnp.concatenate([low[:UNIT], high[:UNIT]], axis=0))
            lent.append(jnp.concatenate([low[UNIT:], high[UNIT:]], axis=0))
        local, lent = jnp.stack(local), across_high(jnp.stack(lent))
        return jnp.stack([jnp.where(zh == 0, local, lent), jnp.where(zh == 0, lent, local)], axis=1)

    outputs = placed(
        [
            (jnp.where(first_core, hidden_one, hidden_two), jnp.where(first_core, rows_two[1], hidden_beside)),
            (jnp.where(first_core, grad_low, grad_mid), jnp.where(first_core, grad_beside, grad_rows[1])),
        ]
    )
    hidden, in_grads = outputs[0], outputs[1].astype(F32)
    outs = run(
        final_kernel,
        at,
        (
            *first_sums, *second_sums,
            w_qkv[0], w_up[0], norm1_gain, norm1_shift, norm2_gain, norm2_shift,
        ),
        [((128, 3072), F32), ((128, 4096), F32), ((512, 1024), F32), ((128, 1024), F32)]
        + [((1, 256), F32), ((1, 128), F32), ((1, 512), F32)]
        + [((1, 128), F32)] * 5,
        [
            pltpu.VMEM((2, 4, 144, 1536), BF),
            pltpu.VMEM((24, 128), F32),
            pltpu.VMEM((32, 128), F32),
            pltpu.VMEM((8, 128), F32),
            pltpu.SemaphoreType.DMA((8,)),
        ],
        spaces=[anywhere] * 16 + [vmem] * 6,
    )
    grad_qkv, grad_up, grad_down, grad_dense, bias_qk, bias_v, bias_up, bias_out, *norms = outs
    return (
        hidden[None], in_grads[None], grad_qkv[None], bias_qk, bias_v, grad_dense[None], bias_out,
        grad_up[None], bias_up, grad_down[None], bias_out, *norms,
    )


def solution(mesh):
    mesh = Mesh(mesh.devices.reshape(2, 4, 2, 4, 2), AXES)
    rows = P("core", SHARDS, None)
    vector = P("core", SHARDS)
    tokens = P(SHARDS, ("x", "z_hi"), None)
    layered = P("core", SHARDS, ("x", "z_hi"), None)
    in_specs = (
        tokens, P(SHARDS, None),
        rows, vector, rows, vector, rows, vector, rows, vector, vector, vector, vector, vector,
        tokens,
    )
    out_specs = (
        layered, layered,
        rows, vector, vector, rows, vector, rows, vector, rows, vector, vector, vector, vector, vector,
    )
    return jax.shard_map(shards, mesh=mesh, in_specs=in_specs, out_specs=out_specs, check_vma=False)
```
